32 devices in a mesh: dp: 8 (over z, core), seq: 4 (over y, x).
Axes of the slice: x: 2, y: 2, z: 4, core: 2. Of those that a mesh axis runs over, the one named last changes fastest.
Arguments:
- byte_ids: int32 [128, 2048], P('dp', 'seq'), may hold values from 0 to 255
- lengths: int32 [128], P('dp'), may hold values from 512 to 2048, as said below
- embed: float32 [256, 768], P('dp'), may hold values from -6 to 6
- conv: float32 [5, 768, 768], P(None, 'dp'), may hold values from -0.09375 to 0.09375
- score: float32 [768], replicated, may hold values from -0.4375 to 0.4375
- out_grad: float32 [128, 1024, 768], P('dp', 'seq'), may hold values from -6 to 6
- embed_left: float32 [256, 256], P('dp')
- embed_right: float32 [768, 768], P('dp')
- conv_left: float32 [5, 768, 768], P(None, 'dp')
- conv_right: float32 [5, 768, 768], P(None, 'dp')
- embed_left_root: float32 [256, 256], P('dp')
- embed_right_root: float32 [768, 768], replicated
- conv_left_root: float32 [5, 768, 768], P(None, 'dp')
- conv_right_root: float32 [5, 768, 768], replicated
- score_second: float32 [768], replicated, may hold values from 20132.66 to 80530.64
Outputs:
- output: float32 [128, 1024, 768], P('dp', 'seq')
- entropy: float32 [], replicated
- embed_grad: float32 [256, 768], P('dp')
- conv_grad: float32 [5, 768, 768], P(None, 'dp')
- score_grad: float32 [768], replicated
- new_embed: float32 [256, 768], P('dp')
- new_conv: float32 [5, 768, 768], P(None, 'dp')
- new_score: float32 [768], replicated
- new_embed_left: float32 [256, 256], P('dp')
- new_embed_right: float32 [768, 768], P('dp')
- new_conv_left: float32 [5, 768, 768], P(None, 'dp')
- new_conv_right: float32 [5, 768, 768], P(None, 'dp')
- new_score_second: float32 [768], replicated
The draws below stay inside these ranges and needn't reach their ends.
Inputs may be any that keep to these rules, and one draw needn't show every extreme that they name: `lengths`: in each aligned block of 16 rows one row, chosen by the seed, has all 2048 bytes.
All inputs are finite; a program needn't handle non-finite values.
Results may differ from the reference program's by a relative error of at most 0.0007.
The reference program's roundings to bfloat16 on the way count: a program that leaves them out, or rounds other values in their place, can miss the bound.
Values may be sent and summed in bfloat16 or wider, within the bound.
No kernel may reach another device: no remote copies, remote signals or barrier semaphores. Data moves between devices by JAX's collectives and lax.ppermute only.
A program may use at most 576 MiB of HBM per device.

```python
import math
from functools import partial
import jax
import jax.numpy as jnp
import numpy as np
from jax import lax

D = 768
VOCAB = 256
TAPS = 5
SIZES = 4
LEN = 2048
ROWS_DEV = 16
ROWS = 128
HALF = 1024


def draw_lengths(key, part):
    first, second = jax.random.split(key)
    drawn = jax.random.randint(first, (ROWS,), LEN // 4, LEN + 1)
    chosen = jax.random.randint(second, (ROWS // ROWS_DEV,), 0, ROWS_DEV)
    full_rows = jnp.arange(ROWS // ROWS_DEV, dtype=jnp.int32) * ROWS_DEV + chosen
    return drawn.at[full_rows].set(LEN).astype(jnp.int32)


def conv_square():
    return 0.06 * ROWS * LEN


def embed_square():
    return 0.0003 * ROWS * LEN


def diagonal_matrix(key, count, order, level):
    factors = jnp.exp(jax.random.uniform(key, (count, order), jnp.float32, 0.0, math.log(4.0)))
    identity = jnp.eye(order, dtype=jnp.float32)
    return level * factors[:, :, None] * identity[None, :, :]


def root_matrix(key, count, order, level):
    first, second = jax.random.split(key)
    factors = jnp.exp(jax.random.uniform(first, (count, order), jnp.float32, math.log(0.5), math.log(2.0)))
    noise = jax.random.normal(second, (count, order, order), jnp.float32)
    mirrored = (noise + jnp.swapaxes(noise, 1, 2)) * (0.3 / math.sqrt(2.0 * order))
    identity = jnp.eye(order, dtype=jnp.float32)
    return level * (factors[:, :, None] * identity[None, :, :] + mirrored)


def draw_embed_left(key, part):
    return diagonal_matrix(jax.random.fold_in(key, 1), 1, VOCAB, D * embed_square() / 9.0)[0]


def draw_embed_right(key, part):
    return diagonal_matrix(jax.random.fold_in(key, 2), 1, D, VOCAB * embed_square() / 9.0)[0]


def draw_conv_left(key, part):
    return diagonal_matrix(jax.random.fold_in(key, 3), TAPS, D, D * conv_square() / 9.0)


def draw_conv_right(key, part):
    return diagonal_matrix(jax.random.fold_in(key, 4), TAPS, D, D * conv_square() / 9.0)


def draw_embed_left_root(key, part):
    return root_matrix(jax.random.fold_in(key, 5), 1, VOCAB, (0.33 * D * embed_square()) ** (-0.25))[0]


def draw_embed_right_root(key, part):
    return root_matrix(jax.random.fold_in(key, 6), 1, D, (0.33 * VOCAB * embed_square()) ** (-0.25))[0]


def draw_conv_left_root(key, part):
    return root_matrix(jax.random.fold_in(key, 7), TAPS, D, (0.33 * D * conv_square()) ** (-0.25))


def draw_conv_right_root(key, part):
    return root_matrix(jax.random.fold_in(key, 8), TAPS, D, (0.33 * D * conv_square()) ** (-0.25))


def with_ends(array, stream_key, least, largest):
    place = [jax.random.randint(jax.random.fold_in(stream_key, axis), (), 0, length) for axis, length in enumerate(array.shape)]
    longest = array.shape.index(max(array.shape))
    next_to = place[:longest] + [(place[longest] + 1) % array.shape[longest]] + place[longest + 1:]
    return array.at[tuple(place)].set(least).at[tuple(next_to)].set(largest)


def block_scale(rng, extent, cuts, least, high):
    loudness, own = 1.0, jax.random.fold_in(rng, 6)
    for dim, shards_of in cuts:
        heights = jnp.exp(jax.random.uniform(jax.random.fold_in(own, dim), (shards_of,), jnp.float32, least / len(cuts), high / len(cuts)))
        loudness = loudness * jnp.repeat(heights, extent[dim] // shards_of).reshape([-1 if axis == dim else 1 for axis in range(len(extent))])
    return loudness


def rank_bounds(amount, lean):
    loads = [(1 << 20) // math.isqrt(standing ** lean) + 1 for standing in range(1, amount + 1)]
    deviation = 1 + sum(loads) // (1 << 30)
    return np.cumsum(np.array([max(1, weight // deviation) for weight in loads]))


def ranked(rng, shape, count, slope):
    table = rank_bounds(count, slope)
    ticket = jax.random.randint(jax.random.fold_in(rng, 1), shape, 0, int(table[count - 1]))
    standing = jnp.searchsorted(jnp.asarray(table, jnp.int32), ticket, side="right")
    return jax.random.permutation(jax.random.fold_in(rng, 2), count)[standing].astype(jnp.int32)


def gaussian(stream_key, extent, scale, reach, shards=(), kind=jnp.bfloat16):
    result = jax.random.normal(stream_key, extent, jnp.float32) * scale
    if len(shards) > 0:
        result = block_scale(stream_key, extent, shards, -0.22, 0.18) * result
    return jnp.clip(result, min=-reach, max=reach).astype(kind)


def setup_inputs(seed: int = 0) -> dict:
    streams_of = jax.random.split(jax.random.key(seed), 16)
    return {
        "byte_ids": with_ends(ranked(streams_of[0], (ROWS, LEN), VOCAB, 2), jax.random.fold_in(streams_of[0], 3), 0, VOCAB - 1).astype(jnp.int32),
        "lengths": draw_lengths(jax.random.fold_in(streams_of[15], 71), 0),
        "embed": gaussian(streams_of[2], (VOCAB, D), 1.0, 6.0, ((0, 8),), jnp.float32),
        "conv": gaussian(streams_of[3], (TAPS, D, D), (TAPS * D) ** -0.5, 0.09375, ((1, 8),), jnp.float32),
        "score": gaussian(streams_of[4], (D,), (D // 4) ** -0.5, 0.4375, (), jnp.float32),
        "out_grad": gaussian(streams_of[5], (ROWS, HALF, D), 1.0, 6.0, ((0, 8), (1, 4)), jnp.float32),
        "embed_left": draw_embed_left(jax.random.fold_in(streams_of[15], 71), 0),
        "embed_right": draw_embed_right(jax.random.fold_in(streams_of[15], 71), 0),
        "conv_left": draw_conv_left(jax.random.fold_in(streams_of[15], 71), 0),
        "conv_right": draw_conv_right(jax.random.fold_in(streams_of[15], 71), 0),
        "embed_left_root": draw_embed_left_root(jax.random.fold_in(streams_of[15], 71), 0),
        "embed_right_root": draw_embed_right_root(jax.random.fold_in(streams_of[15], 71), 0),
        "conv_left_root": draw_conv_left_root(jax.random.fold_in(streams_of[15], 71), 0),
        "conv_right_root": draw_conv_right_root(jax.random.fold_in(streams_of[15], 71), 0),
        "score_second": jnp.clip(jnp.exp(jax.random.uniform(streams_of[14], (D,), jnp.float32, math.log(20132.66), math.log(80530.64))), 20132.66, 80530.64),
    }


BETA_STAT = 0.9
BETA_SECOND = 0.99
RATE_EMBED = 10.0
RATE_CONV = 0.25
RATE_SCORE = 0.012
EPSILON = 1e-08

@jax.custom_vjp
def low(v):
    return lax.optimization_barrier(v.astype(jnp.bfloat16)).astype(jnp.float32)

@jax.custom_vjp
def low_back(v):
    return v

def low_keep(v):
    return (low(v), None)

def low_pass(kept, grad):
    return (grad,)

def back_keep(v):
    return (v, None)

def back_low(kept, grad):
    return (low(grad),)
low.defvjp(low_keep, low_pass)
low_back.defvjp(back_keep, back_low)

def pool_sizes(hidden):
    count_rows = hidden.shape[0]
    pooled = []
    for block_size in range(1, SIZES + 1):
        padded_len = -(-LEN // block_size) * block_size
        padded = jnp.pad(hidden, ((0, 0), (0, padded_len - LEN), (0, 0)))
        blocks = lax.optimization_barrier(jnp.sum(padded.reshape(count_rows, padded_len // block_size, block_size, D), axis=2)) / block_size
        pooled.append(jnp.repeat(blocks, block_size, axis=1)[:, :LEN])
    return pooled

def group_forward(embed_low, conv_low, score_in, group_ids, group_valid):
    highest = lax.Precision.HIGHEST
    count_rows = group_ids.shape[0]
    inputs = group_valid[:, :, None] * embed_low[group_ids]
    padded = jnp.pad(inputs, ((0, 0), (2, 2), (0, 0)))
    hidden = jnp.zeros((count_rows, LEN, D), inputs.dtype)
    for tap in range(TAPS):
        hidden = hidden + jnp.einsum('gld,de->gle', padded[:, tap:tap + LEN], conv_low[tap], precision=highest)
    hidden = low_back(group_valid[:, :, None] * hidden)
    pooled = pool_sizes(hidden)
    scores = jnp.stack([jnp.einsum('gld,d->gl', item, score_in, precision=highest) for item in pooled])
    size_probs = jax.nn.softmax(scores, axis=0)
    mixed = jnp.zeros_like(hidden)
    for level in range(SIZES):
        mixed = mixed + size_probs[level][:, :, None] * pooled[level]
    mixed = group_valid[:, :, None] * mixed
    output = lax.optimization_barrier(jnp.sum(mixed.reshape(count_rows, HALF, 2, D), axis=2)) * 0.5
    entropy_part = jnp.sum(group_valid * -lax.optimization_barrier(jnp.sum(size_probs * jnp.log(size_probs), axis=0)))
    return (output, entropy_part)

def shampoo(grad, weight, left, right, left_root, right_root, rate):
    highest = lax.Precision.HIGHEST
    new_left = BETA_STAT * left + (1.0 - BETA_STAT) * jnp.dot(grad, grad.T, precision=highest)
    new_right = BETA_STAT * right + (1.0 - BETA_STAT) * jnp.dot(grad.T, grad, precision=highest)
    step = jnp.dot(jnp.dot(left_root, grad, precision=highest), right_root, precision=highest)
    return (weight - rate * step, new_left, new_right)

def reference(byte_ids, lengths, embed, conv, score, out_grad, embed_left, embed_right, conv_left, conv_right, embed_left_root, embed_right_root, conv_left_root, conv_right_root, score_second):
    valid = (jnp.arange(LEN, dtype=jnp.int32)[None, :] < lengths[:, None]).astype(jnp.float32)
    grouped_ids = byte_ids.reshape(ROWS // 2, 2, LEN)
    grouped_valid = valid.reshape(ROWS // 2, 2, LEN)

    def whole(embed_in, conv_in, score_in):
        embed_low = low(embed_in)
        conv_low = low(conv_in)

        def one_group(carry, pieces):
            group_ids, group_valid = pieces
            output, entropy_part = group_forward(embed_low, conv_low, score_in, group_ids, group_valid)
            return (carry + entropy_part, output)
        entropy_sum, outputs = lax.scan(jax.checkpoint(one_group), jnp.zeros((), jnp.float32), (grouped_ids, grouped_valid))
        return (outputs.reshape(ROWS, HALF, D), entropy_sum)
    output, pullback, entropy_sum = jax.vjp(whole, embed, conv, score, has_aux=True)
    embed_grad, conv_grad, score_grad = pullback(out_grad)
    entropy = entropy_sum / jnp.sum(valid)
    new_embed, new_embed_left, new_embed_right = shampoo(embed_grad, embed, embed_left, embed_right, embed_left_root, embed_right_root, RATE_EMBED)
    conv_rule = jax.vmap(partial(shampoo, rate=RATE_CONV))
    new_conv, new_conv_left, new_conv_right = conv_rule(conv_grad, conv, conv_left, conv_right, conv_left_root, conv_right_root)
    new_score_second = BETA_SECOND * score_second + (1.0 - BETA_SECOND) * score_grad * score_grad
    new_score = score - RATE_SCORE * score_grad / (jnp.sqrt(new_score_second) + EPSILON)
    return (output, entropy, embed_grad, conv_grad, score_grad, new_embed, new_conv, new_score, new_embed_left, new_embed_right, new_conv_left, new_conv_right, new_score_second)
```

```python
from functools import partial

import jax
import jax.numpy as jnp
from jax import lax
from jax.experimental import pallas as pl
from jax.experimental.pallas import tpu as pltpu
from jax.sharding import PartitionSpec as P

VOCAB = 256
SIZES = 4
BETA_STAT = 0.9
BETA_SECOND = 0.99
RATE_EMBED = 10.0
RATE_CONV = 0.25
RATE_SCORE = 0.012
EPSILON = 1e-08
TILE = 128
HALO = 8
BLOCKS = 32
WIN = TILE // 2 + 16
BF = jnp.bfloat16
F32 = jnp.float32


def split(v):
    high = v.astype(BF)
    return high, (v - high.astype(F32)).astype(BF)


def roll_to(v, offset):
    width = v.shape[-1]
    return v if offset == 0 else pltpu.roll(v, (-offset) % width, v.ndim - 1)


def lookup_body(where_ref, mid_ref, g_ref, gh_ref, score_ref, near_ref, far_ref, hid_ref, rim_ref, band_ref, gext, table_ref, *, masks, taps):
    length = hid_ref.shape[1] * TILE
    half = length // 2
    blocks = table_ref.shape[1] // TILE
    slots = near_ref.shape[1] // len(masks[0])

    @pl.when(pl.program_id(0) == 0)
    def _():
        for h in range(2):
            for spot in range(near_ref.shape[1]):
                for other, source in enumerate((near_ref, far_ref)):
                    group = 2 * (where_ref[1] ^ masks[h][spot // slots]) + ((where_ref[0] & 1) ^ other)
                    unit = group * slots + spot % slots

                    @pl.when(unit < taps * blocks)
                    def _():
                        row = pl.multiple_of((h * taps + unit // blocks) * VOCAB, VOCAB)
                        column = pl.multiple_of(unit % blocks * TILE, TILE)
                        table_ref[pl.ds(row, VOCAB), pl.ds(column, TILE)] = source[h, spot]

    gext[0:8] = gh_ref[0, 0:8]
    gext[8 : half + 8] = g_ref[0]
    gext[half + 8 : half + 16] = gh_ref[0, 8:16]
    nt = (((1,), (1,)), ((), ()))
    tiles = length // TILE
    mid = mid_ref[0]
    rim = jnp.where(lax.broadcasted_iota(jnp.int32, (8, TILE), 1) < TILE // 2, mid[:, TILE + length :], mid[:, 0:TILE])
    mid = jnp.concatenate([mid[:, TILE : TILE + length], pltpu.roll(rim, HALO, 1)], axis=1)
    cells = lax.broadcasted_iota(jnp.int32, (VOCAB, length + TILE), 0)
    hits = [(mid[k : k + 1] == cells).astype(F32).astype(BF) for k in range(taps)]
    onehot = jnp.concatenate(hits + hits, axis=0)[:, 0 : length + 2 * HALO]
    for n in range(0, table_ref.shape[1], 256):
        h_high, h_low = split(
            lax.dot_general(onehot, table_ref[:, n : n + 256], (((0,), (0,)), ((), ())), preferred_element_type=F32)
        )
        for i in range(tiles):
            hid_ref[0, i, 0:TILE, n : n + 256] = h_high[i * TILE : (i + 1) * TILE]
            hid_ref[0, i, TILE : 2 * TILE, n : n + 256] = h_low[i * TILE : (i + 1) * TILE]
        rim_ref[0, 0:16, n : n + 256] = h_high[length:]
        rim_ref[0, 16:32, n : n + 256] = h_low[length:]
    for i in range(length // TILE):
        g_high, g_low = split(gext[i * TILE // 2 : i * TILE // 2 + WIN])
        left = jnp.concatenate([g_high, g_low, score_ref[0:16]], axis=0)
        gram = lax.dot_general(left, hid_ref[0, i], nt, preferred_element_type=F32)
        band = gram[0:WIN, 0:TILE] + gram[WIN : 2 * WIN, 0:TILE] + gram[0:WIN, TILE:]
        dots = gram[2 * WIN : 2 * WIN + 1, 0:TILE] + gram[2 * WIN + 1 : 2 * WIN + 2, 0:TILE] + gram[2 * WIN : 2 * WIN + 1, TILE:]
        place = lax.broadcasted_iota(jnp.int32, (WIN, TILE), 0) - 8
        gap = place - (lax.broadcasted_iota(jnp.int32, (WIN, TILE), 1) >> 1)
        rows = [jnp.sum(jnp.where(gap == d, band, 0.0), axis=0, keepdims=True) for d in (-1, 0, 1)]
        band_ref[0, :, TILE * (i + 1) : TILE * (i + 2)] = jnp.concatenate(rows + [dots, jnp.zeros((4, TILE), F32)], axis=0)
    rims = rim_ref[0]
    g_high, g_low = split(jnp.concatenate([gext[0:16], gext[half : half + 16]], axis=0))
    gram = lax.dot_general(jnp.concatenate([g_high, g_low, score_ref[0:16]], axis=0), rims, nt, preferred_element_type=F32)
    band = gram[0:32, 0:16] + gram[32:64, 0:16] + gram[0:32, 16:32]
    dots = gram[64:65, 0:16] + gram[65:66, 0:16] + gram[64:65, 16:32]
    row = lax.broadcasted_iota(jnp.int32, (32, 16), 0)
    lane = lax.broadcasted_iota(jnp.int32, (32, 16), 1)
    place = jnp.where(row < 16, row - 8, half - 24 + row)
    spot = jnp.where(lane < 8, lane - 8, length + lane - 8)
    gap = place - (spot >> 1)
    rows = [jnp.sum(jnp.where(gap == d, band, 0.0), axis=0, keepdims=True) for d in (-1, 0, 1)]
    both = jnp.concatenate(rows + [dots, jnp.zeros((4, 16), F32)], axis=0)
    both = pltpu.roll(jnp.concatenate([both, jnp.zeros((8, TILE - 16), F32)], axis=1), TILE - 8, 1)
    band_ref[0, :, 0:TILE] = both
    band_ref[0, :, TILE + length :] = both


def lookup(where, mid, out_grad, grad_rim, score_rows, near, far, masks, taps):
    rows, _, span = mid.shape
    half, width = out_grad.shape[1:]
    tiles = 2 * half // TILE
    whole = lambda *shape: pl.BlockSpec(shape, lambda r: (0,) * len(shape), pipeline_mode=pl.Buffered(1))
    by_row = lambda *shape: pl.BlockSpec((1, *shape), lambda r: (r,) + (0,) * len(shape))
    return pl.pallas_call(
        partial(lookup_body, masks=masks, taps=taps),
        grid=(rows,),
        in_specs=[
            pl.BlockSpec(memory_space=pltpu.SMEM),
            by_row(8, span),
            by_row(half, width),
            by_row(16, width),
            whole(*score_rows.shape),
            whole(*near.shape),
            whole(*far.shape),
        ],
        out_specs=[by_row(tiles, 2 * TILE, width), by_row(32, width), by_row(8, span)],
        out_shape=[
            jax.ShapeDtypeStruct((rows, tiles, 2 * TILE, width), BF),
            jax.ShapeDtypeStruct((rows, 32, width), BF),
            jax.ShapeDtypeStruct((rows, 8, span), F32),
        ],
        scratch_shapes=[
            pltpu.VMEM((half + 16, width), F32),
            pltpu.VMEM((2 * taps * VOCAB, width), BF),
        ],
        compiler_params=pltpu.CompilerParams(vmem_limit_bytes=56 << 20),
    )(where, mid, out_grad, grad_rim, score_rows, near, far)


def weigh_body(band_ref, lengths_ref, start_ref, out_ref, sums_ref):
    rows, _, span = band_ref.shape
    length = span - 2 * TILE
    start = start_ref[0]
    lane = lax.broadcasted_iota(jnp.int32, (rows, span), 1)
    place = start + lane - TILE
    valid = ((place >= 0) & (place < lengths_ref[...])).astype(F32)
    phase3 = lax.rem(place + 3 * TILE, 3)
    phase4 = place & 3
    even = (place & 1) == 0
    inside = {
        1: {0: None},
        2: {0: None, 1: even, -1: ~even},
        3: {0: None, 1: phase3 <= 1, 2: phase3 == 0, -1: phase3 >= 1, -2: phase3 == 2},
        4: {0: None, **{d: phase4 <= 3 - d for d in (1, 2, 3)}, **{-d: phase4 >= d for d in (1, 2, 3)}},
    }

    def over_block(size, pick):
        total = pick(0)
        for d, mask in inside[size].items():
            if d != 0:
                total = total + jnp.where(mask, pick(d), 0.0)
        return total

    def shifts(v):
        return {d: roll_to(v, d) for d in range(-3, 4)}

    dots = shifts(band_ref[:, 3, :] * valid)
    scores = [over_block(b, lambda d: dots[d]) * (1.0 / b) for b in range(1, SIZES + 1)]
    highest = jnp.maximum(jnp.maximum(scores[0], scores[1]), jnp.maximum(scores[2], scores[3]))
    powers = [jnp.exp(item - highest) for item in scores]
    total = powers[0] + powers[1] + powers[2] + powers[3]
    probs = [item / total for item in powers]
    log_total = jnp.log(total)
    entropy = jnp.zeros_like(total)
    for b in range(SIZES):
        entropy = entropy - probs[b] * (scores[b] - highest - log_total)
    own = (lane >= TILE) & (lane < TILE + length)
    own_valid = jnp.where(own, valid, 0.0)
    entropy = jnp.sum(jnp.where(own, entropy * valid, 0.0), axis=1, keepdims=True)
    count = jnp.sum(own_valid, axis=1, keepdims=True)
    sums_ref[...] = jnp.where(lax.broadcasted_iota(jnp.int32, (rows, TILE), 1) == 0, entropy, count)
    below, same, above = (shifts(band_ref[:, d, :] * valid) for d in range(3))
    near = {0: same[0], 1: jnp.where(even, same[1], below[1]), 2: below[2], 3: below[3]}
    near.update({-1: jnp.where(even, above[-1], same[-1]), -2: above[-2], -3: above[-3]})
    inner = [over_block(b, lambda d: near[d]) * (valid * (0.5 / b)) for b in range(1, SIZES + 1)]
    mean = probs[0] * inner[0] + probs[1] * inner[1] + probs[2] * inner[2] + probs[3] * inner[3]
    score_in = [probs[b] * (inner[b] - mean) for b in range(SIZES)]
    pull = jnp.zeros_like(total)
    for b in range(1, SIZES + 1):
        moved = shifts(score_in[b - 1])
        pull = pull + over_block(b, lambda d: moved[d]) * (1.0 / b)
    weight = {d: jnp.zeros_like(total) for d in range(-3, 4)}
    for b in range(1, SIZES + 1):
        moved = shifts(probs[b - 1] * valid * (0.5 / b))
        for d, mask in inside[b].items():
            weight[d] = weight[d] + (moved[d] if mask is None else jnp.where(mask, moved[d], 0.0))
    out_ref[:, 0, :] = valid * (weight[-2] + jnp.where(even, weight[-1], weight[-3]))
    out_ref[:, 1, :] = valid * (weight[0] + jnp.where(even, weight[1], weight[-1]))
    out_ref[:, 2, :] = valid * (weight[2] + jnp.where(even, weight[3], weight[1]))
    out_ref[:, 3, :] = valid * pull
    for d in range(4, 8):
        out_ref[:, d, :] = jnp.zeros_like(total)


def weigh(band, lengths, start):
    rows, _, span = band.shape
    vmem = pl.BlockSpec(memory_space=pltpu.VMEM)
    return pl.pallas_call(
        weigh_body,
        in_specs=[vmem, vmem, pl.BlockSpec(memory_space=pltpu.SMEM)],
        out_specs=[vmem, vmem],
        out_shape=[jax.ShapeDtypeStruct(band.shape, F32), jax.ShapeDtypeStruct((rows, TILE), F32)],
    )(band, lengths.reshape(rows, 1), start.reshape(1))


def apply_body(
    me_ref, mid_ref, g_ref, gh_ref, score_ref, hid_ref, rim_ref, weight_ref, sums_ref,
    out_ref, keep_ref, send_ref, extra_ref, onehot, hgrad, gext, total, table_ref, pull_ref,
):
    length = hid_ref.shape[1] * TILE
    half = length // 2
    taps = table_ref.shape[0] // VOCAB

    @pl.when(pl.program_id(0) == 0)
    def _():
        table_ref[...] = jnp.zeros_like(table_ref)
        pull_ref[...] = jnp.zeros_like(pull_ref)

    cells = lax.broadcasted_iota(jnp.int32, (VOCAB, length), 0)
    for tap in range(taps):
        hit = mid_ref[0, tap : tap + 1, TILE : TILE + length] == cells
        onehot[tap * VOCAB : (tap + 1) * VOCAB] = hit.astype(F32).astype(BF)
    gext[0:8] = gh_ref[0, 0:8]
    gext[8 : half + 8] = g_ref[0]
    gext[half + 8 : half + 16] = gh_ref[0, 8:16]
    total[...] = jnp.zeros_like(total)
    pulled = jnp.zeros((1, total.shape[1]), F32)
    for i in range(length // TILE):
        w = weight_ref[0, :, TILE * (i + 1) : TILE * (i + 2)]
        place = lax.broadcasted_iota(jnp.int32, (WIN, TILE), 0) - 8
        gap = place - (lax.broadcasted_iota(jnp.int32, (WIN, TILE), 1) >> 1)
        a = jnp.where(gap == 0, w[1:2], 0.0)
        a = jnp.where(gap == -1, w[0:1], a)
        a = jnp.where(gap == 1, w[2:3], a)
        a_high, a_low = split(a)
        q_high, q_low = split(w[3:4])
        sub = lax.broadcasted_iota(jnp.int32, (16, TILE), 0)
        q = jnp.where(sub < 2, q_high.astype(F32), jnp.where(sub == 2, q_low.astype(F32), 0.0)).astype(BF)
        g_high, g_low = split(gext[i * TILE // 2 : i * TILE // 2 + WIN])
        stack = jnp.concatenate([g_high, g_low, g_high, score_ref[16:32]], axis=0)
        left = jnp.concatenate([a_high, a_high, a_low, q], axis=0)
        hg = lax.dot_general(left, stack, (((0,), (0,)), ((), ())), preferred_element_type=F32)
        hgrad[i * TILE : (i + 1) * TILE] = hg.astype(BF)
        left = jnp.concatenate([a_high, a_low, q], axis=0)
        res = jnp.dot(jnp.concatenate([left, left], axis=1), hid_ref[0, i], preferred_element_type=F32)
        total[i * TILE // 2 : i * TILE // 2 + WIN] += res[0:WIN] + res[WIN : 2 * WIN]
        pulled = pulled + res[2 * WIN : 2 * WIN + 1] + res[2 * WIN + 2 : 2 * WIN + 3]
    lane = lax.broadcasted_iota(jnp.int32, (8, TILE), 1)
    w = jnp.where(lane < 64, weight_ref[0, :, TILE + length :], weight_ref[0, :, 0:TILE])
    w = pltpu.roll(w, 8, 1)[:, 0:16]
    row = lax.broadcasted_iota(jnp.int32, (32, 16), 0)
    lane = lax.broadcasted_iota(jnp.int32, (32, 16), 1)
    place = jnp.where(row < 16, row - 8, half - 24 + row)
    spot = jnp.where(lane < 8, lane - 8, length + lane - 8)
    gap = place - (spot >> 1)
    a = jnp.where(gap == 0, w[1:2], 0.0)
    a = jnp.where(gap == -1, w[0:1], a)
    a = jnp.where(gap == 1, w[2:3], a)
    a_high, a_low = split(a)
    left = jnp.concatenate([a_high, a_low], axis=0)
    res = jnp.dot(jnp.concatenate([left, left], axis=1), rim_ref[0], preferred_element_type=F32)
    res = res[0:32] + res[32:64]
    total[8:16] += res[8:16]
    total[half : half + 8] += res[16:24]
    out_ref[0] = total[8 : half + 8]
    pull_ref[0:1] += pulled
    table_ref[...] += jnp.dot(onehot[...], hgrad[...], preferred_element_type=F32)

    @pl.when(pl.program_id(0) == pl.num_programs(0) - 1)
    def _():
        row = lax.broadcasted_iota(jnp.int32, pull_ref.shape, 0)
        lane = lax.broadcasted_iota(jnp.int32, pull_ref.shape, 1)
        counts = jnp.sum(sums_ref[...], axis=0, keepdims=True)
        counts = jnp.concatenate([counts] + [jnp.zeros_like(counts)] * (pull_ref.shape[1] // TILE - 1), axis=1)
        extra = jnp.where((row == 1) & (lane < 2), counts, pull_ref[...])
        part = extra.shape[1] // 2
        block = table_ref.shape[0] // BLOCKS
        for h in range(2):
            extra_ref[h] = extra[:, h * part : (h + 1) * part]
            send_ref[h, BLOCKS // 2 * block :] = extra[:, h * part : (h + 1) * part]
            for p in range(BLOCKS):
                source = pl.multiple_of((me_ref[h] ^ p) * block, 8)
                rows = table_ref[pl.ds(source, block), h * part : (h + 1) * part]
                target = keep_ref if p < BLOCKS // 2 else send_ref
                target[h, p % (BLOCKS // 2) * block : (p % (BLOCKS // 2) + 1) * block] = rows


def apply_weights(me, mid, out_grad, grad_rim, score_rows, hid, rim, weight, sums, taps):
    rows, _, span = mid.shape
    half, width = out_grad.shape[1:]
    tiles = 2 * half // TILE
    whole = lambda *shape: pl.BlockSpec(shape, lambda r: (0,) * len(shape), pipeline_mode=pl.Buffered(1))
    by_row = lambda *shape: pl.BlockSpec((1, *shape), lambda r: (r,) + (0,) * len(shape))
    return pl.pallas_call(
        apply_body,
        grid=(rows,),
        in_specs=[
            pl.BlockSpec(memory_space=pltpu.SMEM),
            by_row(8, span),
            by_row(half, width),
            by_row(16, width),
            whole(*score_rows.shape),
            by_row(tiles, 2 * TILE, width),
            by_row(32, width),
            by_row(8, span),
            whole(*sums.shape),
        ],
        out_specs=[
            by_row(half, width),
            whole(2, taps * VOCAB // 2, width // 2),
            whole(2, taps * VOCAB // 2 + 8, width // 2),
            whole(2, 8, width // 2),
        ],
        out_shape=[
            jax.ShapeDtypeStruct((rows, half, width), F32),
            jax.ShapeDtypeStruct((2, taps * VOCAB // 2, width // 2), F32),
            jax.ShapeDtypeStruct((2, taps * VOCAB // 2 + 8, width // 2), F32),
            jax.ShapeDtypeStruct((2, 8, width // 2), F32),
        ],
        scratch_shapes=[
            pltpu.VMEM((taps * VOCAB, 2 * half), BF),
            pltpu.VMEM((2 * half, width), BF),
            pltpu.VMEM((half + 16, width), F32),
            pltpu.VMEM((half + 16, width), F32),
            pltpu.VMEM((taps * VOCAB, width), F32),
            pltpu.VMEM((8, width), F32),
        ],
        compiler_params=pltpu.CompilerParams(vmem_limit_bytes=56 << 20),
    )(me, mid, out_grad, grad_rim, score_rows, hid, rim, weight, sums)


def shifted_rim(cells, width):
    count = lax.axis_size("seq")
    head, tail = cells[:, :width], cells[:, cells.shape[1] - width :]
    left = lax.ppermute(tail, "seq", [(i, i + 1) for i in range(count - 1)])
    right = lax.ppermute(head, "seq", [(i + 1, i) for i in range(count - 1)])
    return left, right


def marked_ids(byte_ids, lengths, start, taps):
    rows, length = byte_ids.shape
    left, right = shifted_rim(byte_ids, HALO)
    near = jnp.concatenate([left, byte_ids, right], axis=1)
    place = start - HALO + jnp.arange(length + 2 * HALO, dtype=jnp.int32)
    valid = (place[None, :] >= 0) & (place[None, :] < lengths[:, None])
    near = jnp.where(valid, near, -1)
    near = jnp.pad(near, ((0, 0), (TILE - HALO + 2, TILE - HALO + 2)), constant_values=-1)
    span = length + 2 * TILE
    lists = [near[:, k : k + span] for k in range(taps)]
    lists += [jnp.full((rows, span), -1, jnp.int32)] * (8 - taps)
    return jnp.stack(lists, axis=1)


NN = (((1,), (0,)), ((), ()))
NT = (((1,), (1,)), ((), ()))
TN = (((0,), (0,)), ((), ()))


def dot(a, b, dims):
    return lax.dot_general(a, b, dims, preferred_element_type=F32)


def dot2(a, pair, dims):
    return dot(a, pair[0], dims) + dot(a, pair[1], dims)


def dot3(left, right, dims):
    return dot(left[0], right[0], dims) + dot(left[0], right[1], dims) + dot(left[1], right[0], dims)


def bits_of(count):
    return [1 << i for i in range(count.bit_length() - 1)]


def exchange_plan(seq_size, dp_size):
    across = bits_of(seq_size)
    half = len(across) // 2
    along = [("dp", 2 * bit) for bit in reversed(bits_of(dp_size // 2))]
    orders = [across, across[half:] + across[:half]]
    return [[("dp", 1)] + [("seq", bit) for bit in order] + along for order in orders]


def block_index(plan):
    index = jnp.int32(0)
    for axis, bit in plan[: BLOCKS.bit_length() - 1]:
        index = 2 * index + ((lax.axis_index(axis) & bit) != 0).astype(jnp.int32)
    return index


def swap(cells, axis, bit):
    return lax.ppermute(cells, axis, [(i, i ^ bit) for i in range(lax.axis_size(axis))])


def pack_body(where_ref, conv_ref, embed_ref, out_ref, *, slots):
    taps, own, width = conv_ref.shape
    rows = embed_ref.shape[0]
    blocks = width // TILE
    for j in range(blocks):
        out_ref[j * rows : (j + 1) * rows] = embed_ref[:, j * TILE : (j + 1) * TILE].astype(BF)
    for i in range(2 * slots):
        group = 2 * where_ref[1] + ((where_ref[0] & 1) ^ (i // slots))
        unit = jnp.minimum(group * slots + i % slots, taps * blocks - 1)
        column = pl.multiple_of(unit % blocks * TILE, TILE)
        first = blocks * rows + i * own
        out_ref[first : first + own] = conv_ref[unit // blocks, :, pl.ds(column, TILE)].astype(BF)


def pack_weights(where, conv, embed, slots):
    vmem = pl.BlockSpec(memory_space=pltpu.VMEM)
    rows = embed.shape[0] * embed.shape[1] // TILE + 2 * slots * conv.shape[1]
    return pl.pallas_call(
        partial(pack_body, slots=slots),
        in_specs=[pl.BlockSpec(memory_space=pltpu.SMEM), vmem, vmem],
        out_specs=vmem,
        out_shape=jax.ShapeDtypeStruct((rows, TILE), BF),
    )(where, conv, embed)


def tables_body(where_ref, score_ref, *refs, slots, own, rows):
    *near, far_ref, embed_ref, stack_ref, high_ref, low_ref, units = refs
    blocks = embed_ref.shape[1] // TILE
    first = blocks * rows
    for m, near_ref in enumerate(near):
        for other in range(2):
            source = far_ref.at[m] if other else near_ref
            place = where_ref[0] ^ (2 * m + other)
            for j in range(blocks):
                embed_ref[pl.ds(pl.multiple_of(place * rows, 16), rows), j * TILE : (j + 1) * TILE] = source[
                    j * rows : (j + 1) * rows
                ]
            for t in range(slots):
                units[t, pl.ds(pl.multiple_of(place * own, 16), own)] = source[first + t * own : first + (t + 1) * own]
    for t in range(slots):
        high, low = split(jnp.dot(embed_ref[...], units[t], preferred_element_type=F32))
        high_ref[t], low_ref[t] = high, low
    high, low = (part.astype(F32) for part in split(score_ref[...]))
    row = lax.broadcasted_iota(jnp.int32, stack_ref.shape, 0)
    highs, lows = (row == 0) | (row == 16) | (row == 18), (row == 1) | (row == 17)
    stack_ref[...] = jnp.where(highs, high, jnp.where(lows, low, 0.0)).astype(BF)


def make_tables(where, score, near, far, slots, own, rows):
    width = score.shape[0]
    vmem = pl.BlockSpec(memory_space=pltpu.VMEM)
    unit = jax.ShapeDtypeStruct((slots, VOCAB, TILE), BF)
    return pl.pallas_call(
        partial(tables_body, slots=slots, own=own, rows=rows),
        in_specs=[pl.BlockSpec(memory_space=pltpu.SMEM)] + [vmem] * (len(near) + 2),
        out_specs=[vmem] * 4,
        out_shape=[jax.ShapeDtypeStruct((VOCAB, width), BF), jax.ShapeDtypeStruct((32, width), BF), unit, unit],
        scratch_shapes=[pltpu.VMEM((slots, width, TILE), BF)],
    )(where, score.reshape(1, width), *near, far)


def gather_tables(where, embed, conv, score, rims):
    taps, own, width = conv.shape
    rows = embed.shape[0]
    seq, chips = lax.axis_size("seq"), lax.axis_size("dp") // 2
    slots = -(-taps * (width // TILE) // (2 * seq))
    pack = pack_weights(where, conv, embed, slots)
    near = [pack] + [swap(pack, "dp", 2 * m) for m in range(1, chips)]
    first = rows * width // TILE
    other = first + slots * own
    far = swap(jnp.stack([jnp.concatenate([item[:first], item[other:]], axis=0) for item in near]), "dp", 1)
    far, rims = lax.optimization_barrier((far, rims))
    embed_all, score_rows, *parts = make_tables(where, score, near, far, slots, own, rows)
    across = bits_of(seq)
    masks = []
    for h in range(2):
        found = [0]
        half = len(across) // 2
        for bit in across[half:] + across[:half] if h else across:
            parts[h] = jnp.concatenate([parts[h], swap(parts[h], "seq", bit)], axis=0)
            found = found + [mask ^ bit for mask in found]
        masks.append(found)
    units = jnp.stack(parts)
    return embed_all, score_rows, units, swap(units, "dp", 1), masks, rims


def sum_over_devices(keep, send, extra, plans, ready):
    block = keep.shape[1] // (BLOCKS // 2)
    depth = BLOCKS.bit_length() - 1
    got = swap(send, "dp", 1)
    cells = keep + got[:, : keep.shape[1]]
    extra = extra + got[:, keep.shape[1] :]
    across = len([axis for axis, _ in plans[0] if axis == "seq"])
    parts, extras = [], []
    for h in range(2):
        part, more = cells[h], extra[h]
        for step, (axis, bit) in enumerate(plans[h][1 : 1 + across]):
            if step == 1 and h == 0:
                part, ready = lax.optimization_barrier((part, ready))
            rest = part.shape[0] // 2
            got = swap(jnp.concatenate([part[rest:], more], axis=0), axis, bit)
            part, more = part[:rest] + got[:rest], more + got[rest:]
        parts.append(part)
        extras.append(more)
    cells, extra = jnp.stack(parts), jnp.stack(extras)
    along = 1 << (depth - 1 - across)
    if along > 1:
        got = [
            swap(jnp.concatenate([cells[:, m * block : (m + 1) * block], extra], axis=1), "dp", 2 * m)
            for m in range(1, along)
        ]
        cells, extra = cells[:, :block], extra
        for item in got:
            cells, extra = cells + item[:, :block], extra + item[:, block:]
    for axis, bit in plans[0][depth:]:
        got = swap(jnp.concatenate([cells, extra], axis=1), axis, bit)
        cells, extra = cells + got[:, :block], extra + got[:, block:]
    if along > 1:
        cells = jnp.concatenate([cells] + [swap(cells, "dp", 2 * m) for m in range(1, along)], axis=1)
    parts = []
    for h in range(2):
        part = cells[h]
        for axis, bit in reversed(plans[h][1 : 1 + across]):
            part = jnp.concatenate([part, swap(part, axis, bit)], axis=0)
        parts.append(part)
    cells = jnp.stack(parts)
    return cells, swap(cells, "dp", 1), extra, ready


def pick_rows(count, total, first):
    row = lax.broadcasted_iota(jnp.int32, (count, total), 0)
    return (lax.broadcasted_iota(jnp.int32, (count, total), 1) == row + first).astype(F32).astype(BF)


def order_body(me_ref, near_ref, far_ref, conv_ref, high_ref, low_ref, grad_ref, table):
    block = table.shape[0] // BLOCKS
    part = table.shape[1] // 2
    for h in range(2):
        for p in range(BLOCKS):
            source = near_ref if p < BLOCKS // 2 else far_ref
            rows = source[h, p % (BLOCKS // 2) * block : (p % (BLOCKS // 2) + 1) * block]
            table[pl.ds(pl.multiple_of((me_ref[h] ^ p) * block, 8), block), h * part : (h + 1) * part] = rows
    taps = conv_ref.shape[0]
    total = jnp.zeros(grad_ref.shape, F32)
    for k in range(taps):
        pair = split(table[k * VOCAB : (k + 1) * VOCAB])
        high_ref[k], low_ref[k] = pair
        total = total + dot2(conv_ref[k], pair, NT)
    grad_ref[...] = total


def order_table(me, near, far, conv_low):
    taps, own, width = conv_low.shape
    vmem = pl.BlockSpec(memory_space=pltpu.VMEM)
    table = jax.ShapeDtypeStruct((taps, VOCAB, width), BF)
    return pl.pallas_call(
        order_body,
        in_specs=[pl.BlockSpec(memory_space=pltpu.SMEM), vmem, vmem, vmem],
        out_specs=[vmem, vmem, vmem],
        out_shape=[table, table, jax.ShapeDtypeStruct((own, VOCAB), F32)],
        scratch_shapes=[pltpu.VMEM((taps * VOCAB, width), F32)],
        compiler_params=pltpu.CompilerParams(vmem_limit_bytes=60 << 20),
    )(me, near, far, conv_low)


def dot2_left(pair, b, dims):
    return dot(pair[0], b, dims) + dot(pair[1], b, dims)


def both(left, right, dims):
    count = left[0].shape[0]
    first = dot(jnp.concatenate(left, axis=0), right[0], dims)
    return first[:count] + first[count:] + dot(left[0], right[1], dims)


def ready_body(where_ref, embed_ref, left_root_ref, right_root_ref, square_high, square_low, columns_ref, rooted_high, rooted_low, right_high, right_low):
    own, width = left_root_ref.shape[1:]
    embed = embed_ref[...]

    @pl.when(pl.program_id(0) == 0)
    def _():
        square_high[...], square_low[...] = split(dot(embed, embed, NT))
        columns_ref[...] = dot(pick_rows(own, width, where_ref[0] * own), embed, NT).astype(BF)

    rooted_high[0], rooted_low[0] = split(dot2_left(split(left_root_ref[0]), embed, NT))
    right_high[0], right_low[0] = split(right_root_ref[0])


def make_ready(where, embed_all, left_root, right_root):
    taps, own, width = left_root.shape
    by_tap = lambda *shape: pl.BlockSpec((1, *shape), lambda k: (k,) + (0,) * len(shape))
    whole = lambda *shape: pl.BlockSpec(shape, lambda k: (0,) * len(shape))
    like = lambda *shape: jax.ShapeDtypeStruct(shape, BF)
    return pl.pallas_call(
        ready_body,
        grid=(taps,),
        in_specs=[
            pl.BlockSpec(memory_space=pltpu.SMEM),
            whole(VOCAB, width),
            by_tap(own, width),
            by_tap(width, width),
        ],
        out_specs=[whole(VOCAB, VOCAB)] * 2 + [whole(own, VOCAB)] + [by_tap(own, VOCAB)] * 2 + [by_tap(width, width)] * 2,
        out_shape=[like(VOCAB, VOCAB)] * 2
        + [like(own, VOCAB)]
        + [like(taps, own, VOCAB)] * 2
        + [like(taps, width, width)] * 2,
        compiler_params=pltpu.CompilerParams(vmem_limit_bytes=60 << 20),
        cost_estimate=pl.CostEstimate(flops=4 << 30, bytes_accessed=32 << 20, transcendentals=0),
    )(where, embed_all, left_root, right_root)


def conv_body(
    where_ref, high_ref, low_ref, embed_ref, square_high, square_low, columns_ref, rooted_high, rooted_low, right_high, right_low,
    weight_ref, left_ref, right_ref, grad_out, weight_out, left_out, right_out,
):
    own, width = weight_ref.shape[1:]
    table = high_ref[0], low_ref[0]
    columns = columns_ref[...]
    pick = pick_rows(own, width, where_ref[0] * own)
    high = dot(jnp.concatenate([columns, rooted_high[0], rooted_low[0]], axis=0), table[0], NN)
    low = dot(jnp.concatenate([columns, rooted_high[0]], axis=0), table[1], NN)
    grad = high[:own] + low[:own]
    inner = high[own : 2 * own] + high[2 * own :] + low[own:]
    grad_out[0] = grad
    grad = split(grad)
    high = dot(jnp.concatenate([grad[0], grad[1], pick], axis=0), table[0], NT)
    low = dot(jnp.concatenate([grad[0], pick], axis=0), table[1], NT)
    crossed = split(high[:own] + high[own : 2 * own] + low[:own])
    mine = split(high[2 * own :] + low[own:])
    step = both(split(inner), (right_high[0], right_low[0]), NN)
    weight_out[0] = weight_ref[0] - RATE_CONV * step
    outer = dot(jnp.concatenate(crossed, axis=0), embed_ref[...], NN)
    left_out[0] = BETA_STAT * left_ref[0] + (1.0 - BETA_STAT) * (outer[:own] + outer[own:])
    outer = both(split(both(mine, (square_high[...], square_low[...]), NN)), table, NN)
    right_out[0] = BETA_STAT * right_ref[0] + (1.0 - BETA_STAT) * outer


def renew_conv(where, high, low, embed_all, ready, conv, left, right):
    taps, own, width = conv.shape
    by_tap = lambda *shape: pl.BlockSpec((1, *shape), lambda k: (k,) + (0,) * len(shape))
    whole = lambda *shape: pl.BlockSpec(shape, lambda k: (0,) * len(shape))
    rows = by_tap(own, width)
    return pl.pallas_call(
        conv_body,
        grid=(taps,),
        in_specs=[
            pl.BlockSpec(memory_space=pltpu.SMEM),
            by_tap(VOCAB, width),
            by_tap(VOCAB, width),
            whole(VOCAB, width),
            whole(VOCAB, VOCAB),
            whole(VOCAB, VOCAB),
            whole(own, VOCAB),
            by_tap(own, VOCAB),
            by_tap(own, VOCAB),
            by_tap(width, width),
            by_tap(width, width),
            rows,
            rows,
            rows,
        ],
        out_specs=[rows] * 4,
        out_shape=[jax.ShapeDtypeStruct(conv.shape, F32)] * 4,
        compiler_params=pltpu.CompilerParams(vmem_limit_bytes=60 << 20),
        cost_estimate=pl.CostEstimate(flops=8 << 30, bytes_accessed=32 << 20, transcendentals=0),
    )(where, high, low, embed_all, *ready, conv, left, right)


def embed_body(
    owner_ref, near_ref, far_ref, weight_ref, left_ref, right_ref, left_root_ref, right_root_ref,
    grad_out, weight_out, left_out, right_out, table,
):
    count, own, _ = near_ref.shape
    rows = weight_ref.shape[0]
    owner = owner_ref[0]
    for m in range(count):
        table[pl.ds(pl.multiple_of((owner ^ (2 * m)) * own, 8), own)] = near_ref[m]
        table[pl.ds(pl.multiple_of((owner ^ (2 * m + 1)) * own, 8), own)] = far_ref[m]
    pair = split(table[...])
    grad = dot2(pick_rows(rows, VOCAB, owner * rows), pair, NT)
    grad_out[...] = grad
    left_out[...] = BETA_STAT * left_ref[...] + (1.0 - BETA_STAT) * dot3(split(grad), pair, NN)
    right_out[...] = BETA_STAT * right_ref[...] + (1.0 - BETA_STAT) * dot3(split(near_ref[0]), pair, NT)
    step = dot3(split(dot3(split(left_root_ref[...]), pair, NT)), split(right_root_ref[...]), NN)
    weight_out[...] = weight_ref[...] - RATE_EMBED * step


def renew_embed(owner, near, far, embed, left, right, left_root, right_root):
    vmem = pl.BlockSpec(memory_space=pltpu.VMEM)
    shapes = [jax.ShapeDtypeStruct(item.shape, F32) for item in (embed, embed, left, right)]
    return pl.pallas_call(
        embed_body,
        in_specs=[pl.BlockSpec(memory_space=pltpu.SMEM)] + [vmem] * 7,
        out_specs=[vmem] * 4,
        out_shape=shapes,
        scratch_shapes=[pltpu.VMEM((embed.shape[1], VOCAB), F32)],
        compiler_params=pltpu.CompilerParams(vmem_limit_bytes=60 << 20),
    )(owner, near, far, embed, left, right, left_root, right_root)


def shards(
    byte_ids,
    lengths,
    embed,
    conv,
    score,
    out_grad,
    embed_left,
    embed_right,
    conv_left,
    conv_right,
    embed_left_root,
    embed_right_root,
    conv_left_root,
    conv_right_root,
    score_second,
):
    length = byte_ids.shape[1]
    width = embed.shape[1]
    taps = conv.shape[0]
    owner = lax.axis_index("dp")
    start = lax.axis_index("seq") * length
    conv_low = conv.astype(BF)
    where = jnp.stack([owner, lax.axis_index("seq")]).astype(jnp.int32)
    mid = marked_ids(byte_ids, lengths, start, taps)
    left, right = shifted_rim(out_grad, 1)
    zero = jnp.zeros((byte_ids.shape[0], 7, width), F32)
    grad_rim = jnp.concatenate([zero, left, right, zero], axis=1)
    embed_all, scores, near, far, masks, (mid, grad_rim) = gather_tables(where, embed, conv, score, (mid, grad_rim))
    hidden, rim, band = lookup(where, mid, out_grad, grad_rim, scores, near, far, masks, taps)
    weights, sums = weigh(band, lengths, start)
    plans = exchange_plan(lax.axis_size("seq"), lax.axis_size("dp"))
    me = jnp.stack([block_index(plan) for plan in plans])
    output, keep, send, extra = apply_weights(
        me, mid, out_grad, grad_rim, scores, hidden, rim, weights, sums, taps
    )
    ready = make_ready(where, embed_all, conv_left_root, conv_right_root)
    near, far, extra, ready = sum_over_devices(keep, send, extra, plans, ready)
    score_grad = extra[:, 0].reshape(width)
    entropy = extra[0, 1, 0] / extra[0, 1, 1]
    high, low, columns = order_table(me, near, far, conv_low)
    near = jnp.stack([columns] + [swap(columns, "dp", 2 * m) for m in range(1, lax.axis_size("dp") // 2)])
    conv_grad, new_conv, new_conv_left, new_conv_right = renew_conv(
        where, high, low, embed_all, ready, conv, conv_left, conv_right
    )
    near, conv_grad = lax.optimization_barrier((near, conv_grad))
    far = swap(near, "dp", 1)
    embed_grad, new_embed, new_embed_left, new_embed_right = renew_embed(
        where, near, far, embed, embed_left, embed_right, embed_left_root, embed_right_root
    )
    new_score_second = BETA_SECOND * score_second + (1.0 - BETA_SECOND) * score_grad * score_grad
    new_score = score - RATE_SCORE * score_grad / (jnp.sqrt(new_score_second) + EPSILON)
    return (
        output,
        entropy,
        embed_grad,
        conv_grad,
        score_grad,
        new_embed,
        new_conv,
        new_score,
        new_embed_left,
        new_embed_right,
        new_conv_left,
        new_conv_right,
        new_score_second,
    )


def solution(mesh):
    placed = (
        P("dp", "seq"),
        P("dp"),
        P("dp", None),
        P(None, "dp", None),
        P(),
        P("dp", "seq", None),
        P("dp", None),
        P("dp", None),
        P(None, "dp", None),
        P(None, "dp", None),
        P("dp", None),
        P(),
        P(None, "dp", None),
        P(),
        P(),
    )
    return jax.shard_map(
        shards,
        mesh=mesh,
        in_specs=placed,
        out_specs=(
            P("dp", "seq", None),
            P(),
            P("dp", None),
            P(None, "dp", None),
            P(),
            P("dp", None),
            P(None, "dp", None),
            P(),
            P("dp", None),
            P("dp", None),
            P(None, "dp", None),
            P(None, "dp", None),
            P(),
        ),
        check_vma=False,
    )
```

```python
from functools import partial

import jax
import jax.numpy as jnp
from jax import lax
from jax.experimental import pallas as pl
from jax.experimental.pallas import tpu as pltpu
from jax.sharding import PartitionSpec as P

VOCAB = 256
SIZES = 4
BETA_STAT = 0.9
BETA_SECOND = 0.99
RATE_EMBED = 10.0
RATE_CONV = 0.25
RATE_SCORE = 0.012
EPSILON = 1e-08
TILE = 128
HALO = 8
BLOCKS = 32
WIN = TILE // 2 + 16
BF = jnp.bfloat16
F32 = jnp.float32


def split(v):
    high = v.astype(BF)
    return high, (v - high.astype(F32)).astype(BF)


def exponent_of(v):
    return jnp.clip(jnp.floor(jnp.log2(jnp.maximum(v, 1e-30))) + 1.0, -90.0, 120.0)


def to_code(v, exponent):
    scaled = v * jnp.exp2(15.0 - exponent)
    code = jnp.clip(jnp.floor(scaled + 0.5), -32767.0, 32767.0)
    return code, scaled - code


def as_short(v):
    return v.astype(jnp.int32).astype(jnp.int16)


def as_float(v):
    return v.astype(jnp.int32).astype(F32)


def encode(rows, extra):
    exponent = exponent_of(jnp.max(jnp.abs(rows), axis=0, keepdims=True))
    code, _ = to_code(rows, exponent)
    few = extra[0:2]
    powers = exponent_of(jnp.abs(few))
    high, rest = to_code(few, powers)
    low = jnp.floor(rest * 16384.0 + 0.5)
    blank = jnp.zeros((9, rows.shape[1]), F32)
    return as_short(jnp.concatenate([code, exponent, high, low, powers, blank], axis=0))


def decode(cells):
    cells = as_float(cells)
    count = cells.shape[0] - 16
    more = cells[count:]
    extra = (more[1:3] + more[3:5] * (1.0 / 16384.0)) * jnp.exp2(more[5:7] - 15.0)
    extra = jnp.concatenate([extra, jnp.zeros((6, extra.shape[1]), F32)], axis=0)
    return cells[:count] * jnp.exp2(more[0:1] - 15.0), extra


def roll_to(v, offset):
    width = v.shape[-1]
    return v if offset == 0 else pltpu.roll(v, (-offset) % width, v.ndim - 1)


def score_rows(score_ref):
    high, low = (part.astype(F32) for part in split(score_ref[...]))
    row = lax.broadcasted_iota(jnp.int32, (16, high.shape[1]), 0)
    return jnp.where((row == 0) | (row == 2), high, jnp.where(row == 1, low, 0.0)).astype(BF)


def grad_window(g_ref, gh_ref, i, tiles):
    half = tiles * TILE // 2
    first, last = i * TILE // 2 - 8, (i + 1) * TILE // 2 + 8
    parts = [g_ref[0, max(first, 0) : min(last, half)]]
    if i == 0:
        parts = [gh_ref[0, 0:8]] + parts
    if i == tiles - 1:
        parts = parts + [gh_ref[0, 8:16]]
    return split(jnp.concatenate(parts, axis=0))


def lookup_body(
    where_ref, mid_ref, next_ref, g_ref, gh_ref, score_ref, near_ref, far_ref, hid_ref, rim_ref, band_ref, table_ref, onehot_ref,
    *, masks, taps,
):
    length = hid_ref.shape[1] * TILE
    blocks = table_ref.shape[1] // TILE
    slots = near_ref.shape[1] // len(masks[0])

    @pl.when(pl.program_id(0) == 0)
    def _():
        for h in range(2):
            for spot in range(near_ref.shape[1]):
                for other, source in enumerate((near_ref, far_ref)):
                    group = 2 * (where_ref[1] ^ masks[h][spot // slots]) + ((where_ref[0] & 1) ^ other)
                    unit = group * slots + spot % slots

                    @pl.when(unit < taps * blocks)
                    def _():
                        row = pl.multiple_of((h * taps + unit // blocks) * VOCAB, VOCAB)
                        column = pl.multiple_of(unit % blocks * TILE, TILE)
                        table_ref[pl.ds(row, VOCAB), pl.ds(column, TILE)] = source[h, spot]

    nt = (((1,), (1,)), ((), ()))
    tiles = length // TILE
    lanes = lax.broadcasted_iota(jnp.int32, (1, VOCAB), 1).astype(F32)

    def mark(ref):
        columns = jnp.transpose(ref[0].astype(F32))
        ids = [columns[TILE : TILE + length], columns[TILE - HALO : TILE], columns[TILE + length : TILE + length + HALO]]
        ids = jnp.concatenate(ids, axis=0)
        for k in range(taps):
            onehot_ref[:, k * VOCAB : (k + 1) * VOCAB] = (ids[:, k : k + 1] == lanes).astype(F32).astype(BF)

    @pl.when(pl.program_id(0) == 0)
    def _():
        mark(mid_ref)

    onehot = onehot_ref[...]
    onehot = jnp.concatenate([onehot, onehot], axis=1)
    for n in range(0, table_ref.shape[1], 256):
        hidden = jnp.dot(onehot, table_ref[:, n : n + 256], preferred_element_type=F32)
        h_high, h_low = split(hidden[0:length])
        for i in range(tiles):
            hid_ref[0, i, 0:TILE, n : n + 256] = h_high[i * TILE : (i + 1) * TILE]
            hid_ref[0, i, TILE : 2 * TILE, n : n + 256] = h_low[i * TILE : (i + 1) * TILE]
        rim_ref[0, :, n : n + 256] = hidden[length:]
    score = score_rows(score_ref)
    for i in range(tiles):
        left = jnp.concatenate([*grad_window(g_ref, gh_ref, i, tiles), score], axis=0)
        gram = lax.dot_general(left, hid_ref[0, i], nt, preferred_element_type=F32)
        band = gram[0:WIN, 0:TILE] + gram[WIN : 2 * WIN, 0:TILE] + gram[0:WIN, TILE:]
        dots = gram[2 * WIN : 2 * WIN + 1, 0:TILE] + gram[2 * WIN + 1 : 2 * WIN + 2, 0:TILE] + gram[2 * WIN : 2 * WIN + 1, TILE:]
        place = lax.broadcasted_iota(jnp.int32, (WIN, TILE), 0) - 8
        gap = place - (lax.broadcasted_iota(jnp.int32, (WIN, TILE), 1) >> 1)
        rows = [jnp.sum(jnp.where(gap == d, band, 0.0), axis=0, keepdims=True) for d in (-1, 0, 1)]
        band_ref[0, :, TILE * (i + 1) : TILE * (i + 2)] = jnp.concatenate(rows + [dots, jnp.zeros((4, TILE), F32)], axis=0)
    mark(next_ref)
    blank = jnp.zeros((8, TILE), F32)
    band_ref[0, :, 0:TILE] = blank
    band_ref[0, :, TILE + length :] = blank


def lookup(where, mid, out_grad, grad_rim, score, near, far, masks, taps):
    rows, _, span = mid.shape
    half, width = out_grad.shape[1:]
    length = 2 * half
    tiles = length // TILE
    whole = lambda *shape: pl.BlockSpec(shape, lambda r: (0,) * len(shape), pipeline_mode=pl.Buffered(1))
    by_row = lambda *shape: pl.BlockSpec((1, *shape), lambda r: (r,) + (0,) * len(shape))
    return pl.pallas_call(
        partial(lookup_body, masks=masks, taps=taps),
        grid=(rows,),
        in_specs=[
            pl.BlockSpec(memory_space=pltpu.SMEM),
            by_row(8, span),
            pl.BlockSpec((1, 8, span), lambda r: (jnp.minimum(r + 1, rows - 1), 0, 0)),
            by_row(half, width),
            by_row(16, width),
            whole(1, width),
            whole(*near.shape),
            whole(*far.shape),
        ],
        out_specs=[by_row(tiles, 2 * TILE, width), by_row(16, width), by_row(8, span)],
        out_shape=[
            jax.ShapeDtypeStruct((rows, tiles, 2 * TILE, width), BF),
            jax.ShapeDtypeStruct((rows, 16, width), F32),
            jax.ShapeDtypeStruct((rows, 8, span), F32),
        ],
        scratch_shapes=[
            pltpu.VMEM((2 * taps * VOCAB, width), BF),
            pltpu.VMEM((length + 2 * HALO, taps * VOCAB), BF),
        ],
        compiler_params=pltpu.CompilerParams(vmem_limit_bytes=56 << 20),
    )(where, mid, mid, out_grad, grad_rim, score.reshape(1, width), near, far)


def weigh_body(band_ref, lengths_ref, start_ref, score_ref, rim_ref, edge_ref, out_ref, sums_ref, spill_ref):
    rows, _, span = band_ref.shape
    length = span - 2 * TILE
    start = start_ref[0]
    lane = lax.broadcasted_iota(jnp.int32, (rows, span), 1)
    place = start + lane - TILE
    valid = ((place >= 0) & (place < lengths_ref[...])).astype(F32)
    phase3 = lax.rem(place + 3 * TILE, 3)
    phase4 = place & 3
    even = (place & 1) == 0
    inside = {
        1: {0: None},
        2: {0: None, 1: even, -1: ~even},
        3: {0: None, 1: phase3 <= 1, 2: phase3 == 0, -1: phase3 >= 1, -2: phase3 == 2},
        4: {0: None, **{d: phase4 <= 3 - d for d in (1, 2, 3)}, **{-d: phase4 >= d for d in (1, 2, 3)}},
    }

    def over_block(size, pick):
        total = pick(0)
        for d, mask in inside[size].items():
            if d != 0:
                total = total + jnp.where(mask, pick(d), 0.0)
        return total

    def shifts(v):
        return {d: roll_to(v, d) for d in range(-3, 4)}

    base = [band_ref[:, d, :] for d in range(4)]
    edges = [edge_ref[j] for j in range(4)]
    meets = {4: {2: 0}, 5: {2: 0}, 6: {1: 0, 2: 1}, 7: {1: 0, 2: 1}}
    meets.update({8: {1: 3, 0: 2}, 9: {1: 3, 0: 2}, 10: {0: 3}, 11: {0: 3}})
    spots = {spot: TILE - 8 + spot + (length if spot >= 8 else 0) for spot in meets}
    near = {spot: rim_ref[:, spot, :] for spot in meets}
    for spot, pairs in meets.items():
        here = lane == spots[spot]
        base[3] = jnp.where(here, jnp.sum(near[spot] * score_ref[...], axis=1, keepdims=True), base[3])
        for d, j in pairs.items():
            base[d] = jnp.where(here, jnp.sum(near[spot] * edges[j], axis=1, keepdims=True), base[d])
    dots = shifts(base[3] * valid)
    scores = [over_block(b, lambda d: dots[d]) * (1.0 / b) for b in range(1, SIZES + 1)]
    highest = jnp.maximum(jnp.maximum(scores[0], scores[1]), jnp.maximum(scores[2], scores[3]))
    powers = [jnp.exp(item - highest) for item in scores]
    total = powers[0] + powers[1] + powers[2] + powers[3]
    probs = [item / total for item in powers]
    log_total = jnp.log(total)
    entropy = jnp.zeros_like(total)
    for b in range(SIZES):
        entropy = entropy - probs[b] * (scores[b] - highest - log_total)
    own = (lane >= TILE) & (lane < TILE + length)
    own_valid = jnp.where(own, valid, 0.0)
    entropy = jnp.sum(jnp.where(own, entropy * valid, 0.0), axis=1, keepdims=True)
    count = jnp.sum(own_valid, axis=1, keepdims=True)
    sums_ref[...] = jnp.where(lax.broadcasted_iota(jnp.int32, (rows, TILE), 1) == 0, entropy, count)
    below, same, above = (shifts(base[d] * valid) for d in range(3))
    close = {0: same[0], 1: jnp.where(even, same[1], below[1]), 2: below[2], 3: below[3]}
    close.update({-1: jnp.where(even, above[-1], same[-1]), -2: above[-2], -3: above[-3]})
    inner = [over_block(b, lambda d: close[d]) * (valid * (0.5 / b)) for b in range(1, SIZES + 1)]
    mean = probs[0] * inner[0] + probs[1] * inner[1] + probs[2] * inner[2] + probs[3] * inner[3]
    score_in = [probs[b] * (inner[b] - mean) for b in range(SIZES)]
    pull = jnp.zeros_like(total)
    for b in range(1, SIZES + 1):
        moved = shifts(score_in[b - 1])
        pull = pull + over_block(b, lambda d: moved[d]) * (1.0 / b)
    weight = {d: jnp.zeros_like(total) for d in range(-3, 4)}
    for b in range(1, SIZES + 1):
        moved = shifts(probs[b - 1] * valid * (0.5 / b))
        for d, mask in inside[b].items():
            weight[d] = weight[d] + (moved[d] if mask is None else jnp.where(mask, moved[d], 0.0))
    below = valid * (weight[-2] + jnp.where(even, weight[-1], weight[-3]))
    above = valid * (weight[2] + jnp.where(even, weight[3], weight[1]))
    pick = lambda v, spot: jnp.sum(jnp.where(lane == spots[spot], v, 0.0), axis=1, keepdims=True) * near[spot]
    spill_ref[...] = jnp.zeros_like(spill_ref)
    spill_ref[:, 0, :] = pick(above, 6) + pick(above, 7)
    spill_ref[:, 7, :] = pick(below, 8) + pick(below, 9)
    out_ref[:, 0, :] = below
    out_ref[:, 1, :] = valid * (weight[0] + jnp.where(even, weight[1], weight[-1]))
    out_ref[:, 2, :] = above
    out_ref[:, 3, :] = valid * pull
    for d in range(4, 8):
        out_ref[:, d, :] = jnp.zeros_like(total)


def weigh(band, lengths, start, score, rim, edges):
    rows, _, span = band.shape
    vmem = pl.BlockSpec(memory_space=pltpu.VMEM)
    return pl.pallas_call(
        weigh_body,
        in_specs=[vmem, vmem, pl.BlockSpec(memory_space=pltpu.SMEM), vmem, vmem, vmem],
        out_specs=[vmem, vmem, vmem],
        out_shape=[
            jax.ShapeDtypeStruct(band.shape, F32),
            jax.ShapeDtypeStruct((rows, TILE), F32),
            jax.ShapeDtypeStruct((rows, 8, rim.shape[2]), F32),
        ],
    )(band, lengths.reshape(rows, 1), start.reshape(1), score.reshape(1, -1), rim, edges)


def apply_body(
    me_ref, mid_ref, g_ref, gh_ref, score_ref, hid_ref, spill_ref, weight_ref, sums_ref,
    out_ref, keep_ref, send_ref, extra_ref, onehot, hgrad, total, table_ref, pull_ref, staged,
):
    length = hid_ref.shape[1] * TILE
    half = length // 2
    taps = table_ref.shape[0] // VOCAB

    @pl.when(pl.program_id(0) == 0)
    def _():
        table_ref[...] = jnp.zeros_like(table_ref)
        pull_ref[...] = jnp.zeros_like(pull_ref)

    cells = lax.broadcasted_iota(jnp.int32, (VOCAB, length), 0)
    for tap in range(taps):
        hit = mid_ref[0, tap : tap + 1, TILE : TILE + length] == cells
        onehot[tap * VOCAB : (tap + 1) * VOCAB] = hit.astype(F32).astype(BF)
    total[...] = jnp.zeros_like(total)
    pulled = jnp.zeros((1, total.shape[1]), F32)
    score = score_rows(score_ref)
    for i in range(length // TILE):
        w = weight_ref[0, :, TILE * (i + 1) : TILE * (i + 2)]
        place = lax.broadcasted_iota(jnp.int32, (WIN, TILE), 0) - 8
        gap = place - (lax.broadcasted_iota(jnp.int32, (WIN, TILE), 1) >> 1)
        a = jnp.where(gap == 0, w[1:2], 0.0)
        a = jnp.where(gap == -1, w[0:1], a)
        a = jnp.where(gap == 1, w[2:3], a)
        a_high, a_low = split(a)
        q_high, q_low = split(w[3:4])
        sub = lax.broadcasted_iota(jnp.int32, (16, TILE), 0)
        q = jnp.where(sub < 2, q_high.astype(F32), jnp.where(sub == 2, q_low.astype(F32), 0.0)).astype(BF)
        g_high, g_low = grad_window(g_ref, gh_ref, i, length // TILE)
        stack = jnp.concatenate([g_high, g_low, g_high, score], axis=0)
        left = jnp.concatenate([a_high, a_high, a_low, q], axis=0)
        hg = lax.dot_general(left, stack, (((0,), (0,)), ((), ())), preferred_element_type=F32)
        hgrad[i * TILE : (i + 1) * TILE] = hg.astype(BF)
        left = jnp.concatenate([a_high, a_low, q], axis=0)
        res = jnp.dot(jnp.concatenate([left, left], axis=1), hid_ref[0, i], preferred_element_type=F32)
        total[i * TILE // 2 : i * TILE // 2 + WIN] += res[0:WIN] + res[WIN : 2 * WIN]
        pulled = pulled + res[2 * WIN : 2 * WIN + 1] + res[2 * WIN + 2 : 2 * WIN + 3]
    total[8:16] += jnp.where(lax.broadcasted_iota(jnp.int32, spill_ref.shape[1:], 0) == 0, spill_ref[0], 0.0)
    total[half : half + 8] += jnp.where(lax.broadcasted_iota(jnp.int32, spill_ref.shape[1:], 0) == 7, spill_ref[0], 0.0)
    out_ref[0] = total[8 : half + 8]
    pull_ref[0:1] += pulled
    table_ref[...] += jnp.dot(onehot[...], hgrad[...], preferred_element_type=F32)

    @pl.when(pl.program_id(0) == pl.num_programs(0) - 1)
    def _():
        row = lax.broadcasted_iota(jnp.int32, pull_ref.shape, 0)
        lane = lax.broadcasted_iota(jnp.int32, pull_ref.shape, 1)
        counts = jnp.sum(sums_ref[...], axis=0, keepdims=True)
        counts = jnp.concatenate([counts] + [jnp.zeros_like(counts)] * (pull_ref.shape[1] // TILE - 1), axis=1)
        extra = jnp.where((row == 1) & (lane < 2), counts, pull_ref[...])
        part = extra.shape[1] // 2
        block = table_ref.shape[0] // BLOCKS
        half_rows = BLOCKS // 2 * block
        for h in range(2):
            mine = extra[:, h * part : (h + 1) * part]
            extra_ref[h] = mine
            for p in range(BLOCKS):
                source = pl.multiple_of((me_ref[h] ^ p) * block, 8)
                rows = table_ref[pl.ds(source, block), h * part : (h + 1) * part]
                if p < BLOCKS // 2:
                    keep_ref[h, p * block : (p + 1) * block] = rows
                else:
                    staged[p * block - half_rows : (p + 1) * block - half_rows] = rows
            send_ref[h] = encode(staged[...], mine)


def apply_weights(me, mid, out_grad, grad_rim, score, hid, spill, weight, sums, taps):
    rows, _, span = mid.shape
    half, width = out_grad.shape[1:]
    tiles = 2 * half // TILE
    whole = lambda *shape: pl.BlockSpec(shape, lambda r: (0,) * len(shape), pipeline_mode=pl.Buffered(1))
    by_row = lambda *shape: pl.BlockSpec((1, *shape), lambda r: (r,) + (0,) * len(shape))
    return pl.pallas_call(
        apply_body,
        grid=(rows,),
        in_specs=[
            pl.BlockSpec(memory_space=pltpu.SMEM),
            by_row(8, span),
            by_row(half, width),
            by_row(16, width),
            whole(1, width),
            by_row(tiles, 2 * TILE, width),
            by_row(8, width),
            by_row(8, span),
            whole(*sums.shape),
        ],
        out_specs=[
            by_row(half, width),
            whole(2, taps * VOCAB // 2, width // 2),
            whole(2, taps * VOCAB // 2 + 16, width // 2),
            whole(2, 8, width // 2),
        ],
        out_shape=[
            jax.ShapeDtypeStruct((rows, half, width), F32),
            jax.ShapeDtypeStruct((2, taps * VOCAB // 2, width // 2), F32),
            jax.ShapeDtypeStruct((2, taps * VOCAB // 2 + 16, width // 2), jnp.int16),
            jax.ShapeDtypeStruct((2, 8, width // 2), F32),
        ],
        scratch_shapes=[
            pltpu.VMEM((taps * VOCAB, 2 * half), BF),
            pltpu.VMEM((2 * half, width), BF),
            pltpu.VMEM((half + 16, width), F32),
            pltpu.VMEM((taps * VOCAB, width), F32),
            pltpu.VMEM((8, width), F32),
            pltpu.VMEM((taps * VOCAB // 2, width // 2), F32),
        ],
        compiler_params=pltpu.CompilerParams(vmem_limit_bytes=56 << 20),
    )(me, mid, out_grad, grad_rim, score.reshape(1, width), hid, spill, weight, sums)


def shifted_rim(cells, width):
    count = lax.axis_size("seq")
    head, tail = cells[:, :width], cells[:, cells.shape[1] - width :]
    left = lax.ppermute(tail, "seq", [(i, i + 1) for i in range(count - 1)])
    right = lax.ppermute(head, "seq", [(i + 1, i) for i in range(count - 1)])
    return left, right


def marked_ids(byte_ids, lengths, start, taps):
    rows, length = byte_ids.shape
    left, right = shifted_rim(byte_ids, HALO)
    near = jnp.concatenate([left, byte_ids, right], axis=1)
    place = start - HALO + jnp.arange(length + 2 * HALO, dtype=jnp.int32)
    valid = (place[None, :] >= 0) & (place[None, :] < lengths[:, None])
    near = jnp.where(valid, near, -1)
    near = jnp.pad(near, ((0, 0), (TILE - HALO + 2, TILE - HALO + 2)), constant_values=-1)
    span = length + 2 * TILE
    lists = [near[:, k : k + span] for k in range(taps)]
    lists += [jnp.full((rows, span), -1, jnp.int32)] * (8 - taps)
    return jnp.stack(lists, axis=1)


NN = (((1,), (0,)), ((), ()))
NT = (((1,), (1,)), ((), ()))
TN = (((0,), (0,)), ((), ()))


def dot(a, b, dims):
    return lax.dot_general(a, b, dims, preferred_element_type=F32)


def dot2(a, pair, dims):
    return dot(a, pair[0], dims) + dot(a, pair[1], dims)


def dot3(left, right, dims):
    return dot(left[0], right[0], dims) + dot(left[0], right[1], dims) + dot(left[1], right[0], dims)


def bits_of(count):
    return [1 << i for i in range(count.bit_length() - 1)]


def exchange_plan(seq_size, dp_size):
    across = bits_of(seq_size)
    half = len(across) // 2
    along = [("dp", 2 * bit) for bit in reversed(bits_of(dp_size // 2))]
    orders = [across, across[half:] + across[:half]]
    return [[("dp", 1)] + [("seq", bit) for bit in order] + along for order in orders]


def block_index(plan):
    index = jnp.int32(0)
    for axis, bit in plan[: BLOCKS.bit_length() - 1]:
        index = 2 * index + ((lax.axis_index(axis) & bit) != 0).astype(jnp.int32)
    return index


def swap(cells, axis, bit):
    return lax.ppermute(cells, axis, [(i, i ^ bit) for i in range(lax.axis_size(axis))])


def pack_body(where_ref, conv_ref, embed_ref, out_ref, *, slots):
    taps, own, width = conv_ref.shape
    rows = embed_ref.shape[0]
    blocks = width // TILE
    for j in range(blocks):
        out_ref[j * rows : (j + 1) * rows] = embed_ref[:, j * TILE : (j + 1) * TILE].astype(BF)
    for i in range(2 * slots):
        group = 2 * where_ref[1] + ((where_ref[0] & 1) ^ (i // slots))
        unit = jnp.minimum(group * slots + i % slots, taps * blocks - 1)
        column = pl.multiple_of(unit % blocks * TILE, TILE)
        first = blocks * rows + i * own
        out_ref[first : first + own] = conv_ref[unit // blocks, :, pl.ds(column, TILE)].astype(BF)


def pack_weights(where, conv, embed, slots):
    vmem = pl.BlockSpec(memory_space=pltpu.VMEM)
    rows = embed.shape[0] * embed.shape[1] // TILE + 2 * slots * conv.shape[1]
    return pl.pallas_call(
        partial(pack_body, slots=slots),
        in_specs=[pl.BlockSpec(memory_space=pltpu.SMEM), vmem, vmem],
        out_specs=vmem,
        out_shape=jax.ShapeDtypeStruct((rows, TILE), BF),
    )(where, conv, embed)


def tables_body(where_ref, *refs, slots, own, rows):
    *near, far_ref, embed_ref, high_ref, low_ref, units = refs
    blocks = embed_ref.shape[1] // TILE
    first = blocks * rows
    for m, near_ref in enumerate(near):
        for other in range(2):
            source = far_ref.at[m] if other else near_ref
            place = where_ref[0] ^ (2 * m + other)
            for j in range(blocks):
                embed_ref[pl.ds(pl.multiple_of(place * rows, 16), rows), j * TILE : (j + 1) * TILE] = source[
                    j * rows : (j + 1) * rows
                ]
            for t in range(slots):
                units[t, pl.ds(pl.multiple_of(place * own, 16), own)] = source[first + t * own : first + (t + 1) * own]
    for t in range(slots):
        high, low = split(jnp.dot(embed_ref[...], units[t], preferred_element_type=F32))
        high_ref[t], low_ref[t] = high, low


def make_tables(where, near, far, slots, own, rows):
    width = 2 * len(near) * own
    vmem = pl.BlockSpec(memory_space=pltpu.VMEM)
    unit = jax.ShapeDtypeStruct((slots, VOCAB, TILE), BF)
    return pl.pallas_call(
        partial(tables_body, slots=slots, own=own, rows=rows),
        in_specs=[pl.BlockSpec(memory_space=pltpu.SMEM)] + [vmem] * (len(near) + 1),
        out_specs=[vmem] * 3,
        out_shape=[jax.ShapeDtypeStruct((VOCAB, width), BF), unit, unit],
        scratch_shapes=[pltpu.VMEM((slots, width, TILE), BF)],
    )(where, *near, far)


def gather_tables(where, embed, conv, left_root, rims):
    taps, own, width = conv.shape
    rows = embed.shape[0]
    seq, chips = lax.axis_size("seq"), lax.axis_size("dp") // 2
    slots = -(-taps * (width // TILE) // (2 * seq))
    pack = pack_weights(where, conv, embed, slots)
    near = [pack] + [swap(pack, "dp", 2 * m) for m in range(1, chips)]
    first = rows * width // TILE
    other = first + slots * own
    far = swap(jnp.stack([jnp.concatenate([item[:first], item[other:]], axis=0) for item in near]), "dp", 1)
    far, rims = lax.optimization_barrier((far, rims))
    embed_all, *parts = make_tables(where, near, far, slots, own, rows)
    ready = make_ready(where, embed_all, left_root)
    across = bits_of(seq)
    masks = []
    for h in range(2):
        found = [0]
        half = len(across) // 2
        for bit in across[half:] + across[:half] if h else across:
            parts[h] = jnp.concatenate([parts[h], swap(parts[h], "seq", bit)], axis=0)
            found = found + [mask ^ bit for mask in found]
        masks.append(found)
    units, ready = lax.optimization_barrier((jnp.stack(parts), ready))
    return embed_all, units, swap(units, "dp", 1), masks, ready, rims


def fold_body(keep_ref, extra_ref, *refs, gots, pieces, joint):
    got_refs, keep_out, extra_out, *sends = refs[:gots], refs[gots], refs[gots + 1], *refs[gots + 2 :]
    rest = keep_ref.shape[1] // pieces
    for h in range(2):
        total, extra = keep_ref[h], extra_ref[h]
        for ref in got_refs if got_refs[0].ndim == 3 else got_refs[h : h + 1]:
            cells, more = decode(ref[h] if ref.ndim == 3 else ref[...])
            total, extra = total + cells, extra + more
        keep_out[h] = total[:rest]
        extra_out[h] = extra
        for m in range(1, pieces):
            code = encode(total[m * rest : (m + 1) * rest], extra)
            if joint:
                sends[m - 1][h] = code
            else:
                sends[h][...] = code


def fold(keep, extra, got, pieces, joint):
    _, count, width = keep.shape
    rest = count // pieces
    cells = jax.ShapeDtypeStruct((2, rest + 16, width) if joint else (rest + 16, width), jnp.int16)
    sends = 0 if pieces == 1 else pieces - 1 if joint else 2
    vmem = pl.BlockSpec(memory_space=pltpu.VMEM)
    return pl.pallas_call(
        partial(fold_body, gots=len(got), pieces=pieces, joint=joint),
        in_specs=[vmem] * (2 + len(got)),
        out_specs=[vmem] * (2 + sends),
        out_shape=[jax.ShapeDtypeStruct((2, rest, width), F32), jax.ShapeDtypeStruct(extra.shape, F32)] + [cells] * sends,
    )(keep, extra, *got)


def finish_body(cells_ref, out_ref):
    count = cells_ref.shape[1]
    for h in range(2):
        rows = cells_ref[h]
        exponent = exponent_of(jnp.max(jnp.abs(rows), axis=0, keepdims=True))
        code, _ = to_code(rows, exponent)
        out_ref[h] = as_short(jnp.concatenate([code, jnp.broadcast_to(exponent, (8, rows.shape[1]))], axis=0))


def finish(cells):
    vmem = pl.BlockSpec(memory_space=pltpu.VMEM)
    return pl.pallas_call(
        finish_body,
        in_specs=[vmem],
        out_specs=vmem,
        out_shape=jax.ShapeDtypeStruct((2, cells.shape[1] + 8, cells.shape[2]), jnp.int16),
    )(cells)


def sum_over_devices(keep, send, extra, plans):
    depth = BLOCKS.bit_length() - 1
    across = len([axis for axis, _ in plans[0] if axis == "seq"])
    along = 1 << (depth - 1 - across)
    got = [swap(send, "dp", 1)]
    for step in range(1, 1 + across):
        keep, extra, *sends = fold(keep, extra, got, 2, False)
        got = [swap(sends[h], *plans[h][step]) for h in range(2)]
    keep, extra, *sends = fold(keep, extra, got, along, True)
    if along > 1:
        got = [swap(item, "dp", 2 * m) for m, item in enumerate(sends, 1)]
        keep, extra = fold(keep, extra, got, 1, True)
    for axis, bit in plans[0][depth:]:
        keep, extra = keep + swap(keep, axis, bit), extra + swap(extra, axis, bit)
    cells = finish(keep)
    if along > 1:
        cells = jnp.concatenate([cells] + [swap(cells, "dp", 2 * m) for m in range(1, along)], axis=1)
    parts = []
    for h in range(2):
        part = cells[h]
        for axis, bit in reversed(plans[h][1 : 1 + across]):
            part = jnp.concatenate([part, swap(part, axis, bit)], axis=0)
        parts.append(part)
    cells = jnp.stack(parts)
    return cells, swap(cells, "dp", 1), extra


def pick_rows(count, total, first):
    row = lax.broadcasted_iota(jnp.int32, (count, total), 0)
    return (lax.broadcasted_iota(jnp.int32, (count, total), 1) == row + first).astype(F32).astype(BF)


def order_body(me_ref, near_ref, far_ref, conv_ref, high_ref, low_ref, grad_ref, table):
    block = table.shape[0] // BLOCKS
    part = table.shape[1] // 2
    for h in range(2):
        for p in range(BLOCKS):
            source = near_ref if p < BLOCKS // 2 else far_ref
            first = p % (BLOCKS // 2) * (block + 8)
            cells = as_float(source[h, first : first + block + 8])
            rows = cells[:block] * jnp.exp2(cells[block : block + 1] - 15.0)
            table[pl.ds(pl.multiple_of((me_ref[h] ^ p) * block, 8), block), h * part : (h + 1) * part] = rows
    taps = conv_ref.shape[0]
    total = jnp.zeros(grad_ref.shape, F32)
    for k in range(taps):
        pair = split(table[k * VOCAB : (k + 1) * VOCAB])
        high_ref[k], low_ref[k] = pair
        total = total + dot2(conv_ref[k], pair, NT)
    grad_ref[...] = total


def order_table(me, near, far, conv_low):
    taps, own, width = conv_low.shape
    vmem = pl.BlockSpec(memory_space=pltpu.VMEM)
    table = jax.ShapeDtypeStruct((taps, VOCAB, width), BF)
    return pl.pallas_call(
        order_body,
        in_specs=[pl.BlockSpec(memory_space=pltpu.SMEM), vmem, vmem, vmem],
        out_specs=[vmem, vmem, vmem],
        out_shape=[table, table, jax.ShapeDtypeStruct((own, VOCAB), F32)],
        scratch_shapes=[pltpu.VMEM((taps * VOCAB, width), F32)],
        compiler_params=pltpu.CompilerParams(vmem_limit_bytes=60 << 20),
    )(me, near, far, conv_low)


def dot2_left(pair, b, dims):
    return dot(pair[0], b, dims) + dot(pair[1], b, dims)


def both(left, right, dims):
    count = left[0].shape[0]
    first = dot(jnp.concatenate(left, axis=0), right[0], dims)
    return first[:count] + first[count:] + dot(left[0], right[1], dims)


def ready_body(where_ref, embed_ref, left_root_ref, square_high, square_low, columns_ref, rooted_high, rooted_low):
    own, width = left_root_ref.shape[1:]
    embed = embed_ref[...]

    @pl.when(pl.program_id(0) == 0)
    def _():
        square_high[...], square_low[...] = split(dot(embed, embed, NT))
        columns_ref[...] = dot(pick_rows(own, width, where_ref[0] * own), embed, NT).astype(BF)

    rooted_high[0], rooted_low[0] = split(dot2_left(split(left_root_ref[0]), embed, NT))


def make_ready(where, embed_all, left_root):
    taps, own, width = left_root.shape
    by_tap = lambda *shape: pl.BlockSpec((1, *shape), lambda k: (k,) + (0,) * len(shape))
    whole = lambda *shape: pl.BlockSpec(shape, lambda k: (0,) * len(shape))
    like = lambda *shape: jax.ShapeDtypeStruct(shape, BF)
    return pl.pallas_call(
        ready_body,
        grid=(taps,),
        in_specs=[
            pl.BlockSpec(memory_space=pltpu.SMEM),
            whole(VOCAB, width),
            by_tap(own, width),
        ],
        out_specs=[whole(VOCAB, VOCAB)] * 2 + [whole(own, VOCAB)] + [by_tap(own, VOCAB)] * 2,
        out_shape=[like(VOCAB, VOCAB)] * 2
        + [like(own, VOCAB)]
        + [like(taps, own, VOCAB)] * 2,
        compiler_params=pltpu.CompilerParams(vmem_limit_bytes=60 << 20),
        cost_estimate=pl.CostEstimate(flops=1 << 30, bytes_accessed=3 << 20, transcendentals=0),
    )(where, embed_all, left_root)


def conv_body(
    where_ref, high_ref, low_ref, embed_ref, square_high, square_low, columns_ref, rooted_high, rooted_low, right_root_ref,
    weight_ref, left_ref, right_ref, grad_out, weight_out, left_out, right_out,
):
    own, width = weight_ref.shape[1:]
    table = high_ref[0], low_ref[0]
    columns = columns_ref[...]
    pick = pick_rows(own, width, where_ref[0] * own)
    high = dot(jnp.concatenate([columns, rooted_high[0], rooted_low[0]], axis=0), table[0], NN)
    low = dot(jnp.concatenate([columns, rooted_high[0]], axis=0), table[1], NN)
    grad = high[:own] + low[:own]
    inner = high[own : 2 * own] + high[2 * own :] + low[own:]
    grad_out[0] = grad
    grad = split(grad)
    high = dot(jnp.concatenate([grad[0], grad[1], pick], axis=0), table[0], NT)
    low = dot(jnp.concatenate([grad[0], pick], axis=0), table[1], NT)
    crossed = split(high[:own] + high[own : 2 * own] + low[:own])
    mine = split(high[2 * own :] + low[own:])
    step = both(split(inner), split(right_root_ref[0]), NN)
    weight_out[0] = weight_ref[0] - RATE_CONV * step
    outer = dot(jnp.concatenate(crossed, axis=0), embed_ref[...], NN)
    left_out[0] = BETA_STAT * left_ref[0] + (1.0 - BETA_STAT) * (outer[:own] + outer[own:])
    outer = both(split(both(mine, (square_high[...], square_low[...]), NN)), table, NN)
    right_out[0] = BETA_STAT * right_ref[0] + (1.0 - BETA_STAT) * outer


def renew_conv(where, high, low, embed_all, ready, right_root, conv, left, right):
    taps, own, width = conv.shape
    by_tap = lambda *shape: pl.BlockSpec((1, *shape), lambda k: (k,) + (0,) * len(shape))
    whole = lambda *shape: pl.BlockSpec(shape, lambda k: (0,) * len(shape))
    rows = by_tap(own, width)
    return pl.pallas_call(
        conv_body,
        grid=(taps,),
        in_specs=[
            pl.BlockSpec(memory_space=pltpu.SMEM),
            by_tap(VOCAB, width),
            by_tap(VOCAB, width),
            whole(VOCAB, width),
            whole(VOCAB, VOCAB),
            whole(VOCAB, VOCAB),
            whole(own, VOCAB),
            by_tap(own, VOCAB),
            by_tap(own, VOCAB),
            by_tap(width, width),
            rows,
            rows,
            rows,
        ],
        out_specs=[rows] * 4,
        out_shape=[jax.ShapeDtypeStruct(conv.shape, F32)] * 4,
        compiler_params=pltpu.CompilerParams(vmem_limit_bytes=60 << 20),
        cost_estimate=pl.CostEstimate(flops=8 << 30, bytes_accessed=32 << 20, transcendentals=0),
    )(where, high, low, embed_all, *ready, right_root, conv, left, right)


def embed_body(
    owner_ref, near_ref, far_ref, weight_ref, left_ref, right_ref, left_root_ref, right_root_ref,
    grad_out, weight_out, left_out, right_out, table,
):
    count, own, _ = near_ref.shape
    rows = weight_ref.shape[0]
    owner = owner_ref[0]
    for m in range(count):
        table[pl.ds(pl.multiple_of((owner ^ (2 * m)) * own, 8), own)] = near_ref[m]
        table[pl.ds(pl.multiple_of((owner ^ (2 * m + 1)) * own, 8), own)] = far_ref[m]
    pair = split(table[...])
    grad = dot2(pick_rows(rows, VOCAB, owner * rows), pair, NT)
    grad_out[...] = grad
    left_out[...] = BETA_STAT * left_ref[...] + (1.0 - BETA_STAT) * dot3(split(grad), pair, NN)
    right_out[...] = BETA_STAT * right_ref[...] + (1.0 - BETA_STAT) * dot3(split(near_ref[0]), pair, NT)
    step = dot3(split(dot3(split(left_root_ref[...]), pair, NT)), split(right_root_ref[...]), NN)
    weight_out[...] = weight_ref[...] - RATE_EMBED * step


def renew_embed(owner, near, far, embed, left, right, left_root, right_root):
    vmem = pl.BlockSpec(memory_space=pltpu.VMEM)
    shapes = [jax.ShapeDtypeStruct(item.shape, F32) for item in (embed, embed, left, right)]
    return pl.pallas_call(
        embed_body,
        in_specs=[pl.BlockSpec(memory_space=pltpu.SMEM)] + [vmem] * 7,
        out_specs=[vmem] * 4,
        out_shape=shapes,
        scratch_shapes=[pltpu.VMEM((embed.shape[1], VOCAB), F32)],
        compiler_params=pltpu.CompilerParams(vmem_limit_bytes=60 << 20),
    )(owner, near, far, embed, left, right, left_root, right_root)


def shards(
    byte_ids,
    lengths,
    embed,
    conv,
    score,
    out_grad,
    embed_left,
    embed_right,
    conv_left,
    conv_right,
    embed_left_root,
    embed_right_root,
    conv_left_root,
    conv_right_root,
    score_second,
):
    length = byte_ids.shape[1]
    width = embed.shape[1]
    taps = conv.shape[0]
    owner = lax.axis_index("dp")
    start = lax.axis_index("seq") * length
    conv_low = conv.astype(BF)
    where = jnp.stack([owner, lax.axis_index("seq")]).astype(jnp.int32)
    mid = marked_ids(byte_ids, lengths, start, taps)
    left, right = shifted_rim(out_grad, 1)
    zero = jnp.zeros((byte_ids.shape[0], 7, width), F32)
    grad_rim = jnp.concatenate([zero, left, right, zero], axis=1)
    edges = jnp.stack([left[:, 0], out_grad[:, 0], out_grad[:, -1], right[:, 0]])
    embed_all, near, far, masks, ready, (mid, grad_rim) = gather_tables(
        where, embed, conv, conv_left_root, (mid, grad_rim)
    )
    hidden, rim, band = lookup(where, mid, out_grad, grad_rim, score, near, far, masks, taps)
    weights, sums, spill = weigh(band, lengths, start, score, rim, edges)
    plans = exchange_plan(lax.axis_size("seq"), lax.axis_size("dp"))
    me = jnp.stack([block_index(plan) for plan in plans])
    output, keep, send, extra = apply_weights(
        me, mid, out_grad, grad_rim, score, hidden, spill, weights, sums, taps
    )
    near, far, extra = sum_over_devices(keep, send, extra, plans)
    score_grad = extra[:, 0].reshape(width)
    entropy = extra[0, 1, 0] / extra[0, 1, 1]
    high, low, columns = order_table(me, near, far, conv_low)
    near = jnp.stack([columns] + [swap(columns, "dp", 2 * m) for m in range(1, lax.axis_size("dp") // 2)])
    conv_grad, new_conv, new_conv_left, new_conv_right = renew_conv(
        where, high, low, embed_all, ready, conv_right_root, conv, conv_left, conv_right
    )
    near, conv_grad = lax.optimization_barrier((near, conv_grad))
    far = swap(near, "dp", 1)
    embed_grad, new_embed, new_embed_left, new_embed_right = renew_embed(
        where, near, far, embed, embed_left, embed_right, embed_left_root, embed_right_root
    )
    new_score_second = BETA_SECOND * score_second + (1.0 - BETA_SECOND) * score_grad * score_grad
    new_score = score - RATE_SCORE * score_grad / (jnp.sqrt(new_score_second) + EPSILON)
    return (
        output,
        entropy,
        embed_grad,
        conv_grad,
        score_grad,
        new_embed,
        new_conv,
        new_score,
        new_embed_left,
        new_embed_right,
        new_conv_left,
        new_conv_right,
        new_score_second,
    )


def solution(mesh):
    placed = (
        P("dp", "seq"),
        P("dp"),
        P("dp", None),
        P(None, "dp", None),
        P(),
        P("dp", "seq", None),
        P("dp", None),
        P("dp", None),
        P(None, "dp", None),
        P(None, "dp", None),
        P("dp", None),
        P(),
        P(None, "dp", None),
        P(),
        P(),
    )
    return jax.shard_map(
        shards,
        mesh=mesh,
        in_specs=placed,
        out_specs=(
            P("dp", "seq", None),
            P(),
            P("dp", None),
            P(None, "dp", None),
            P(),
            P("dp", None),
            P(None, "dp", None),
            P(),
            P("dp", None),
            P("dp", None),
            P(None, "dp", None),
            P(None, "dp", None),
            P(),
        ),
        check_vma=False,
    )
```

```python
from functools import partial

import jax
import jax.numpy as jnp
from jax import lax
from jax.experimental import pallas as pl
from jax.experimental.pallas import tpu as pltpu
from jax.sharding import PartitionSpec as P

VOCAB = 256
SIZES = 4
BETA_STAT = 0.9
BETA_SECOND = 0.99
RATE_EMBED = 10.0
RATE_CONV = 0.25
RATE_SCORE = 0.012
EPSILON = 1e-08
TILE = 128
HALO = 8
BLOCKS = 32
GROUP = 2
WIN = TILE // 2 + 16
BF = jnp.bfloat16
F32 = jnp.float32


def split(v):
    high = v.astype(BF)
    return high, (v - high.astype(F32)).astype(BF)


def exponent_of(v):
    return jnp.clip(jnp.floor(jnp.log2(jnp.maximum(v, 1e-30))) + 1.0, -90.0, 120.0)


def to_code(v, exponent):
    scaled = v * jnp.exp2(15.0 - exponent)
    code = jnp.clip(jnp.floor(scaled + 0.5), -32767.0, 32767.0)
    return code, scaled - code


def as_short(v):
    return v.astype(jnp.int32).astype(jnp.int16)


def as_float(v):
    return v.astype(jnp.int32).astype(F32)


def encode(rows, extra):
    exponent = exponent_of(jnp.max(jnp.abs(rows), axis=0, keepdims=True))
    code, _ = to_code(rows, exponent)
    few = extra[0:2]
    powers = exponent_of(jnp.abs(few))
    high, rest = to_code(few, powers)
    low = jnp.floor(rest * 16384.0 + 0.5)
    blank = jnp.zeros((9, rows.shape[1]), F32)
    return as_short(jnp.concatenate([code, exponent, high, low, powers, blank], axis=0))


def decode(cells):
    cells = as_float(cells)
    count = cells.shape[0] - 16
    more = cells[count:]
    extra = (more[1:3] + more[3:5] * (1.0 / 16384.0)) * jnp.exp2(more[5:7] - 15.0)
    extra = jnp.concatenate([extra, jnp.zeros((6, extra.shape[1]), F32)], axis=0)
    return cells[:count] * jnp.exp2(more[0:1] - 15.0), extra


def roll_to(v, offset):
    width = v.shape[-1]
    return v if offset == 0 else pltpu.roll(v, (-offset) % width, v.ndim - 1)


def score_rows(score_ref):
    high, low = (part.astype(F32) for part in split(score_ref[...]))
    row = lax.broadcasted_iota(jnp.int32, (16, high.shape[1]), 0)
    return jnp.where((row == 0) | (row == 2), high, jnp.where(row == 1, low, 0.0)).astype(BF)


def grad_window(g_ref, gh_ref, r, i, tiles):
    half = tiles * TILE // 2
    first, last = i * TILE // 2 - 8, (i + 1) * TILE // 2 + 8
    parts = [g_ref[r, max(first, 0) : min(last, half)]]
    if i == 0:
        parts = [gh_ref[r, 0:8]] + parts
    if i == tiles - 1:
        parts = parts + [gh_ref[r, 8:16]]
    return split(jnp.concatenate(parts, axis=0))


def lookup_body(
    where_ref, mid_ref, next_ref, g_ref, gh_ref, score_ref, near_ref, far_ref, hid_ref, rim_ref, band_ref, table_ref, onehot_ref, spread, hidden,
    *, masks, taps,
):
    length = hid_ref.shape[1] * TILE
    blocks = table_ref.shape[1] // TILE
    slots = near_ref.shape[1] // len(masks[0])

    @pl.when(pl.program_id(0) == 0)
    def _():
        for h in range(2):
            for spot in range(near_ref.shape[1]):
                for other, source in enumerate((near_ref, far_ref)):
                    group = 2 * (where_ref[1] ^ masks[h][spot // slots]) + ((where_ref[0] & 1) ^ other)
                    unit = group * slots + spot % slots

                    @pl.when(unit < taps * blocks)
                    def _():
                        row = pl.multiple_of((h * taps + unit // blocks) * VOCAB, VOCAB)
                        column = pl.multiple_of(unit % blocks * TILE, TILE)
                        table_ref[pl.ds(row, VOCAB), pl.ds(column, TILE)] = source[h, spot]

    nt = (((1,), (1,)), ((), ()))
    tiles = length // TILE
    lanes = lax.broadcasted_iota(jnp.int32, (1, VOCAB), 1).astype(F32)

    def mark(ref):
        columns = jnp.transpose(ref[0].astype(F32))
        ids = [columns[TILE : TILE + length], columns[TILE - HALO : TILE], columns[TILE + length : TILE + length + HALO]]
        ids = jnp.concatenate(ids, axis=0)
        for k in range(taps):
            onehot_ref[:, k * VOCAB : (k + 1) * VOCAB] = (ids[:, k : k + 1] == lanes).astype(F32).astype(BF)

    @pl.when(pl.program_id(0) == 0)
    def _():
        mark(mid_ref)

    onehot = onehot_ref[...]
    onehot = jnp.concatenate([onehot, onehot], axis=1)
    for m in range(spread.shape[0]):
        at = slice(m * TILE, (m + 1) * TILE)
        spread[m, 0:8] = jnp.broadcast_to(gh_ref[0, 7:8, at], (8, TILE))
        spread[m, 8 + length :] = jnp.broadcast_to(gh_ref[0, 8:9, at], (8, TILE))
        rows = g_ref[0, :, at]
        spread[m, pl.ds(8, length // 2, stride=2)] = rows
        spread[m, pl.ds(9, length // 2, stride=2)] = rows
    for n in range(0, table_ref.shape[1], 256):
        cells = jnp.dot(onehot, table_ref[:, n : n + 256], preferred_element_type=F32)
        hidden[:, n : n + 256] = cells
        h_high, h_low = split(cells[0:length])
        for i in range(tiles):
            hid_ref[0, i, 0:TILE, n : n + 256] = h_high[i * TILE : (i + 1) * TILE]
            hid_ref[0, i, TILE : 2 * TILE, n : n + 256] = h_low[i * TILE : (i + 1) * TILE]
        rim_ref[0, :, n : n + 256] = cells[length:]
    mark(next_ref)
    columns = []
    for t in range(0, length, 64):
        sums = [jnp.zeros((64, TILE), F32)] * 4
        for m in range(spread.shape[0]):
            part = hidden[t : t + 64, m * TILE : (m + 1) * TILE]
            for d in range(3):
                sums[d] = sums[d] + part * spread[m, 6 + 2 * d + t : 6 + 2 * d + t + 64]
            sums[3] = sums[3] + part * score_ref[:, m * TILE : (m + 1) * TILE]
        row = [jnp.sum(item, axis=1, keepdims=True) for item in sums]
        columns.append(jnp.concatenate(row + [jnp.zeros((64, 4), F32)], axis=1))
    band_ref[0, :, TILE : TILE + length] = jnp.transpose(jnp.concatenate(columns, axis=0))
    blank = jnp.zeros((8, TILE), F32)
    band_ref[0, :, 0:TILE] = blank
    band_ref[0, :, TILE + length :] = blank


def lookup(where, mid, out_grad, grad_rim, score, near, far, masks, taps):
    rows, _, span = mid.shape
    half, width = out_grad.shape[1:]
    length = 2 * half
    tiles = length // TILE
    whole = lambda *shape: pl.BlockSpec(shape, lambda r: (0,) * len(shape), pipeline_mode=pl.Buffered(1))
    by_row = lambda *shape: pl.BlockSpec((1, *shape), lambda r: (r,) + (0,) * len(shape))
    return pl.pallas_call(
        partial(lookup_body, masks=masks, taps=taps),
        grid=(rows,),
        in_specs=[
            pl.BlockSpec(memory_space=pltpu.SMEM),
            by_row(8, span),
            pl.BlockSpec((1, 8, span), lambda r: (jnp.minimum(r + 1, rows - 1), 0, 0)),
            by_row(half, width),
            by_row(16, width),
            whole(1, width),
            whole(*near.shape),
            whole(*far.shape),
        ],
        out_specs=[by_row(tiles, 2 * TILE, width), by_row(16, width), by_row(8, span)],
        out_shape=[
            jax.ShapeDtypeStruct((rows, tiles, 2 * TILE, width), BF),
            jax.ShapeDtypeStruct((rows, 16, width), F32),
            jax.ShapeDtypeStruct((rows, 8, span), F32),
        ],
        scratch_shapes=[
            pltpu.VMEM((2 * taps * VOCAB, width), BF),
            pltpu.VMEM((length + 2 * HALO, taps * VOCAB), BF),
            pltpu.VMEM((width // TILE, length + 16, TILE), F32),
            pltpu.VMEM((length + 2 * HALO, width), F32),
        ],
        compiler_params=pltpu.CompilerParams(vmem_limit_bytes=56 << 20),
    )(where, mid, mid, out_grad, grad_rim, score.reshape(1, width), near, far)


def weigh_body(band_ref, lengths_ref, start_ref, score_ref, rim_ref, edge_ref, out_ref, sums_ref, spill_ref):
    rows, _, span = band_ref.shape
    length = span - 2 * TILE
    start = start_ref[0]
    lane = lax.broadcasted_iota(jnp.int32, (rows, span), 1)
    place = start + lane - TILE
    valid = ((place >= 0) & (place < lengths_ref[...])).astype(F32)
    phase3 = lax.rem(place + 3 * TILE, 3)
    phase4 = place & 3
    even = (place & 1) == 0
    inside = {
        1: {0: None},
        2: {0: None, 1: even, -1: ~even},
        3: {0: None, 1: phase3 <= 1, 2: phase3 == 0, -1: phase3 >= 1, -2: phase3 == 2},
        4: {0: None, **{d: phase4 <= 3 - d for d in (1, 2, 3)}, **{-d: phase4 >= d for d in (1, 2, 3)}},
    }

    def over_block(size, pick):
        total = pick(0)
        for d, mask in inside[size].items():
            if d != 0:
                total = total + jnp.where(mask, pick(d), 0.0)
        return total

    def shifts(v):
        return {d: roll_to(v, d) for d in range(-3, 4)}

    base = [band_ref[:, d, :] for d in range(4)]
    edges = [edge_ref[j] for j in range(4)]
    meets = {4: {2: 0}, 5: {2: 0}, 6: {1: 0, 2: 1}, 7: {1: 0, 2: 1}}
    meets.update({8: {1: 3, 0: 2}, 9: {1: 3, 0: 2}, 10: {0: 3}, 11: {0: 3}})
    spots = {spot: TILE - 8 + spot + (length if spot >= 8 else 0) for spot in meets}
    near = {spot: rim_ref[:, spot, :] for spot in meets}
    for spot, pairs in meets.items():
        here = lane == spots[spot]
        base[3] = jnp.where(here, jnp.sum(near[spot] * score_ref[...], axis=1, keepdims=True), base[3])
        for d, j in pairs.items():
            base[d] = jnp.where(here, jnp.sum(near[spot] * edges[j], axis=1, keepdims=True), base[d])
    dots = shifts(base[3] * valid)
    scores = [over_block(b, lambda d: dots[d]) * (1.0 / b) for b in range(1, SIZES + 1)]
    highest = jnp.maximum(jnp.maximum(scores[0], scores[1]), jnp.maximum(scores[2], scores[3]))
    powers = [jnp.exp(item - highest) for item in scores]
    total = powers[0] + powers[1] + powers[2] + powers[3]
    probs = [item / total for item in powers]
    log_total = jnp.log(total)
    entropy = jnp.zeros_like(total)
    for b in range(SIZES):
        entropy = entropy - probs[b] * (scores[b] - highest - log_total)
    own = (lane >= TILE) & (lane < TILE + length)
    own_valid = jnp.where(own, valid, 0.0)
    entropy = jnp.sum(jnp.where(own, entropy * valid, 0.0), axis=1, keepdims=True)
    count = jnp.sum(own_valid, axis=1, keepdims=True)
    sums_ref[...] = jnp.where(lax.broadcasted_iota(jnp.int32, (rows, TILE), 1) == 0, entropy, count)
    below, same, above = (shifts(base[d] * valid) for d in range(3))
    close = {0: same[0], 1: jnp.where(even, same[1], below[1]), 2: below[2], 3: below[3]}
    close.update({-1: jnp.where(even, above[-1], same[-1]), -2: above[-2], -3: above[-3]})
    inner = [over_block(b, lambda d: close[d]) * (valid * (0.5 / b)) for b in range(1, SIZES + 1)]
    mean = probs[0] * inner[0] + probs[1] * inner[1] + probs[2] * inner[2] + probs[3] * inner[3]
    score_in = [probs[b] * (inner[b] - mean) for b in range(SIZES)]
    pull = jnp.zeros_like(total)
    for b in range(1, SIZES + 1):
        moved = shifts(score_in[b - 1])
        pull = pull + over_block(b, lambda d: moved[d]) * (1.0 / b)
    weight = {d: jnp.zeros_like(total) for d in range(-3, 4)}
    for b in range(1, SIZES + 1):
        moved = shifts(probs[b - 1] * valid * (0.5 / b))
        for d, mask in inside[b].items():
            weight[d] = weight[d] + (moved[d] if mask is None else jnp.where(mask, moved[d], 0.0))
    below = valid * (weight[-2] + jnp.where(even, weight[-1], weight[-3]))
    above = valid * (weight[2] + jnp.where(even, weight[3], weight[1]))
    pick = lambda v, spot: jnp.sum(jnp.where(lane == spots[spot], v, 0.0), axis=1, keepdims=True) * near[spot]
    spill_ref[...] = jnp.zeros_like(spill_ref)
    spill_ref[:, 0, :] = pick(above, 6) + pick(above, 7)
    spill_ref[:, 7, :] = pick(below, 8) + pick(below, 9)
    out_ref[:, 0, :] = below
    out_ref[:, 1, :] = valid * (weight[0] + jnp.where(even, weight[1], weight[-1]))
    out_ref[:, 2, :] = above
    out_ref[:, 3, :] = valid * pull
    for d in range(4, 8):
        out_ref[:, d, :] = jnp.zeros_like(total)


def weigh(band, lengths, start, score, rim, edges):
    rows, _, span = band.shape
    vmem = pl.BlockSpec(memory_space=pltpu.VMEM)
    return pl.pallas_call(
        weigh_body,
        in_specs=[vmem, vmem, pl.BlockSpec(memory_space=pltpu.SMEM), vmem, vmem, vmem],
        out_specs=[vmem, vmem, vmem],
        out_shape=[
            jax.ShapeDtypeStruct(band.shape, F32),
            jax.ShapeDtypeStruct((rows, TILE), F32),
            jax.ShapeDtypeStruct((rows, 8, rim.shape[2]), F32),
        ],
    )(band, lengths.reshape(rows, 1), start.reshape(1), score.reshape(1, -1), rim, edges)


def apply_body(
    me_ref, mid_ref, g_ref, gh_ref, score_ref, hid_ref, spill_ref, weight_ref, sums_ref,
    out_ref, keep_ref, send_ref, extra_ref, onehot, hgrad, total, table_ref, pull_ref, staged,
):
    length = hid_ref.shape[1] * TILE
    half = length // 2
    taps = table_ref.shape[0] // VOCAB

    @pl.when(pl.program_id(0) == 0)
    def _():
        table_ref[...] = jnp.zeros_like(table_ref)
        pull_ref[...] = jnp.zeros_like(pull_ref)

    score = score_rows(score_ref)
    for r in range(mid_ref.shape[0]):
        cells = lax.broadcasted_iota(jnp.int32, (VOCAB, length), 0)
        for tap in range(taps):
            hit = mid_ref[r, tap : tap + 1, TILE : TILE + length] == cells
            onehot[tap * VOCAB : (tap + 1) * VOCAB, r * length : (r + 1) * length] = hit.astype(F32).astype(BF)
        total[...] = jnp.zeros_like(total)
        pulled = jnp.zeros((1, total.shape[1]), F32)
        for i in range(length // TILE):
            w = weight_ref[r, :, TILE * (i + 1) : TILE * (i + 2)]
            place = lax.broadcasted_iota(jnp.int32, (WIN, TILE), 0) - 8
            gap = place - (lax.broadcasted_iota(jnp.int32, (WIN, TILE), 1) >> 1)
            a = jnp.where(gap == 0, w[1:2], 0.0)
            a = jnp.where(gap == -1, w[0:1], a)
            a = jnp.where(gap == 1, w[2:3], a)
            a_high, a_low = split(a)
            q_high, q_low = split(w[3:4])
            sub = lax.broadcasted_iota(jnp.int32, (16, TILE), 0)
            q = jnp.where(sub < 2, q_high.astype(F32), jnp.where(sub == 2, q_low.astype(F32), 0.0)).astype(BF)
            g_high, g_low = grad_window(g_ref, gh_ref, r, i, length // TILE)
            stack = jnp.concatenate([g_high, g_low, g_high, score], axis=0)
            left = jnp.concatenate([a_high, a_high, a_low, q], axis=0)
            hg = lax.dot_general(left, stack, (((0,), (0,)), ((), ())), preferred_element_type=F32)
            hgrad[r * length + i * TILE : r * length + (i + 1) * TILE] = hg.astype(BF)
            left = jnp.concatenate([a_high, a_low, q], axis=0)
            res = jnp.dot(jnp.concatenate([left, left], axis=1), hid_ref[r, i], preferred_element_type=F32)
            total[i * TILE // 2 : i * TILE // 2 + WIN] += res[0:WIN] + res[WIN : 2 * WIN]
            pulled = pulled + res[2 * WIN : 2 * WIN + 1] + res[2 * WIN + 2 : 2 * WIN + 3]
        total[8:16] += jnp.where(lax.broadcasted_iota(jnp.int32, spill_ref.shape[1:], 0) == 0, spill_ref[r], 0.0)
        total[half : half + 8] += jnp.where(lax.broadcasted_iota(jnp.int32, spill_ref.shape[1:], 0) == 7, spill_ref[r], 0.0)
        out_ref[r] = total[8 : half + 8]
        pull_ref[0:1] += pulled
    table_ref[...] += jnp.dot(onehot[...], hgrad[...], preferred_element_type=F32)

    @pl.when(pl.program_id(0) == pl.num_programs(0) - 1)
    def _():
        row = lax.broadcasted_iota(jnp.int32, pull_ref.shape, 0)
        lane = lax.broadcasted_iota(jnp.int32, pull_ref.shape, 1)
        counts = jnp.sum(sums_ref[...], axis=0, keepdims=True)
        counts = jnp.concatenate([counts] + [jnp.zeros_like(counts)] * (pull_ref.shape[1] // TILE - 1), axis=1)
        extra = jnp.where((row == 1) & (lane < 2), counts, pull_ref[...])
        part = extra.shape[1] // 2
        block = table_ref.shape[0] // BLOCKS
        half_rows = BLOCKS // 2 * block
        for h in range(2):
            mine = extra[:, h * part : (h + 1) * part]
            extra_ref[h] = mine
            for p in range(BLOCKS):
                source = pl.multiple_of((me_ref[h] ^ p) * block, 8)
                rows = table_ref[pl.ds(source, block), h * part : (h + 1) * part]
                if p < BLOCKS // 2:
                    keep_ref[h, p * block : (p + 1) * block] = rows
                else:
                    staged[p * block - half_rows : (p + 1) * block - half_rows] = rows
            send_ref[h] = encode(staged[...], mine)


def apply_weights(me, mid, out_grad, grad_rim, score, hid, spill, weight, sums, taps):
    rows, _, span = mid.shape
    half, width = out_grad.shape[1:]
    tiles = 2 * half // TILE
    whole = lambda *shape: pl.BlockSpec(shape, lambda r: (0,) * len(shape), pipeline_mode=pl.Buffered(1))
    by_row = lambda *shape: pl.BlockSpec((GROUP, *shape), lambda r: (r,) + (0,) * len(shape))
    return pl.pallas_call(
        apply_body,
        grid=(rows // GROUP,),
        in_specs=[
            pl.BlockSpec(memory_space=pltpu.SMEM),
            by_row(8, span),
            by_row(half, width),
            by_row(16, width),
            whole(1, width),
            by_row(tiles, 2 * TILE, width),
            by_row(8, width),
            by_row(8, span),
            whole(*sums.shape),
        ],
        out_specs=[
            by_row(half, width),
            whole(2, taps * VOCAB // 2, width // 2),
            whole(2, taps * VOCAB // 2 + 16, width // 2),
            whole(2, 8, width // 2),
        ],
        out_shape=[
            jax.ShapeDtypeStruct((rows, half, width), F32),
            jax.ShapeDtypeStruct((2, taps * VOCAB // 2, width // 2), F32),
            jax.ShapeDtypeStruct((2, taps * VOCAB // 2 + 16, width // 2), jnp.int16),
            jax.ShapeDtypeStruct((2, 8, width // 2), F32),
        ],
        scratch_shapes=[
            pltpu.VMEM((taps * VOCAB, GROUP * 2 * half), BF),
            pltpu.VMEM((GROUP * 2 * half, width), BF),
            pltpu.VMEM((half + 16, width), F32),
            pltpu.VMEM((taps * VOCAB, width), F32),
            pltpu.VMEM((8, width), F32),
            pltpu.VMEM((taps * VOCAB // 2, width // 2), F32),
        ],
        compiler_params=pltpu.CompilerParams(vmem_limit_bytes=56 << 20),
    )(me, mid, out_grad, grad_rim, score.reshape(1, width), hid, spill, weight, sums)


def shifted_rim(cells, width):
    count = lax.axis_size("seq")
    head, tail = cells[:, :width], cells[:, cells.shape[1] - width :]
    left = lax.ppermute(tail, "seq", [(i, i + 1) for i in range(count - 1)])
    right = lax.ppermute(head, "seq", [(i + 1, i) for i in range(count - 1)])
    return left, right


def marked_ids(byte_ids, lengths, start, taps):
    rows, length = byte_ids.shape
    left, right = shifted_rim(byte_ids, HALO)
    near = jnp.concatenate([left, byte_ids, right], axis=1)
    place = start - HALO + jnp.arange(length + 2 * HALO, dtype=jnp.int32)
    valid = (place[None, :] >= 0) & (place[None, :] < lengths[:, None])
    near = jnp.where(valid, near, -1)
    near = jnp.pad(near, ((0, 0), (TILE - HALO + 2, TILE - HALO + 2)), constant_values=-1)
    span = length + 2 * TILE
    lists = [near[:, k : k + span] for k in range(taps)]
    lists += [jnp.full((rows, span), -1, jnp.int32)] * (8 - taps)
    return jnp.stack(lists, axis=1)


NN = (((1,), (0,)), ((), ()))
NT = (((1,), (1,)), ((), ()))
TN = (((0,), (0,)), ((), ()))


def dot(a, b, dims):
    return lax.dot_general(a, b, dims, preferred_element_type=F32)


def dot2(a, pair, dims):
    return dot(a, pair[0], dims) + dot(a, pair[1], dims)


def dot3(left, right, dims):
    return dot(left[0], right[0], dims) + dot(left[0], right[1], dims) + dot(left[1], right[0], dims)


def bits_of(count):
    return [1 << i for i in range(count.bit_length() - 1)]


def exchange_plan(seq_size, dp_size):
    across = bits_of(seq_size)
    half = len(across) // 2
    along = [("dp", 2 * bit) for bit in reversed(bits_of(dp_size // 2))]
    orders = [across, across[half:] + across[:half]]
    return [[("dp", 1)] + [("seq", bit) for bit in order] + along for order in orders]


def block_index(plan):
    index = jnp.int32(0)
    for axis, bit in plan[: BLOCKS.bit_length() - 1]:
        index = 2 * index + ((lax.axis_index(axis) & bit) != 0).astype(jnp.int32)
    return index


def swap(cells, axis, bit):
    return lax.ppermute(cells, axis, [(i, i ^ bit) for i in range(lax.axis_size(axis))])


def pack_body(where_ref, conv_ref, embed_ref, out_ref, *, slots):
    taps, own, width = conv_ref.shape
    rows = embed_ref.shape[0]
    blocks = width // TILE
    for j in range(blocks):
        out_ref[j * rows : (j + 1) * rows] = embed_ref[:, j * TILE : (j + 1) * TILE].astype(BF)
    for i in range(2 * slots):
        group = 2 * where_ref[1] + ((where_ref[0] & 1) ^ (i // slots))
        unit = jnp.minimum(group * slots + i % slots, taps * blocks - 1)
        column = pl.multiple_of(unit % blocks * TILE, TILE)
        first = blocks * rows + i * own
        out_ref[first : first + own] = conv_ref[unit // blocks, :, pl.ds(column, TILE)].astype(BF)


def pack_weights(where, conv, embed, slots):
    vmem = pl.BlockSpec(memory_space=pltpu.VMEM)
    rows = embed.shape[0] * embed.shape[1] // TILE + 2 * slots * conv.shape[1]
    return pl.pallas_call(
        partial(pack_body, slots=slots),
        in_specs=[pl.BlockSpec(memory_space=pltpu.SMEM), vmem, vmem],
        out_specs=vmem,
        out_shape=jax.ShapeDtypeStruct((rows, TILE), BF),
    )(where, conv, embed)


def tables_body(where_ref, *refs, slots, own, rows):
    *near, far_ref, embed_ref, high_ref, low_ref, units = refs
    blocks = embed_ref.shape[1] // TILE
    first = blocks * rows
    for m, near_ref in enumerate(near):
        for other in range(2):
            source = far_ref.at[m] if other else near_ref
            place = where_ref[0] ^ (2 * m + other)
            for j in range(blocks):
                embed_ref[pl.ds(pl.multiple_of(place * rows, 16), rows), j * TILE : (j + 1) * TILE] = source[
                    j * rows : (j + 1) * rows
                ]
            for t in range(slots):
                units[t, pl.ds(pl.multiple_of(place * own, 16), own)] = source[first + t * own : first + (t + 1) * own]
    for t in range(slots):
        high, low = split(jnp.dot(embed_ref[...], units[t], preferred_element_type=F32))
        high_ref[t], low_ref[t] = high, low


def make_tables(where, near, far, slots, own, rows):
    width = 2 * len(near) * own
    vmem = pl.BlockSpec(memory_space=pltpu.VMEM)
    unit = jax.ShapeDtypeStruct((slots, VOCAB, TILE), BF)
    return pl.pallas_call(
        partial(tables_body, slots=slots, own=own, rows=rows),
        in_specs=[pl.BlockSpec(memory_space=pltpu.SMEM)] + [vmem] * (len(near) + 1),
        out_specs=[vmem] * 3,
        out_shape=[jax.ShapeDtypeStruct((VOCAB, width), BF), unit, unit],
        scratch_shapes=[pltpu.VMEM((slots, width, TILE), BF)],
    )(where, *near, far)


def gather_tables(where, embed, conv, left_root, rims):
    taps, own, width = conv.shape
    rows = embed.shape[0]
    seq, chips = lax.axis_size("seq"), lax.axis_size("dp") // 2
    slots = -(-taps * (width // TILE) // (2 * seq))
    pack = pack_weights(where, conv, embed, slots)
    near = [pack] + [swap(pack, "dp", 2 * m) for m in range(1, chips)]
    first = rows * width // TILE
    other = first + slots * own
    far = swap(jnp.stack([jnp.concatenate([item[:first], item[other:]], axis=0) for item in near]), "dp", 1)
    far, rims = lax.optimization_barrier((far, rims))
    embed_all, *parts = make_tables(where, near, far, slots, own, rows)
    ready = make_ready(where, embed_all, left_root)
    across = bits_of(seq)
    masks = []
    for h in range(2):
        found = [0]
        half = len(across) // 2
        for bit in across[half:] + across[:half] if h else across:
            parts[h] = jnp.concatenate([parts[h], swap(parts[h], "seq", bit)], axis=0)
            found = found + [mask ^ bit for mask in found]
        masks.append(found)
    units, ready = lax.optimization_barrier((jnp.stack(parts), ready))
    return embed_all, units, swap(units, "dp", 1), masks, ready, rims


def fold_body(keep_ref, extra_ref, *refs, gots, pieces, joint):
    got_refs, keep_out, extra_out, *sends = refs[:gots], refs[gots], refs[gots + 1], *refs[gots + 2 :]
    rest = keep_ref.shape[1] // pieces
    for h in range(2):
        total, extra = keep_ref[h], extra_ref[h]
        for ref in got_refs if got_refs[0].ndim == 3 else got_refs[h : h + 1]:
            cells, more = decode(ref[h] if ref.ndim == 3 else ref[...])
            total, extra = total + cells, extra + more
        keep_out[h] = total[:rest]
        extra_out[h] = extra
        for m in range(1, pieces):
            code = encode(total[m * rest : (m + 1) * rest], extra)
            if joint:
                sends[m - 1][h] = code
            else:
                sends[h][...] = code


def fold(keep, extra, got, pieces, joint):
    _, count, width = keep.shape
    rest = count // pieces
    cells = jax.ShapeDtypeStruct((2, rest + 16, width) if joint else (rest + 16, width), jnp.int16)
    sends = 0 if pieces == 1 else pieces - 1 if joint else 2
    vmem = pl.BlockSpec(memory_space=pltpu.VMEM)
    return pl.pallas_call(
        partial(fold_body, gots=len(got), pieces=pieces, joint=joint),
        in_specs=[vmem] * (2 + len(got)),
        out_specs=[vmem] * (2 + sends),
        out_shape=[jax.ShapeDtypeStruct((2, rest, width), F32), jax.ShapeDtypeStruct(extra.shape, F32)] + [cells] * sends,
    )(keep, extra, *got)


def finish_body(cells_ref, out_ref):
    count = cells_ref.shape[1]
    for h in range(2):
        rows = cells_ref[h]
        exponent = exponent_of(jnp.max(jnp.abs(rows), axis=0, keepdims=True))
        code, _ = to_code(rows, exponent)
        out_ref[h] = as_short(jnp.concatenate([code, jnp.broadcast_to(exponent, (8, rows.shape[1]))], axis=0))


def finish(cells):
    vmem = pl.BlockSpec(memory_space=pltpu.VMEM)
    return pl.pallas_call(
        finish_body,
        in_specs=[vmem],
        out_specs=vmem,
        out_shape=jax.ShapeDtypeStruct((2, cells.shape[1] + 8, cells.shape[2]), jnp.int16),
    )(cells)


def sum_over_devices(keep, send, extra, plans):
    depth = BLOCKS.bit_length() - 1
    across = len([axis for axis, _ in plans[0] if axis == "seq"])
    along = 1 << (depth - 1 - across)
    got = [swap(send, "dp", 1)]
    for step in range(1, 1 + across):
        keep, extra, *sends = fold(keep, extra, got, 2, False)
        got = [swap(sends[h], *plans[h][step]) for h in range(2)]
    keep, extra, *sends = fold(keep, extra, got, along, True)
    if along > 1:
        got = [swap(item, "dp", 2 * m) for m, item in enumerate(sends, 1)]
        keep, extra = fold(keep, extra, got, 1, True)
    for axis, bit in plans[0][depth:]:
        keep, extra = keep + swap(keep, axis, bit), extra + swap(extra, axis, bit)
    cells = finish(keep)
    if along > 1:
        cells = jnp.concatenate([cells] + [swap(cells, "dp", 2 * m) for m in range(1, along)], axis=1)
    parts = []
    for h in range(2):
        part = cells[h]
        for axis, bit in reversed(plans[h][1 : 1 + across]):
            part = jnp.concatenate([part, swap(part, axis, bit)], axis=0)
        parts.append(part)
    cells = jnp.stack(parts)
    return cells, swap(cells, "dp", 1), extra


def pick_rows(count, total, first):
    row = lax.broadcasted_iota(jnp.int32, (count, total), 0)
    return (lax.broadcasted_iota(jnp.int32, (count, total), 1) == row + first).astype(F32).astype(BF)


def order_body(
    me_ref, near_ref, far_ref, conv_ref, extra_ref, score_ref, second_ref,
    high_ref, low_ref, grad_ref, entropy_ref, score_grad_ref, score_out_ref, second_out_ref, table,
):
    sums = jnp.concatenate([extra_ref[0], extra_ref[1]], axis=1)
    entropy_ref[...] = sums[1:2, 0:1] / sums[1:2, 1:2]
    score_grad = sums[0:1]
    second = BETA_SECOND * second_ref[...] + (1.0 - BETA_SECOND) * score_grad * score_grad
    score_grad_ref[...] = score_grad
    second_out_ref[...] = second
    score_out_ref[...] = score_ref[...] - RATE_SCORE * score_grad / (jnp.sqrt(second) + EPSILON)
    block = table.shape[0] // BLOCKS
    part = table.shape[1] // 2
    for h in range(2):
        for p in range(BLOCKS):
            source = near_ref if p < BLOCKS // 2 else far_ref
            first = p % (BLOCKS // 2) * (block + 8)
            cells = as_float(source[h, first : first + block + 8])
            rows = cells[:block] * jnp.exp2(cells[block : block + 1] - 15.0)
            table[pl.ds(pl.multiple_of((me_ref[h] ^ p) * block, 8), block), h * part : (h + 1) * part] = rows
    taps = conv_ref.shape[0]
    total = jnp.zeros(grad_ref.shape, F32)
    for k in range(taps):
        pair = split(table[k * VOCAB : (k + 1) * VOCAB])
        high_ref[k], low_ref[k] = pair
        total = total + dot2(conv_ref[k].astype(BF), pair, NT)
    grad_ref[...] = total


def order_table(me, near, far, conv, extra, score, second):
    taps, own, width = conv.shape
    vmem = pl.BlockSpec(memory_space=pltpu.VMEM)
    table = jax.ShapeDtypeStruct((taps, VOCAB, width), BF)
    row = jax.ShapeDtypeStruct((1, width), F32)
    return pl.pallas_call(
        order_body,
        in_specs=[pl.BlockSpec(memory_space=pltpu.SMEM)] + [vmem] * 6,
        out_specs=[vmem] * 7,
        out_shape=[
            table,
            table,
            jax.ShapeDtypeStruct((own, VOCAB), F32),
            jax.ShapeDtypeStruct((1, 1), F32),
            row,
            row,
            row,
        ],
        scratch_shapes=[pltpu.VMEM((taps * VOCAB, width), F32)],
        compiler_params=pltpu.CompilerParams(vmem_limit_bytes=60 << 20),
    )(me, near, far, conv, extra, score.reshape(1, width), second.reshape(1, width))


def dot2_left(pair, b, dims):
    return dot(pair[0], b, dims) + dot(pair[1], b, dims)


def both(left, right, dims):
    count = left[0].shape[0]
    first = dot(jnp.concatenate(left, axis=0), right[0], dims)
    return first[:count] + first[count:] + dot(left[0], right[1], dims)


def ready_body(where_ref, embed_ref, left_root_ref, square_high, square_low, columns_ref, rooted_high, rooted_low):
    own, width = left_root_ref.shape[1:]
    embed = embed_ref[...]

    @pl.when(pl.program_id(0) == 0)
    def _():
        square_high[...], square_low[...] = split(dot(embed, embed, NT))
        columns_ref[...] = dot(pick_rows(own, width, where_ref[0] * own), embed, NT).astype(BF)

    rooted_high[0], rooted_low[0] = split(dot2_left(split(left_root_ref[0]), embed, NT))


def make_ready(where, embed_all, left_root):
    taps, own, width = left_root.shape
    by_tap = lambda *shape: pl.BlockSpec((1, *shape), lambda k: (k,) + (0,) * len(shape))
    whole = lambda *shape: pl.BlockSpec(shape, lambda k: (0,) * len(shape))
    like = lambda *shape: jax.ShapeDtypeStruct(shape, BF)
    return pl.pallas_call(
        ready_body,
        grid=(taps,),
        in_specs=[
            pl.BlockSpec(memory_space=pltpu.SMEM),
            whole(VOCAB, width),
            by_tap(own, width),
        ],
        out_specs=[whole(VOCAB, VOCAB)] * 2 + [whole(own, VOCAB)] + [by_tap(own, VOCAB)] * 2,
        out_shape=[like(VOCAB, VOCAB)] * 2
        + [like(own, VOCAB)]
        + [like(taps, own, VOCAB)] * 2,
        compiler_params=pltpu.CompilerParams(vmem_limit_bytes=60 << 20),
        cost_estimate=pl.CostEstimate(flops=1 << 30, bytes_accessed=3 << 20, transcendentals=0),
    )(where, embed_all, left_root)


def conv_body(
    where_ref, high_ref, low_ref, embed_ref, square_high, square_low, columns_ref, rooted_high, rooted_low, right_root_ref,
    weight_ref, left_ref, right_ref, grad_out, weight_out, left_out, right_out,
):
    own, width = weight_ref.shape[1:]
    table = high_ref[0], low_ref[0]
    columns = columns_ref[...]
    pick = pick_rows(own, width, where_ref[0] * own)
    high = dot(jnp.concatenate([columns, rooted_high[0], rooted_low[0]], axis=0), table[0], NN)
    low = dot(jnp.concatenate([columns, rooted_high[0]], axis=0), table[1], NN)
    grad = high[:own] + low[:own]
    inner = high[own : 2 * own] + high[2 * own :] + low[own:]
    grad_out[0] = grad
    grad = split(grad)
    high = dot(jnp.concatenate([grad[0], grad[1], pick], axis=0), table[0], NT)
    low = dot(jnp.concatenate([grad[0], pick], axis=0), table[1], NT)
    crossed = split(high[:own] + high[own : 2 * own] + low[:own])
    mine = split(high[2 * own :] + low[own:])
    step = both(split(inner), split(right_root_ref[0]), NN)
    weight_out[0] = weight_ref[0] - RATE_CONV * step
    outer = dot(jnp.concatenate(crossed, axis=0), embed_ref[...], NN)
    left_out[0] = BETA_STAT * left_ref[0] + (1.0 - BETA_STAT) * (outer[:own] + outer[own:])
    outer = both(split(both(mine, (square_high[...], square_low[...]), NN)), table, NN)
    right_out[0] = BETA_STAT * right_ref[0] + (1.0 - BETA_STAT) * outer


def renew_conv(where, high, low, embed_all, ready, right_root, conv, left, right):
    taps, own, width = conv.shape
    by_tap = lambda *shape: pl.BlockSpec((1, *shape), lambda k: (k,) + (0,) * len(shape))
    whole = lambda *shape: pl.BlockSpec(shape, lambda k: (0,) * len(shape))
    rows = by_tap(own, width)
    return pl.pallas_call(
        conv_body,
        grid=(taps,),
        in_specs=[
            pl.BlockSpec(memory_space=pltpu.SMEM),
            by_tap(VOCAB, width),
            by_tap(VOCAB, width),
            whole(VOCAB, width),
            whole(VOCAB, VOCAB),
            whole(VOCAB, VOCAB),
            whole(own, VOCAB),
            by_tap(own, VOCAB),
            by_tap(own, VOCAB),
            by_tap(width, width),
            rows,
            rows,
            rows,
        ],
        out_specs=[rows] * 4,
        out_shape=[jax.ShapeDtypeStruct(conv.shape, F32)] * 4,
        compiler_params=pltpu.CompilerParams(vmem_limit_bytes=60 << 20),
        cost_estimate=pl.CostEstimate(flops=8 << 30, bytes_accessed=32 << 20, transcendentals=0),
    )(where, high, low, embed_all, *ready, right_root, conv, left, right)


def embed_body(
    owner_ref, near_ref, far_ref, weight_ref, left_ref, right_ref, left_root_ref, right_root_ref,
    grad_out, weight_out, left_out, right_out, table,
):
    count, own, _ = near_ref.shape
    rows = weight_ref.shape[0]
    owner = owner_ref[0]
    for m in range(count):
        table[pl.ds(pl.multiple_of((owner ^ (2 * m)) * own, 8), own)] = near_ref[m]
        table[pl.ds(pl.multiple_of((owner ^ (2 * m + 1)) * own, 8), own)] = far_ref[m]
    pair = split(table[...])
    grad = dot2(pick_rows(rows, VOCAB, owner * rows), pair, NT)
    grad_out[...] = grad
    left_out[...] = BETA_STAT * left_ref[...] + (1.0 - BETA_STAT) * dot3(split(grad), pair, NN)
    right_out[...] = BETA_STAT * right_ref[...] + (1.0 - BETA_STAT) * dot3(split(near_ref[0]), pair, NT)
    step = dot3(split(dot3(split(left_root_ref[...]), pair, NT)), split(right_root_ref[...]), NN)
    weight_out[...] = weight_ref[...] - RATE_EMBED * step


def renew_embed(owner, near, far, embed, left, right, left_root, right_root):
    vmem = pl.BlockSpec(memory_space=pltpu.VMEM)
    shapes = [jax.ShapeDtypeStruct(item.shape, F32) for item in (embed, embed, left, right)]
    return pl.pallas_call(
        embed_body,
        in_specs=[pl.BlockSpec(memory_space=pltpu.SMEM)] + [vmem] * 7,
        out_specs=[vmem] * 4,
        out_shape=shapes,
        scratch_shapes=[pltpu.VMEM((embed.shape[1], VOCAB), F32)],
        compiler_params=pltpu.CompilerParams(vmem_limit_bytes=60 << 20),
    )(owner, near, far, embed, left, right, left_root, right_root)


def shards(
    byte_ids,
    lengths,
    embed,
    conv,
    score,
    out_grad,
    embed_left,
    embed_right,
    conv_left,
    conv_right,
    embed_left_root,
    embed_right_root,
    conv_left_root,
    conv_right_root,
    score_second,
):
    length = byte_ids.shape[1]
    width = embed.shape[1]
    taps = conv.shape[0]
    owner = lax.axis_index("dp")
    start = lax.axis_index("seq") * length
    where = jnp.stack([owner, lax.axis_index("seq")]).astype(jnp.int32)
    mid = marked_ids(byte_ids, lengths, start, taps)
    left, right = shifted_rim(out_grad, 1)
    zero = jnp.zeros((byte_ids.shape[0], 7, width), F32)
    grad_rim = jnp.concatenate([zero, left, right, zero], axis=1)
    edges = jnp.stack([left[:, 0], out_grad[:, 0], out_grad[:, -1], right[:, 0]])
    embed_all, near, far, masks, ready, (mid, grad_rim) = gather_tables(
        where, embed, conv, conv_left_root, (mid, grad_rim)
    )
    hidden, rim, band = lookup(where, mid, out_grad, grad_rim, score, near, far, masks, taps)
    weights, sums, spill = weigh(band, lengths, start, score, rim, edges)
    plans = exchange_plan(lax.axis_size("seq"), lax.axis_size("dp"))
    me = jnp.stack([block_index(plan) for plan in plans])
    output, keep, send, extra = apply_weights(
        me, mid, out_grad, grad_rim, score, hidden, spill, weights, sums, taps
    )
    near, far, extra = sum_over_devices(keep, send, extra, plans)
    high, low, columns, entropy, score_grad, new_score, new_score_second = order_table(
        me, near, far, conv, extra, score, score_second
    )
    near = jnp.stack([columns] + [swap(columns, "dp", 2 * m) for m in range(1, lax.axis_size("dp") // 2)])
    conv_grad, new_conv, new_conv_left, new_conv_right = renew_conv(
        where, high, low, embed_all, ready, conv_right_root, conv, conv_left, conv_right
    )
    near, conv_grad = lax.optimization_barrier((near, conv_grad))
    far = swap(near, "dp", 1)
    embed_grad, new_embed, new_embed_left, new_embed_right = renew_embed(
        where, near, far, embed, embed_left, embed_right, embed_left_root, embed_right_root
    )
    return (
        output,
        entropy.reshape(()),
        embed_grad,
        conv_grad,
        score_grad.reshape(width),
        new_embed,
        new_conv,
        new_score.reshape(width),
        new_embed_left,
        new_embed_right,
        new_conv_left,
        new_conv_right,
        new_score_second.reshape(width),
    )


def solution(mesh):
    placed = (
        P("dp", "seq"),
        P("dp"),
        P("dp", None),
        P(None, "dp", None),
        P(),
        P("dp", "seq", None),
        P("dp", None),
        P("dp", None),
        P(None, "dp", None),
        P(None, "dp", None),
        P("dp", None),
        P(),
        P(None, "dp", None),
        P(),
        P(),
    )
    return jax.shard_map(
        shards,
        mesh=mesh,
        in_specs=placed,
        out_specs=(
            P("dp", "seq", None),
            P(),
            P("dp", None),
            P(None, "dp", None),
            P(),
            P("dp", None),
            P(None, "dp", None),
            P(),
            P("dp", None),
            P("dp", None),
            P(None, "dp", None),
            P(None, "dp", None),
            P(),
        ),
        check_vma=False,
    )
```

```python
from functools import partial

import jax
import jax.numpy as jnp
from jax import lax
from jax.experimental import pallas as pl
from jax.experimental.pallas import tpu as pltpu
from jax.sharding import PartitionSpec as P

VOCAB = 256
SIZES = 4
BETA_STAT = 0.9
BETA_SECOND = 0.99
RATE_EMBED = 10.0
RATE_CONV = 0.25
RATE_SCORE = 0.012
EPSILON = 1e-08
TILE = 128
HALO = 8
BLOCKS = 32
WIN = TILE // 2 + 16
BF = jnp.bfloat16
F32 = jnp.float32


def split(v):
    high = v.astype(BF)
    return high, (v - high.astype(F32)).astype(BF)


def exponent_of(v):
    return jnp.clip(jnp.ceil(jnp.log2(jnp.maximum(v, 1e-30)) * 16.0), -1440.0, 1920.0) * 0.0625


def to_code(v, exponent):
    scaled = v * jnp.exp2(15.0 - exponent)
    code = jnp.clip(jnp.floor(scaled + 0.5), -32767.0, 32767.0)
    return code, scaled - code


def as_short(v):
    return v.astype(jnp.int32).astype(jnp.int16)


def as_float(v):
    return v.astype(jnp.int32).astype(F32)


def encode(rows, extra):
    exponent = exponent_of(jnp.max(jnp.abs(rows), axis=0, keepdims=True))
    code, _ = to_code(rows, exponent)
    few = extra[0:2]
    powers = exponent_of(jnp.abs(few))
    high, rest = to_code(few, powers)
    low = jnp.floor(rest * 16384.0 + 0.5)
    blank = jnp.zeros((9, rows.shape[1]), F32)
    return as_short(jnp.concatenate([code, exponent * 16.0, high, low, powers * 16.0, blank], axis=0))


def decode(cells):
    cells = as_float(cells)
    count = cells.shape[0] - 16
    more = cells[count:]
    extra = (more[1:3] + more[3:5] * (1.0 / 16384.0)) * jnp.exp2(more[5:7] * 0.0625 - 15.0)
    extra = jnp.concatenate([extra, jnp.zeros((6, extra.shape[1]), F32)], axis=0)
    return cells[:count] * jnp.exp2(more[0:1] * 0.0625 - 15.0), extra


def roll_to(v, offset):
    width = v.shape[-1]
    return v if offset == 0 else pltpu.roll(v, (-offset) % width, v.ndim - 1)


def score_rows(score_ref):
    high, low = (part.astype(F32) for part in split(score_ref[...]))
    row = lax.broadcasted_iota(jnp.int32, (16, high.shape[1]), 0)
    return jnp.where((row == 0) | (row == 2), high, jnp.where(row == 1, low, 0.0)).astype(BF)


def grad_window(g_ref, gh_ref, r, i, tiles):
    half = tiles * TILE // 2
    first, last = i * TILE // 2 - 8, (i + 1) * TILE // 2 + 8
    parts = [g_ref[r, max(first, 0) : min(last, half)]]
    if i == 0:
        parts = [gh_ref[r, 0:8]] + parts
    if i == tiles - 1:
        parts = parts + [gh_ref[r, 8:16]]
    return split(jnp.concatenate(parts, axis=0))


def lookup_body(
    where_ref, mid_ref, next_ref, g_ref, gh_ref, score_ref, near_ref, far_ref, hid_ref, rim_ref, band_ref, table_ref, onehot_ref, spread, hidden,
    *, masks, taps,
):
    length = hid_ref.shape[1] * TILE
    blocks = table_ref.shape[1] // TILE
    slots = near_ref.shape[1] // len(masks[0])

    @pl.when(pl.program_id(0) == 0)
    def _():
        spare = 2 * taps * VOCAB
        for spot in range(near_ref.shape[1]):
            found = []
            for h in range(2):
                for other, source in enumerate((near_ref, far_ref)):
                    group = 2 * (where_ref[1] ^ masks[h][spot // slots]) + ((where_ref[0] & 1) ^ other)
                    unit = group * slots + spot % slots
                    cells = as_float(source[h, spot])
                    power = jnp.transpose(cells[TILE : TILE + 8])[:, 0:1]
                    pair = split(cells[:TILE] * jnp.exp2(power * 0.0625 - 15.0))
                    for low in range(2):
                        row = (low * taps + unit // blocks) * VOCAB + h * TILE
                        row = pl.multiple_of(jnp.where(unit < taps * blocks, row, spare), TILE)
                        found.append((row, pl.multiple_of(unit % blocks * TILE, TILE), pair[low]))
            for row, column, part in found:
                table_ref[pl.ds(row, TILE), pl.ds(column, TILE)] = part

    tiles = length // TILE
    lanes = lax.broadcasted_iota(jnp.int32, (1, VOCAB), 1).astype(F32)

    def mark(ref):
        columns = jnp.transpose(ref[0].astype(F32))
        ids = [columns[TILE : TILE + length], columns[TILE - HALO : TILE], columns[TILE + length : TILE + length + HALO]]
        ids = jnp.concatenate(ids, axis=0)
        for k in range(taps):
            onehot_ref[:, k * VOCAB : (k + 1) * VOCAB] = (ids[:, k : k + 1] == lanes).astype(F32).astype(BF)

    @pl.when(pl.program_id(0) == 0)
    def _():
        mark(mid_ref)

    onehot = onehot_ref[...]
    onehot = jnp.concatenate([onehot, onehot], axis=1)
    for m in range(spread.shape[0]):
        at = slice(m * TILE, (m + 1) * TILE)
        spread[m, 0:8] = jnp.broadcast_to(gh_ref[0, 7:8, at], (8, TILE))
        spread[m, 8 + length :] = jnp.broadcast_to(gh_ref[0, 8:9, at], (8, TILE))
        rows = g_ref[0, :, at]
        spread[m, pl.ds(8, length // 2, stride=2)] = rows
        spread[m, pl.ds(9, length // 2, stride=2)] = rows
    for n in range(0, table_ref.shape[1], 256):
        cells = jnp.dot(onehot, table_ref[0 : 2 * taps * VOCAB, n : n + 256], preferred_element_type=F32)
        hidden[:, n : n + 256] = cells
        h_high, h_low = split(cells[0:length])
        for i in range(tiles):
            hid_ref[0, i, 0:TILE, n : n + 256] = h_high[i * TILE : (i + 1) * TILE]
            hid_ref[0, i, TILE : 2 * TILE, n : n + 256] = h_low[i * TILE : (i + 1) * TILE]
        rim_ref[0, :, n : n + 256] = cells[length:]
    mark(next_ref)
    columns = []
    for t in range(0, length, 64):
        sums = [jnp.zeros((64, TILE), F32)] * 4
        for m in range(spread.shape[0]):
            part = hidden[t : t + 64, m * TILE : (m + 1) * TILE]
            for d in range(3):
                sums[d] = sums[d] + part * spread[m, 6 + 2 * d + t : 6 + 2 * d + t + 64]
            sums[3] = sums[3] + part * score_ref[:, m * TILE : (m + 1) * TILE]
        row = [jnp.sum(item, axis=1, keepdims=True) for item in sums]
        columns.append(jnp.concatenate(row + [jnp.zeros((64, 4), F32)], axis=1))
    band_ref[0, :, TILE : TILE + length] = jnp.transpose(jnp.concatenate(columns, axis=0))
    blank = jnp.zeros((8, TILE), F32)
    band_ref[0, :, 0:TILE] = blank
    band_ref[0, :, TILE + length :] = blank


def weigh_body(band_ref, lengths_ref, start_ref, score_ref, rim_ref, edge_ref, out_ref, sums_ref, spill_ref):
    rows, _, span = band_ref.shape
    length = span - 2 * TILE
    start = start_ref[0]
    lane = lax.broadcasted_iota(jnp.int32, (rows, span), 1)
    place = start + lane - TILE
    valid = ((place >= 0) & (place < lengths_ref[...])).astype(F32)
    phase3 = lax.rem(place + 3 * TILE, 3)
    phase4 = place & 3
    even = (place & 1) == 0
    inside = {
        1: {0: None},
        2: {0: None, 1: even, -1: ~even},
        3: {0: None, 1: phase3 <= 1, 2: phase3 == 0, -1: phase3 >= 1, -2: phase3 == 2},
        4: {0: None, **{d: phase4 <= 3 - d for d in (1, 2, 3)}, **{-d: phase4 >= d for d in (1, 2, 3)}},
    }

    def over_block(size, pick):
        total = pick(0)
        for d, mask in inside[size].items():
            if d != 0:
                total = total + jnp.where(mask, pick(d), 0.0)
        return total

    def shifts(v):
        return {d: roll_to(v, d) for d in range(-3, 4)}

    base = [band_ref[:, d, :] for d in range(4)]
    edges = [edge_ref[j] for j in range(4)]
    meets = {4: {2: 0}, 5: {2: 0}, 6: {1: 0, 2: 1}, 7: {1: 0, 2: 1}}
    meets.update({8: {1: 3, 0: 2}, 9: {1: 3, 0: 2}, 10: {0: 3}, 11: {0: 3}})
    spots = {spot: TILE - 8 + spot + (length if spot >= 8 else 0) for spot in meets}
    near = {spot: rim_ref[:, spot, :] for spot in meets}
    for spot, pairs in meets.items():
        here = lane == spots[spot]
        base[3] = jnp.where(here, jnp.sum(near[spot] * score_ref[...], axis=1, keepdims=True), base[3])
        for d, j in pairs.items():
            base[d] = jnp.where(here, jnp.sum(near[spot] * edges[j], axis=1, keepdims=True), base[d])
    dots = shifts(base[3] * valid)
    scores = [over_block(b, lambda d: dots[d]) * (1.0 / b) for b in range(1, SIZES + 1)]
    highest = jnp.maximum(jnp.maximum(scores[0], scores[1]), jnp.maximum(scores[2], scores[3]))
    powers = [jnp.exp(item - highest) for item in scores]
    total = powers[0] + powers[1] + powers[2] + powers[3]
    probs = [item / total for item in powers]
    log_total = jnp.log(total)
    entropy = jnp.zeros_like(total)
    for b in range(SIZES):
        entropy = entropy - probs[b] * (scores[b] - highest - log_total)
    own = (lane >= TILE) & (lane < TILE + length)
    own_valid = jnp.where(own, valid, 0.0)
    entropy = jnp.sum(jnp.where(own, entropy * valid, 0.0), axis=1, keepdims=True)
    count = jnp.sum(own_valid, axis=1, keepdims=True)
    sums_ref[...] = jnp.where(lax.broadcasted_iota(jnp.int32, (rows, TILE), 1) == 0, entropy, count)
    below, same, above = (shifts(base[d] * valid) for d in range(3))
    close = {0: same[0], 1: jnp.where(even, same[1], below[1]), 2: below[2], 3: below[3]}
    close.update({-1: jnp.where(even, above[-1], same[-1]), -2: above[-2], -3: above[-3]})
    inner = [over_block(b, lambda d: close[d]) * (valid * (0.5 / b)) for b in range(1, SIZES + 1)]
    mean = probs[0] * inner[0] + probs[1] * inner[1] + probs[2] * inner[2] + probs[3] * inner[3]
    score_in = [probs[b] * (inner[b] - mean) for b in range(SIZES)]
    pull = jnp.zeros_like(total)
    for b in range(1, SIZES + 1):
        moved = shifts(score_in[b - 1])
        pull = pull + over_block(b, lambda d: moved[d]) * (1.0 / b)
    weight = {d: jnp.zeros_like(total) for d in range(-3, 4)}
    for b in range(1, SIZES + 1):
        moved = shifts(probs[b - 1] * valid * (0.5 / b))
        for d, mask in inside[b].items():
            weight[d] = weight[d] + (moved[d] if mask is None else jnp.where(mask, moved[d], 0.0))
    below = valid * (weight[-2] + jnp.where(even, weight[-1], weight[-3]))
    above = valid * (weight[2] + jnp.where(even, weight[3], weight[1]))
    pick = lambda v, spot: jnp.sum(jnp.where(lane == spots[spot], v, 0.0), axis=1, keepdims=True) * near[spot]
    spill_ref[...] = jnp.zeros_like(spill_ref)
    spill_ref[:, 0, :] = pick(above, 6) + pick(above, 7)
    spill_ref[:, 7, :] = pick(below, 8) + pick(below, 9)
    out_ref[:, 0, :] = below
    out_ref[:, 1, :] = valid * (weight[0] + jnp.where(even, weight[1], weight[-1]))
    out_ref[:, 2, :] = above
    out_ref[:, 3, :] = valid * pull
    for d in range(4, 8):
        out_ref[:, d, :] = jnp.zeros_like(total)


def apply_body(
    me_ref, mid_ref, g_ref, gh_ref, score_ref, hid_ref, spill_ref, weight_ref, sums_ref,
    out_ref, keep_ref, send_ref, extra_ref, onehot, hgrad, total, table_ref, pull_ref, staged,
    *, first,
):
    length = hid_ref.shape[1] * TILE
    half = length // 2
    taps = table_ref.shape[0] // VOCAB

    @pl.when(pl.program_id(0) == first)
    def _():
        table_ref[...] = jnp.zeros_like(table_ref)
        pull_ref[...] = jnp.zeros_like(pull_ref)

    score = score_rows(score_ref)
    for r in range(mid_ref.shape[0]):
        cells = lax.broadcasted_iota(jnp.int32, (VOCAB, length), 0)
        for tap in range(taps):
            hit = mid_ref[r, tap : tap + 1, TILE : TILE + length] == cells
            onehot[tap * VOCAB : (tap + 1) * VOCAB, r * length : (r + 1) * length] = hit.astype(F32).astype(BF)
        total[...] = jnp.zeros_like(total)
        pulled = jnp.zeros((1, total.shape[1]), F32)
        for i in range(length // TILE):
            w = weight_ref[r, :, TILE * (i + 1) : TILE * (i + 2)]
            place = lax.broadcasted_iota(jnp.int32, (WIN, TILE), 0) - 8
            gap = place - (lax.broadcasted_iota(jnp.int32, (WIN, TILE), 1) >> 1)
            a = jnp.where(gap == 0, w[1:2], 0.0)
            a = jnp.where(gap == -1, w[0:1], a)
            a = jnp.where(gap == 1, w[2:3], a)
            a_high, a_low = split(a)
            q_high, q_low = split(w[3:4])
            sub = lax.broadcasted_iota(jnp.int32, (16, TILE), 0)
            q = jnp.where(sub < 2, q_high.astype(F32), jnp.where(sub == 2, q_low.astype(F32), 0.0)).astype(BF)
            g_high, g_low = grad_window(g_ref, gh_ref, r, i, length // TILE)
            stack = jnp.concatenate([g_high, g_low, g_high, score], axis=0)
            left = jnp.concatenate([a_high, a_high, a_low, q], axis=0)
            hg = lax.dot_general(left, stack, (((0,), (0,)), ((), ())), preferred_element_type=F32)
            hgrad[r * length + i * TILE : r * length + (i + 1) * TILE] = hg.astype(BF)
            left = jnp.concatenate([a_high, a_low, q], axis=0)
            res = jnp.dot(jnp.concatenate([left, left], axis=1), hid_ref[r, i], preferred_element_type=F32)
            total[i * TILE // 2 : i * TILE // 2 + WIN] += res[0:WIN] + res[WIN : 2 * WIN]
            pulled = pulled + res[2 * WIN : 2 * WIN + 1] + res[2 * WIN + 2 : 2 * WIN + 3]
        total[8:16] += jnp.where(lax.broadcasted_iota(jnp.int32, spill_ref.shape[1:], 0) == 0, spill_ref[r], 0.0)
        total[half : half + 8] += jnp.where(lax.broadcasted_iota(jnp.int32, spill_ref.shape[1:], 0) == 7, spill_ref[r], 0.0)
        out_ref[r] = total[8 : half + 8]
        pull_ref[0:1] += pulled
    table_ref[...] += jnp.dot(onehot[...], hgrad[...], preferred_element_type=F32)

    @pl.when(pl.program_id(0) == pl.num_programs(0) - 1)
    def _():
        row = lax.broadcasted_iota(jnp.int32, pull_ref.shape, 0)
        lane = lax.broadcasted_iota(jnp.int32, pull_ref.shape, 1)
        counts = jnp.sum(sums_ref[...], axis=0, keepdims=True)
        counts = jnp.concatenate([counts] + [jnp.zeros_like(counts)] * (pull_ref.shape[1] // TILE - 1), axis=1)
        extra = jnp.where((row == 1) & (lane < 2), counts, pull_ref[...])
        part = extra.shape[1] // 2
        block = table_ref.shape[0] // BLOCKS
        half_rows = BLOCKS // 2 * block
        for h in range(2):
            mine = extra[:, h * part : (h + 1) * part]
            extra_ref[h] = mine
            for p in range(BLOCKS):
                source = pl.multiple_of((me_ref[h] ^ p) * block, 8)
                rows = table_ref[pl.ds(source, block), h * part : (h + 1) * part]
                if p < BLOCKS // 2:
                    keep_ref[h, p * block : (p + 1) * block] = rows
                else:
                    staged[p * block - half_rows : (p + 1) * block - half_rows] = rows
            send_ref[h] = encode(staged[...], mine)


def mix_body(
    where_ref, me_ref, start_ref, lengths_ref, mid_ref, next_ref, g_ref, gh_ref, score_ref, near_ref, far_ref, edge_ref,
    out_ref, keep_ref, send_ref, extra_ref,
    hid, rim, band, weights, sums, spill, table, onehot, spread, hidden, turned, hgrad, total, gathered, pulled, staged,
    *, masks, taps,
):
    step = pl.program_id(0)
    rows = hid.shape[0]

    @pl.when(step < rows)
    def _():
        here = pl.ds(step, 1)
        lookup_body(
            where_ref, mid_ref, next_ref, g_ref, gh_ref, score_ref, near_ref, far_ref,
            hid.at[here], rim.at[here], band.at[here], table, onehot, spread, hidden, masks=masks, taps=taps,
        )

    @pl.when(step == rows)
    def _():
        weigh_body(band, lengths_ref, start_ref, score_ref, rim, edge_ref, weights, sums, spill)

    @pl.when(step >= rows)
    def _():
        here = pl.ds(step - rows, 1)
        apply_body(
            me_ref, mid_ref, g_ref, gh_ref, score_ref, hid.at[here], spill.at[here], weights.at[here], sums,
            out_ref, keep_ref, send_ref, extra_ref, turned, hgrad, total, gathered, pulled, staged, first=rows,
        )


def mix(where, me, start, lengths, mid, out_grad, grad_rim, score, near, far, edges, masks, taps):
    rows, _, span = mid.shape
    half, width = out_grad.shape[1:]
    length = 2 * half
    tiles = length // TILE
    whole = lambda *shape: pl.BlockSpec(shape, lambda t: (0,) * len(shape), pipeline_mode=pl.Buffered(1))
    by_row = lambda *shape: pl.BlockSpec((1, *shape), lambda t: (lax.rem(t, rows),) + (0,) * len(shape))
    smem = pl.BlockSpec(memory_space=pltpu.SMEM)
    return pl.pallas_call(
        partial(mix_body, masks=masks, taps=taps),
        grid=(2 * rows,),
        in_specs=[
            smem,
            smem,
            smem,
            whole(rows, 1),
            by_row(8, span),
            pl.BlockSpec((1, 8, span), lambda t: (jnp.minimum(t + 1, rows - 1), 0, 0)),
            by_row(half, width),
            by_row(16, width),
            whole(1, width),
            whole(*near.shape),
            whole(*far.shape),
            whole(*edges.shape),
        ],
        out_specs=[
            pl.BlockSpec((1, half, width), lambda t: (jnp.maximum(t - rows, 0), 0, 0)),
            whole(2, taps * VOCAB // 2, width // 2),
            whole(2, taps * VOCAB // 2 + 16, width // 2),
            whole(2, 8, width // 2),
        ],
        out_shape=[
            jax.ShapeDtypeStruct((rows, half, width), F32),
            jax.ShapeDtypeStruct((2, taps * VOCAB // 2, width // 2), F32),
            jax.ShapeDtypeStruct((2, taps * VOCAB // 2 + 16, width // 2), jnp.int16),
            jax.ShapeDtypeStruct((2, 8, width // 2), F32),
        ],
        scratch_shapes=[
            pltpu.VMEM((rows, tiles, 2 * TILE, width), BF),
            pltpu.VMEM((rows, 16, width), F32),
            pltpu.VMEM((rows, 8, span), F32),
            pltpu.VMEM((rows, 8, span), F32),
            pltpu.VMEM((rows, TILE), F32),
            pltpu.VMEM((rows, 8, width), F32),
            pltpu.VMEM((2 * taps * VOCAB + TILE, width), BF),
            pltpu.VMEM((length + 2 * HALO, taps * VOCAB), BF),
            pltpu.VMEM((width // TILE, length + 16, TILE), F32),
            pltpu.VMEM((length + 2 * HALO, width), F32),
            pltpu.VMEM((taps * VOCAB, length), BF),
            pltpu.VMEM((length, width), BF),
            pltpu.VMEM((half + 16, width), F32),
            pltpu.VMEM((taps * VOCAB, width), F32),
            pltpu.VMEM((8, width), F32),
            pltpu.VMEM((taps * VOCAB // 2, width // 2), F32),
        ],
        compiler_params=pltpu.CompilerParams(vmem_limit_bytes=60 << 20),
    )(
        where, me, start.reshape(1), lengths.reshape(rows, 1), mid, mid, out_grad, grad_rim, score.reshape(1, width), near, far, edges
    )


def shifted_rim(cells, width):
    count = lax.axis_size("seq")
    head, tail = cells[:, :width], cells[:, cells.shape[1] - width :]
    left = lax.ppermute(tail, "seq", [(i, i + 1) for i in range(count - 1)])
    right = lax.ppermute(head, "seq", [(i + 1, i) for i in range(count - 1)])
    return left, right


def marked_ids(byte_ids, lengths, start, taps):
    rows, length = byte_ids.shape
    left, right = shifted_rim(byte_ids, HALO)
    near = jnp.concatenate([left, byte_ids, right], axis=1)
    place = start - HALO + jnp.arange(length + 2 * HALO, dtype=jnp.int32)
    valid = (place[None, :] >= 0) & (place[None, :] < lengths[:, None])
    near = jnp.where(valid, near, -1)
    near = jnp.pad(near, ((0, 0), (TILE - HALO + 2, TILE - HALO + 2)), constant_values=-1)
    span = length + 2 * TILE
    lists = [near[:, k : k + span] for k in range(taps)]
    lists += [jnp.full((rows, span), -1, jnp.int32)] * (8 - taps)
    return jnp.stack(lists, axis=1)


NN = (((1,), (0,)), ((), ()))
NT = (((1,), (1,)), ((), ()))
TN = (((0,), (0,)), ((), ()))


def dot(a, b, dims):
    return lax.dot_general(a, b, dims, preferred_element_type=F32)


def dot2(a, pair, dims):
    return dot(a, pair[0], dims) + dot(a, pair[1], dims)


def dot3(left, right, dims):
    return dot(left[0], right[0], dims) + dot(left[0], right[1], dims) + dot(left[1], right[0], dims)


def bits_of(count):
    return [1 << i for i in range(count.bit_length() - 1)]


def exchange_plan(seq_size, dp_size):
    across = bits_of(seq_size)
    half = len(across) // 2
    along = [("dp", 2 * bit) for bit in reversed(bits_of(dp_size // 2))]
    orders = [across, across[half:] + across[:half]]
    return [[("dp", 1)] + [("seq", bit) for bit in order] + along for order in orders]


def block_index(plan):
    index = jnp.int32(0)
    for axis, bit in plan[: BLOCKS.bit_length() - 1]:
        index = 2 * index + ((lax.axis_index(axis) & bit) != 0).astype(jnp.int32)
    return index


def swap(cells, axis, bit):
    return lax.ppermute(cells, axis, [(i, i ^ bit) for i in range(lax.axis_size(axis))])


def pack_body(where_ref, conv_ref, embed_ref, out_ref, *, slots):
    taps, own, width = conv_ref.shape
    rows = embed_ref.shape[0]
    blocks = width // TILE
    for j in range(blocks):
        out_ref[j * rows : (j + 1) * rows] = embed_ref[:, j * TILE : (j + 1) * TILE].astype(BF)
    for i in range(2 * slots):
        group = 2 * where_ref[1] + ((where_ref[0] & 1) ^ (i // slots))
        unit = jnp.minimum(group * slots + i % slots, taps * blocks - 1)
        column = pl.multiple_of(unit % blocks * TILE, TILE)
        first = blocks * rows + i * own
        out_ref[first : first + own] = conv_ref[unit // blocks, :, pl.ds(column, TILE)].astype(BF)


def pack_weights(where, conv, embed, slots):
    vmem = pl.BlockSpec(memory_space=pltpu.VMEM)
    rows = embed.shape[0] * embed.shape[1] // TILE + 2 * slots * conv.shape[1]
    return pl.pallas_call(
        partial(pack_body, slots=slots),
        in_specs=[pl.BlockSpec(memory_space=pltpu.SMEM), vmem, vmem],
        out_specs=vmem,
        out_shape=jax.ShapeDtypeStruct((rows, TILE), BF),
    )(where, conv, embed)


def tables_body(where_ref, *refs, slots, own, rows):
    *near, far_ref, embed_ref, upper_ref, lower_ref, units = refs
    blocks = embed_ref.shape[1] // TILE
    first = blocks * rows
    for m, near_ref in enumerate(near):
        for other in range(2):
            source = far_ref.at[m] if other else near_ref
            place = where_ref[0] ^ (2 * m + other)
            for j in range(blocks):
                embed_ref[pl.ds(pl.multiple_of(place * rows, 16), rows), j * TILE : (j + 1) * TILE] = source[
                    j * rows : (j + 1) * rows
                ]
            for t in range(slots):
                units[t, pl.ds(pl.multiple_of(place * own, 16), own)] = source[first + t * own : first + (t + 1) * own]
    for t in range(slots):
        table = jnp.dot(embed_ref[...], units[t], preferred_element_type=F32)
        for h, target in enumerate((upper_ref, lower_ref)):
            rows = table[h * TILE : (h + 1) * TILE]
            exponent = exponent_of(jnp.max(jnp.abs(rows), axis=1, keepdims=True))
            code, _ = to_code(rows, exponent)
            turned = jnp.transpose(jnp.broadcast_to(exponent * 16.0, (TILE, TILE)))[0:16]
            target[t] = as_short(jnp.concatenate([code, turned], axis=0))


def make_tables(where, near, far, slots, own, rows):
    width = 2 * len(near) * own
    vmem = pl.BlockSpec(memory_space=pltpu.VMEM)
    unit = jax.ShapeDtypeStruct((slots, TILE + 16, TILE), jnp.int16)
    return pl.pallas_call(
        partial(tables_body, slots=slots, own=own, rows=rows),
        in_specs=[pl.BlockSpec(memory_space=pltpu.SMEM)] + [vmem] * (len(near) + 1),
        out_specs=[vmem] * 3,
        out_shape=[jax.ShapeDtypeStruct((VOCAB, width), BF), unit, unit],
        scratch_shapes=[pltpu.VMEM((slots, width, TILE), BF)],
    )(where, *near, far)


def gather_tables(where, embed, conv, left_root, rims):
    taps, own, width = conv.shape
    rows = embed.shape[0]
    seq, chips = lax.axis_size("seq"), lax.axis_size("dp") // 2
    slots = -(-taps * (width // TILE) // (2 * seq))
    pack = pack_weights(where, conv, embed, slots)
    near = [pack] + [swap(pack, "dp", 2 * m) for m in range(1, chips)]
    first = rows * width // TILE
    other = first + slots * own
    far = swap(jnp.stack([jnp.concatenate([item[:first], item[other:]], axis=0) for item in near]), "dp", 1)
    far, rims = lax.optimization_barrier((far, rims))
    embed_all, *parts = make_tables(where, near, far, slots, own, rows)
    ready = make_ready(where, embed_all, left_root)
    across = bits_of(seq)
    masks = []
    for h in range(2):
        found = [0]
        half = len(across) // 2
        for bit in across[half:] + across[:half] if h else across:
            parts[h] = jnp.concatenate([parts[h], swap(parts[h], "seq", bit)], axis=0)
            found = found + [mask ^ bit for mask in found]
        masks.append(found)
    units, ready = lax.optimization_barrier((jnp.stack(parts), ready))
    return embed_all, units, swap(units, "dp", 1), masks, ready, rims


def final_code(rows):
    exponent = exponent_of(jnp.max(jnp.abs(rows), axis=0, keepdims=True))
    code, _ = to_code(rows, exponent)
    return as_short(jnp.concatenate([code, jnp.broadcast_to(exponent * 16.0, (8, rows.shape[1]))], axis=0))


def fold_body(keep_ref, extra_ref, *refs, gots, pieces, joint, last):
    got_refs, keep_out, extra_out, *sends = refs[:gots], refs[gots], refs[gots + 1], *refs[gots + 2 :]
    rest = keep_ref.shape[1] // pieces
    for h in range(2):
        total, extra = keep_ref[h], extra_ref[h]
        for ref in got_refs if got_refs[0].ndim == 3 else got_refs[h : h + 1]:
            cells, more = decode(ref[h] if ref.ndim == 3 else ref[...])
            total, extra = total + cells, extra + more
        keep_out[h] = final_code(total) if last else total[:rest]
        extra_out[h] = extra
        for m in range(1, pieces):
            code = encode(total[m * rest : (m + 1) * rest], extra)
            if joint:
                sends[m - 1][h] = code
            else:
                sends[h][...] = code


def fold(keep, extra, got, pieces, joint, last=False):
    _, count, width = keep.shape
    rest = count // pieces
    cells = jax.ShapeDtypeStruct((2, rest + 16, width) if joint else (rest + 16, width), jnp.int16)
    sends = 0 if pieces == 1 else pieces - 1 if joint else 2
    first = jax.ShapeDtypeStruct((2, rest, width), F32)
    if last:
        first = jax.ShapeDtypeStruct((2, rest + 8, width), jnp.int16)
    vmem = pl.BlockSpec(memory_space=pltpu.VMEM)
    return pl.pallas_call(
        partial(fold_body, gots=len(got), pieces=pieces, joint=joint, last=last),
        in_specs=[vmem] * (2 + len(got)),
        out_specs=[vmem] * (2 + sends),
        out_shape=[first, jax.ShapeDtypeStruct(extra.shape, F32)] + [cells] * sends,
    )(keep, extra, *got)


def finish_body(cells_ref, out_ref):
    for h in range(2):
        out_ref[h] = final_code(cells_ref[h])


def finish(cells):
    vmem = pl.BlockSpec(memory_space=pltpu.VMEM)
    return pl.pallas_call(
        finish_body,
        in_specs=[vmem],
        out_specs=vmem,
        out_shape=jax.ShapeDtypeStruct((2, cells.shape[1] + 8, cells.shape[2]), jnp.int16),
    )(cells)


def sum_over_devices(keep, send, extra, plans):
    depth = BLOCKS.bit_length() - 1
    across = len([axis for axis, _ in plans[0] if axis == "seq"])
    along = 1 << (depth - 1 - across)
    got = [swap(send, "dp", 1)]
    for step in range(1, 1 + across):
        keep, extra, *sends = fold(keep, extra, got, 2, False)
        got = [swap(sends[h], *plans[h][step]) for h in range(2)]
    keep, extra, *sends = fold(keep, extra, got, along, True)
    if along > 1:
        got = [swap(item, "dp", 2 * m) for m, item in enumerate(sends, 1)]
        keep, extra = fold(keep, extra, got, 1, True, last=len(plans[0]) == depth)
    for axis, bit in plans[0][depth:]:
        keep, extra = keep + swap(keep, axis, bit), extra + swap(extra, axis, bit)
    cells = keep if keep.dtype == jnp.int16 else finish(keep)
    if along > 1:
        cells = jnp.concatenate([cells] + [swap(cells, "dp", 2 * m) for m in range(1, along)], axis=1)
    parts = []
    for h in range(2):
        part = cells[h]
        for axis, bit in reversed(plans[h][1 : 1 + across]):
            part = jnp.concatenate([part, swap(part, axis, bit)], axis=0)
        parts.append(part)
    cells = jnp.stack(parts)
    return cells, swap(cells, "dp", 1), extra


def pick_rows(count, total, first):
    row = lax.broadcasted_iota(jnp.int32, (count, total), 0)
    return (lax.broadcasted_iota(jnp.int32, (count, total), 1) == row + first).astype(F32).astype(BF)


def order_body(
    me_ref, near_ref, far_ref, conv_ref, extra_ref, score_ref, second_ref,
    high_ref, low_ref, grad_ref, entropy_ref, score_grad_ref, score_out_ref, second_out_ref, table,
):
    sums = jnp.concatenate([extra_ref[0], extra_ref[1]], axis=1)
    entropy_ref[...] = sums[1:2, 0:1] / sums[1:2, 1:2]
    score_grad = sums[0:1]
    second = BETA_SECOND * second_ref[...] + (1.0 - BETA_SECOND) * score_grad * score_grad
    score_grad_ref[...] = score_grad
    second_out_ref[...] = second
    score_out_ref[...] = score_ref[...] - RATE_SCORE * score_grad / (jnp.sqrt(second) + EPSILON)
    block = table.shape[0] // BLOCKS
    part = table.shape[1] // 2
    for h in range(2):
        for p in range(BLOCKS):
            source = near_ref if p < BLOCKS // 2 else far_ref
            first = p % (BLOCKS // 2) * (block + 8)
            cells = as_float(source[h, first : first + block + 8])
            rows = cells[:block] * jnp.exp2(cells[block : block + 1] * 0.0625 - 15.0)
            table[pl.ds(pl.multiple_of((me_ref[h] ^ p) * block, 8), block), h * part : (h + 1) * part] = rows
    taps = conv_ref.shape[0]
    total = jnp.zeros(grad_ref.shape, F32)
    for k in range(taps):
        pair = split(table[k * VOCAB : (k + 1) * VOCAB])
        high_ref[k], low_ref[k] = pair
        total = total + dot2(conv_ref[k].astype(BF), pair, NT)
    grad_ref[...] = total


def order_table(me, near, far, conv, extra, score, second):
    taps, own, width = conv.shape
    vmem = pl.BlockSpec(memory_space=pltpu.VMEM)
    table = jax.ShapeDtypeStruct((taps, VOCAB, width), BF)
    row = jax.ShapeDtypeStruct((1, width), F32)
    return pl.pallas_call(
        order_body,
        in_specs=[pl.BlockSpec(memory_space=pltpu.SMEM)] + [vmem] * 6,
        out_specs=[vmem] * 7,
        out_shape=[
            table,
            table,
            jax.ShapeDtypeStruct((own, VOCAB), F32),
            jax.ShapeDtypeStruct((1, 1), F32),
            row,
            row,
            row,
        ],
        scratch_shapes=[pltpu.VMEM((taps * VOCAB, width), F32)],
        compiler_params=pltpu.CompilerParams(vmem_limit_bytes=60 << 20),
    )(me, near, far, conv, extra, score.reshape(1, width), second.reshape(1, width))


def dot2_left(pair, b, dims):
    return dot(pair[0], b, dims) + dot(pair[1], b, dims)


def both(left, right, dims):
    count = left[0].shape[0]
    first = dot(jnp.concatenate(left, axis=0), right[0], dims)
    return first[:count] + first[count:] + dot(left[0], right[1], dims)


def ready_body(where_ref, embed_ref, left_root_ref, square_high, square_low, columns_ref, rooted_high, rooted_low):
    own, width = left_root_ref.shape[1:]
    embed = embed_ref[...]

    @pl.when(pl.program_id(0) == 0)
    def _():
        square_high[...], square_low[...] = split(dot(embed, embed, NT))
        columns_ref[...] = dot(pick_rows(own, width, where_ref[0] * own), embed, NT).astype(BF)

    rooted_high[0], rooted_low[0] = split(dot2_left(split(left_root_ref[0]), embed, NT))


def make_ready(where, embed_all, left_root):
    taps, own, width = left_root.shape
    by_tap = lambda *shape: pl.BlockSpec((1, *shape), lambda k: (k,) + (0,) * len(shape))
    whole = lambda *shape: pl.BlockSpec(shape, lambda k: (0,) * len(shape))
    like = lambda *shape: jax.ShapeDtypeStruct(shape, BF)
    return pl.pallas_call(
        ready_body,
        grid=(taps,),
        in_specs=[
            pl.BlockSpec(memory_space=pltpu.SMEM),
            whole(VOCAB, width),
            by_tap(own, width),
        ],
        out_specs=[whole(VOCAB, VOCAB)] * 2 + [whole(own, VOCAB)] + [by_tap(own, VOCAB)] * 2,
        out_shape=[like(VOCAB, VOCAB)] * 2
        + [like(own, VOCAB)]
        + [like(taps, own, VOCAB)] * 2,
        compiler_params=pltpu.CompilerParams(vmem_limit_bytes=60 << 20),
        cost_estimate=pl.CostEstimate(flops=1 << 30, bytes_accessed=3 << 20, transcendentals=0),
    )(where, embed_all, left_root)


def conv_body(
    where_ref, high_ref, low_ref, embed_ref, square_high, square_low, columns_ref, rooted_high, rooted_low, right_root_ref,
    weight_ref, left_ref, right_ref, grad_out, weight_out, left_out, right_out,
):
    own, width = weight_ref.shape[1:]
    table = high_ref[0], low_ref[0]
    columns = columns_ref[...]
    pick = pick_rows(own, width, where_ref[0] * own)
    high = dot(jnp.concatenate([columns, rooted_high[0], rooted_low[0]], axis=0), table[0], NN)
    low = dot(jnp.concatenate([columns, rooted_high[0]], axis=0), table[1], NN)
    grad = high[:own] + low[:own]
    inner = high[own : 2 * own] + high[2 * own :] + low[own:]
    grad_out[0] = grad
    grad = split(grad)
    high = dot(jnp.concatenate([grad[0], grad[1], pick], axis=0), table[0], NT)
    low = dot(jnp.concatenate([grad[0], pick], axis=0), table[1], NT)
    crossed = split(high[:own] + high[own : 2 * own] + low[:own])
    mine = split(high[2 * own :] + low[own:])
    step = both(split(inner), split(right_root_ref[0]), NN)
    weight_out[0] = weight_ref[0] - RATE_CONV * step
    outer = dot(jnp.concatenate(crossed, axis=0), embed_ref[...], NN)
    left_out[0] = BETA_STAT * left_ref[0] + (1.0 - BETA_STAT) * (outer[:own] + outer[own:])
    outer = both(split(both(mine, (square_high[...], square_low[...]), NN)), table, NN)
    right_out[0] = BETA_STAT * right_ref[0] + (1.0 - BETA_STAT) * outer


def renew_conv(where, high, low, embed_all, ready, right_root, conv, left, right):
    taps, own, width = conv.shape
    by_tap = lambda *shape: pl.BlockSpec((1, *shape), lambda k: (k,) + (0,) * len(shape))
    whole = lambda *shape: pl.BlockSpec(shape, lambda k: (0,) * len(shape))
    rows = by_tap(own, width)
    return pl.pallas_call(
        conv_body,
        grid=(taps,),
        in_specs=[
            pl.BlockSpec(memory_space=pltpu.SMEM),
            by_tap(VOCAB, width),
            by_tap(VOCAB, width),
            whole(VOCAB, width),
            whole(VOCAB, VOCAB),
            whole(VOCAB, VOCAB),
            whole(own, VOCAB),
            by_tap(own, VOCAB),
            by_tap(own, VOCAB),
            by_tap(width, width),
            rows,
            rows,
            rows,
        ],
        out_specs=[rows] * 4,
        out_shape=[jax.ShapeDtypeStruct(conv.shape, F32)] * 4,
        compiler_params=pltpu.CompilerParams(vmem_limit_bytes=60 << 20),
        cost_estimate=pl.CostEstimate(flops=8 << 30, bytes_accessed=32 << 20, transcendentals=0),
    )(where, high, low, embed_all, *ready, right_root, conv, left, right)


def embed_body(
    owner_ref, near_ref, far_ref, weight_ref, left_ref, right_ref, left_root_ref, right_root_ref,
    grad_out, weight_out, left_out, right_out, table,
):
    count, own, _ = near_ref.shape
    rows = weight_ref.shape[0]
    owner = owner_ref[0]
    for m in range(count):
        table[pl.ds(pl.multiple_of((owner ^ (2 * m)) * own, 8), own)] = near_ref[m]
        table[pl.ds(pl.multiple_of((owner ^ (2 * m + 1)) * own, 8), own)] = far_ref[m]
    pair = split(table[...])
    grad = dot2(pick_rows(rows, VOCAB, owner * rows), pair, NT)
    grad_out[...] = grad
    left_out[...] = BETA_STAT * left_ref[...] + (1.0 - BETA_STAT) * dot3(split(grad), pair, NN)
    right_out[...] = BETA_STAT * right_ref[...] + (1.0 - BETA_STAT) * dot3(split(near_ref[0]), pair, NT)
    step = dot3(split(dot3(split(left_root_ref[...]), pair, NT)), split(right_root_ref[...]), NN)
    weight_out[...] = weight_ref[...] - RATE_EMBED * step


def renew_embed(owner, near, far, embed, left, right, left_root, right_root):
    vmem = pl.BlockSpec(memory_space=pltpu.VMEM)
    shapes = [jax.ShapeDtypeStruct(item.shape, F32) for item in (embed, embed, left, right)]
    return pl.pallas_call(
        embed_body,
        in_specs=[pl.BlockSpec(memory_space=pltpu.SMEM)] + [vmem] * 7,
        out_specs=[vmem] * 4,
        out_shape=shapes,
        scratch_shapes=[pltpu.VMEM((embed.shape[1], VOCAB), F32)],
        compiler_params=pltpu.CompilerParams(vmem_limit_bytes=60 << 20),
    )(owner, near, far, embed, left, right, left_root, right_root)


def shards(
    byte_ids,
    lengths,
    embed,
    conv,
    score,
    out_grad,
    embed_left,
    embed_right,
    conv_left,
    conv_right,
    embed_left_root,
    embed_right_root,
    conv_left_root,
    conv_right_root,
    score_second,
):
    length = byte_ids.shape[1]
    width = embed.shape[1]
    taps = conv.shape[0]
    owner = lax.axis_index("dp")
    start = lax.axis_index("seq") * length
    where = jnp.stack([owner, lax.axis_index("seq")]).astype(jnp.int32)
    mid = marked_ids(byte_ids, lengths, start, taps)
    left, right = shifted_rim(out_grad, 1)
    zero = jnp.zeros((byte_ids.shape[0], 7, width), F32)
    grad_rim = jnp.concatenate([zero, left, right, zero], axis=1)
    edges = jnp.stack([left[:, 0], out_grad[:, 0], out_grad[:, -1], right[:, 0]])
    embed_all, near, far, masks, ready, (mid, grad_rim) = gather_tables(
        where, embed, conv, conv_left_root, (mid, grad_rim)
    )
    plans = exchange_plan(lax.axis_size("seq"), lax.axis_size("dp"))
    me = jnp.stack([block_index(plan) for plan in plans])
    output, keep, send, extra = mix(
        where, me, start, lengths, mid, out_grad, grad_rim, score, near, far, edges, masks, taps
    )
    near, far, extra = sum_over_devices(keep, send, extra, plans)
    high, low, columns, entropy, score_grad, new_score, new_score_second = order_table(
        me, near, far, conv, extra, score, score_second
    )
    near = jnp.stack([columns] + [swap(columns, "dp", 2 * m) for m in range(1, lax.axis_size("dp") // 2)])
    conv_grad, new_conv, new_conv_left, new_conv_right = renew_conv(
        where, high, low, embed_all, ready, conv_right_root, conv, conv_left, conv_right
    )
    near, conv_grad = lax.optimization_barrier((near, conv_grad))
    far = swap(near, "dp", 1)
    embed_grad, new_embed, new_embed_left, new_embed_right = renew_embed(
        where, near, far, embed, embed_left, embed_right, embed_left_root, embed_right_root
    )
    return (
        output,
        entropy.reshape(()),
        embed_grad,
        conv_grad,
        score_grad.reshape(width),
        new_embed,
        new_conv,
        new_score.reshape(width),
        new_embed_left,
        new_embed_right,
        new_conv_left,
        new_conv_right,
        new_score_second.reshape(width),
    )


def solution(mesh):
    placed = (
        P("dp", "seq"),
        P("dp"),
        P("dp", None),
        P(None, "dp", None),
        P(),
        P("dp", "seq", None),
        P("dp", None),
        P("dp", None),
        P(None, "dp", None),
        P(None, "dp", None),
        P("dp", None),
        P(),
        P(None, "dp", None),
        P(),
        P(),
    )
    return jax.shard_map(
        shards,
        mesh=mesh,
        in_specs=placed,
        out_specs=(
            P("dp", "seq", None),
            P(),
            P("dp", None),
            P(None, "dp", None),
            P(),
            P("dp", None),
            P(None, "dp", None),
            P(),
            P("dp", None),
            P("dp", None),
            P(None, "dp", None),
            P(None, "dp", None),
            P(),
        ),
        check_vma=False,
    )
```

```python
from functools import partial

import jax
import jax.numpy as jnp
from jax import lax
from jax.experimental import pallas as pl
from jax.experimental.pallas import tpu as pltpu
from jax.sharding import PartitionSpec as P

VOCAB = 256
SIZES = 4
BETA_STAT = 0.9
BETA_SECOND = 0.99
RATE_EMBED = 10.0
RATE_CONV = 0.25
RATE_SCORE = 0.012
EPSILON = 1e-08
TILE = 128
HALO = 8
BLOCKS = 32
WIN = TILE // 2 + 16
BF = jnp.bfloat16
F32 = jnp.float32
LIGHT = jnp.float8_e4m3fn


def split(v):
    high = v.astype(BF)
    return high, (v - high.astype(F32)).astype(BF)


def exponent_of(v):
    return jnp.clip(jnp.ceil(jnp.log2(jnp.maximum(v, 1e-30)) * 16.0), -1440.0, 1920.0) * 0.0625


def to_code(v, exponent):
    scaled = v * jnp.exp2(15.0 - exponent)
    code = jnp.clip(jnp.floor(scaled + 0.5), -32767.0, 32767.0)
    return code, scaled - code


def as_short(v):
    return v.astype(jnp.int32).astype(jnp.int16)


def as_float(v):
    return v.astype(jnp.int32).astype(F32)


def encode(rows, extra):
    exponent = exponent_of(jnp.max(jnp.abs(rows), axis=0, keepdims=True))
    code, _ = to_code(rows, exponent)
    few = extra[0:2]
    powers = exponent_of(jnp.abs(few))
    high, rest = to_code(few, powers)
    low = jnp.floor(rest * 16384.0 + 0.5)
    blank = jnp.zeros((9, rows.shape[1]), F32)
    return as_short(jnp.concatenate([code, exponent * 16.0, high, low, powers * 16.0, blank], axis=0))


def decode(cells):
    cells = as_float(cells)
    count = cells.shape[0] - 16
    more = cells[count:]
    extra = (more[1:3] + more[3:5] * (1.0 / 16384.0)) * jnp.exp2(more[5:7] * 0.0625 - 15.0)
    extra = jnp.concatenate([extra, jnp.zeros((6, extra.shape[1]), F32)], axis=0)
    return cells[:count] * jnp.exp2(more[0:1] * 0.0625 - 15.0), extra


def roll_to(v, offset):
    width = v.shape[-1]
    return v if offset == 0 else pltpu.roll(v, (-offset) % width, v.ndim - 1)


def score_rows(score_ref):
    high, low = (part.astype(F32) for part in split(score_ref[...]))
    row = lax.broadcasted_iota(jnp.int32, (16, high.shape[1]), 0)
    return jnp.where((row == 0) | (row == 2), high, jnp.where(row == 1, low, 0.0)).astype(BF)


def grad_window(g_ref, gh_ref, r, i, tiles):
    half = tiles * TILE // 2
    first, last = i * TILE // 2 - 8, (i + 1) * TILE // 2 + 8
    parts = [g_ref[r, max(first, 0) : min(last, half)]]
    if i == 0:
        parts = [gh_ref[r, 0:8]] + parts
    if i == tiles - 1:
        parts = parts + [gh_ref[r, 8:16]]
    return split(jnp.concatenate(parts, axis=0))


def lookup_body(
    where_ref, mid_ref, next_ref, g_ref, gh_ref, score_ref, near_ref, far_ref, hid_ref, rim_ref, band_ref, table_ref, onehot_ref, spread, hidden, few_ref, light_ref, scale_ref,
    *, masks, taps,
):
    length = hid_ref.shape[1] * TILE
    blocks = table_ref.shape[1] // TILE
    slots = near_ref.shape[1] // len(masks[0])

    @pl.when(pl.program_id(0) == 0)
    def _():
        spare = taps * VOCAB
        top = jnp.full((1, TILE), -1440.0, F32)
        for h in range(2):
            for spot in range(near_ref.shape[1]):
                for source in (near_ref, far_ref):
                    top = jnp.maximum(top, as_float(source[h, spot, TILE : TILE + 16])[0:1])
        top = jnp.ceil(jnp.max(top, axis=1, keepdims=True) * 0.0625)
        scale_ref[...] = jnp.broadcast_to(jnp.exp2(top - 16.0), scale_ref.shape)
        grow = jnp.exp2(16.0 - top)
        for spot in range(near_ref.shape[1]):
            found = []
            for h in range(2):
                for other, source in enumerate((near_ref, far_ref)):
                    group = 2 * (where_ref[1] ^ masks[h][spot // slots]) + ((where_ref[0] & 1) ^ other)
                    unit = group * slots + spot % slots
                    cells = as_float(source[h, spot])
                    power = jnp.transpose(cells[TILE : TILE + 8])[:, 0:1]
                    rows = cells[:TILE] * jnp.exp2(power * 0.0625 - 15.0)
                    high = rows.astype(BF)
                    low = ((rows - high.astype(F32)) * grow).astype(LIGHT)
                    row = unit // blocks * VOCAB + h * TILE
                    row = pl.multiple_of(jnp.where(unit < taps * blocks, row, spare), TILE)
                    found.append((row, pl.multiple_of(unit % blocks * TILE, TILE), high, low))
            for row, column, high, low in found:
                table_ref[pl.ds(row, TILE), pl.ds(column, TILE)] = high
                few_ref[pl.ds(row, TILE), pl.ds(column, TILE)] = low

    tiles = length // TILE
    lanes = lax.broadcasted_iota(jnp.int32, (1, VOCAB), 1).astype(F32)

    def mark(ref):
        columns = jnp.transpose(ref[0].astype(F32))
        ids = [columns[TILE : TILE + length], columns[TILE - HALO : TILE], columns[TILE + length : TILE + length + HALO]]
        ids = jnp.concatenate(ids, axis=0)
        for k in range(taps):
            hit = (ids[:, k : k + 1] == lanes).astype(F32)
            onehot_ref[:, k * VOCAB : (k + 1) * VOCAB] = hit.astype(BF)
            light_ref[:, k * VOCAB : (k + 1) * VOCAB] = hit.astype(LIGHT)

    @pl.when(pl.program_id(0) == 0)
    def _():
        mark(mid_ref)

    onehot, light = onehot_ref[...], light_ref[...]
    scale = scale_ref[0:1, 0:1]
    for m in range(spread.shape[0]):
        at = slice(m * TILE, (m + 1) * TILE)
        spread[m, 0:8] = jnp.broadcast_to(gh_ref[0, 7:8, at], (8, TILE))
        spread[m, 8 + length :] = jnp.broadcast_to(gh_ref[0, 8:9, at], (8, TILE))
        rows = g_ref[0, :, at]
        spread[m, pl.ds(8, length // 2, stride=2)] = rows
        spread[m, pl.ds(9, length // 2, stride=2)] = rows
    for n in range(0, table_ref.shape[1], 256):
        low = jnp.dot(light, few_ref[0 : taps * VOCAB, n : n + 256], preferred_element_type=F32)
        cells = jnp.dot(onehot, table_ref[0 : taps * VOCAB, n : n + 256], preferred_element_type=F32) + low * scale
        hidden[:, n : n + 256] = cells
        h_high, h_low = split(cells[0:length])
        for i in range(tiles):
            hid_ref[0, i, 0:TILE, n : n + 256] = h_high[i * TILE : (i + 1) * TILE]
            hid_ref[0, i, TILE : 2 * TILE, n : n + 256] = h_low[i * TILE : (i + 1) * TILE]
        rim_ref[0, :, n : n + 256] = cells[length:]
    mark(next_ref)
    columns = []
    for t in range(0, length, 64):
        sums = [jnp.zeros((64, TILE), F32)] * 4
        for m in range(spread.shape[0]):
            part = hidden[t : t + 64, m * TILE : (m + 1) * TILE]
            for d in range(3):
                sums[d] = sums[d] + part * spread[m, 6 + 2 * d + t : 6 + 2 * d + t + 64]
            sums[3] = sums[3] + part * score_ref[:, m * TILE : (m + 1) * TILE]
        row = [jnp.sum(item, axis=1, keepdims=True) for item in sums]
        columns.append(jnp.concatenate(row + [jnp.zeros((64, 4), F32)], axis=1))
    band_ref[0, :, TILE : TILE + length] = jnp.transpose(jnp.concatenate(columns, axis=0))
    blank = jnp.zeros((8, TILE), F32)
    band_ref[0, :, 0:TILE] = blank
    band_ref[0, :, TILE + length :] = blank


def weigh_body(band_ref, lengths_ref, start_ref, score_ref, rim_ref, edge_ref, out_ref, sums_ref, spill_ref):
    rows, _, span = band_ref.shape
    length = span - 2 * TILE
    start = start_ref[0]
    lane = lax.broadcasted_iota(jnp.int32, (rows, span), 1)
    place = start + lane - TILE
    valid = ((place >= 0) & (place < lengths_ref[...])).astype(F32)
    phase3 = lax.rem(place + 3 * TILE, 3)
    phase4 = place & 3
    even = (place & 1) == 0
    inside = {
        1: {0: None},
        2: {0: None, 1: even, -1: ~even},
        3: {0: None, 1: phase3 <= 1, 2: phase3 == 0, -1: phase3 >= 1, -2: phase3 == 2},
        4: {0: None, **{d: phase4 <= 3 - d for d in (1, 2, 3)}, **{-d: phase4 >= d for d in (1, 2, 3)}},
    }

    def over_block(size, pick):
        total = pick(0)
        for d, mask in inside[size].items():
            if d != 0:
                total = total + jnp.where(mask, pick(d), 0.0)
        return total

    def shifts(v):
        return {d: roll_to(v, d) for d in range(-3, 4)}

    base = [band_ref[:, d, :] for d in range(4)]
    edges = [edge_ref[j] for j in range(4)]
    meets = {4: {2: 0}, 5: {2: 0}, 6: {1: 0, 2: 1}, 7: {1: 0, 2: 1}}
    meets.update({8: {1: 3, 0: 2}, 9: {1: 3, 0: 2}, 10: {0: 3}, 11: {0: 3}})
    spots = {spot: TILE - 8 + spot + (length if spot >= 8 else 0) for spot in meets}
    near = {spot: rim_ref[:, spot, :] for spot in meets}
    for spot, pairs in meets.items():
        here = lane == spots[spot]
        base[3] = jnp.where(here, jnp.sum(near[spot] * score_ref[...], axis=1, keepdims=True), base[3])
        for d, j in pairs.items():
            base[d] = jnp.where(here, jnp.sum(near[spot] * edges[j], axis=1, keepdims=True), base[d])
    dots = shifts(base[3] * valid)
    scores = [over_block(b, lambda d: dots[d]) * (1.0 / b) for b in range(1, SIZES + 1)]
    highest = jnp.maximum(jnp.maximum(scores[0], scores[1]), jnp.maximum(scores[2], scores[3]))
    powers = [jnp.exp(item - highest) for item in scores]
    total = powers[0] + powers[1] + powers[2] + powers[3]
    probs = [item / total for item in powers]
    log_total = jnp.log(total)
    entropy = jnp.zeros_like(total)
    for b in range(SIZES):
        entropy = entropy - probs[b] * (scores[b] - highest - log_total)
    own = (lane >= TILE) & (lane < TILE + length)
    own_valid = jnp.where(own, valid, 0.0)
    entropy = jnp.sum(jnp.where(own, entropy * valid, 0.0), axis=1, keepdims=True)
    count = jnp.sum(own_valid, axis=1, keepdims=True)
    sums_ref[...] = jnp.where(lax.broadcasted_iota(jnp.int32, (rows, TILE), 1) == 0, entropy, count)
    below, same, above = (shifts(base[d] * valid) for d in range(3))
    close = {0: same[0], 1: jnp.where(even, same[1], below[1]), 2: below[2], 3: below[3]}
    close.update({-1: jnp.where(even, above[-1], same[-1]), -2: above[-2], -3: above[-3]})
    inner = [over_block(b, lambda d: close[d]) * (valid * (0.5 / b)) for b in range(1, SIZES + 1)]
    mean = probs[0] * inner[0] + probs[1] * inner[1] + probs[2] * inner[2] + probs[3] * inner[3]
    score_in = [probs[b] * (inner[b] - mean) for b in range(SIZES)]
    pull = jnp.zeros_like(total)
    for b in range(1, SIZES + 1):
        moved = shifts(score_in[b - 1])
        pull = pull + over_block(b, lambda d: moved[d]) * (1.0 / b)
    weight = {d: jnp.zeros_like(total) for d in range(-3, 4)}
    for b in range(1, SIZES + 1):
        moved = shifts(probs[b - 1] * valid * (0.5 / b))
        for d, mask in inside[b].items():
            weight[d] = weight[d] + (moved[d] if mask is None else jnp.where(mask, moved[d], 0.0))
    below = valid * (weight[-2] + jnp.where(even, weight[-1], weight[-3]))
    above = valid * (weight[2] + jnp.where(even, weight[3], weight[1]))
    pick = lambda v, spot: jnp.sum(jnp.where(lane == spots[spot], v, 0.0), axis=1, keepdims=True) * near[spot]
    spill_ref[...] = jnp.zeros_like(spill_ref)
    spill_ref[:, 0, :] = pick(above, 6) + pick(above, 7)
    spill_ref[:, 7, :] = pick(below, 8) + pick(below, 9)
    out_ref[:, 0, :] = below
    out_ref[:, 1, :] = valid * (weight[0] + jnp.where(even, weight[1], weight[-1]))
    out_ref[:, 2, :] = above
    out_ref[:, 3, :] = valid * pull
    for d in range(4, 8):
        out_ref[:, d, :] = jnp.zeros_like(total)


def apply_body(
    me_ref, mid_ref, g_ref, gh_ref, score_ref, hid_ref, spill_ref, weight_ref, sums_ref,
    out_ref, keep_ref, send_ref, extra_ref, onehot, hgrad, total, table_ref, pull_ref, staged,
    *, first,
):
    length = hid_ref.shape[1] * TILE
    half = length // 2
    taps = table_ref.shape[0] // VOCAB

    @pl.when(pl.program_id(0) == first)
    def _():
        table_ref[...] = jnp.zeros_like(table_ref)
        pull_ref[...] = jnp.zeros_like(pull_ref)

    score = score_rows(score_ref)
    for r in range(mid_ref.shape[0]):
        cells = lax.broadcasted_iota(jnp.int32, (VOCAB, length), 0)
        for tap in range(taps):
            hit = mid_ref[r, tap : tap + 1, TILE : TILE + length] == cells
            onehot[tap * VOCAB : (tap + 1) * VOCAB, r * length : (r + 1) * length] = hit.astype(F32).astype(BF)
        total[...] = jnp.zeros_like(total)
        pulled = jnp.zeros((1, total.shape[1]), F32)
        for i in range(length // TILE):
            w = weight_ref[r, :, TILE * (i + 1) : TILE * (i + 2)]
            place = lax.broadcasted_iota(jnp.int32, (WIN, TILE), 0) - 8
            gap = place - (lax.broadcasted_iota(jnp.int32, (WIN, TILE), 1) >> 1)
            a = jnp.where(gap == 0, w[1:2], 0.0)
            a = jnp.where(gap == -1, w[0:1], a)
            a = jnp.where(gap == 1, w[2:3], a)
            a_high, a_low = split(a)
            q_high, q_low = split(w[3:4])
            sub = lax.broadcasted_iota(jnp.int32, (16, TILE), 0)
            q = jnp.where(sub < 2, q_high.astype(F32), jnp.where(sub == 2, q_low.astype(F32), 0.0)).astype(BF)
            g_high, g_low = grad_window(g_ref, gh_ref, r, i, length // TILE)
            stack = jnp.concatenate([g_high, g_low, g_high, score], axis=0)
            left = jnp.concatenate([a_high, a_high, a_low, q], axis=0)
            hg = lax.dot_general(left, stack, (((0,), (0,)), ((), ())), preferred_element_type=F32)
            hgrad[r * length + i * TILE : r * length + (i + 1) * TILE] = hg.astype(BF)
            left = jnp.concatenate([a_high, a_low, q], axis=0)
            res = jnp.dot(jnp.concatenate([left, left], axis=1), hid_ref[r, i], preferred_element_type=F32)
            total[i * TILE // 2 : i * TILE // 2 + WIN] += res[0:WIN] + res[WIN : 2 * WIN]
            pulled = pulled + res[2 * WIN : 2 * WIN + 1] + res[2 * WIN + 2 : 2 * WIN + 3]
        total[8:16] += jnp.where(lax.broadcasted_iota(jnp.int32, spill_ref.shape[1:], 0) == 0, spill_ref[r], 0.0)
        total[half : half + 8] += jnp.where(lax.broadcasted_iota(jnp.int32, spill_ref.shape[1:], 0) == 7, spill_ref[r], 0.0)
        out_ref[r] = total[8 : half + 8]
        pull_ref[0:1] += pulled
    table_ref[...] += jnp.dot(onehot[...], hgrad[...], preferred_element_type=F32)

    @pl.when(pl.program_id(0) == pl.num_programs(0) - 1)
    def _():
        row = lax.broadcasted_iota(jnp.int32, pull_ref.shape, 0)
        lane = lax.broadcasted_iota(jnp.int32, pull_ref.shape, 1)
        counts = jnp.sum(sums_ref[...], axis=0, keepdims=True)
        counts = jnp.concatenate([counts] + [jnp.zeros_like(counts)] * (pull_ref.shape[1] // TILE - 1), axis=1)
        extra = jnp.where((row == 1) & (lane < 2), counts, pull_ref[...])
        part = extra.shape[1] // 2
        block = table_ref.shape[0] // BLOCKS
        half_rows = BLOCKS // 2 * block
        for h in range(2):
            mine = extra[:, h * part : (h + 1) * part]
            extra_ref[h] = mine
            for p in range(BLOCKS):
                source = pl.multiple_of((me_ref[h] ^ p) * block, 8)
                rows = table_ref[pl.ds(source, block), h * part : (h + 1) * part]
                if p < BLOCKS // 2:
                    keep_ref[h, p * block : (p + 1) * block] = rows
                else:
                    staged[p * block - half_rows : (p + 1) * block - half_rows] = rows
            send_ref[h] = encode(staged[...], mine)


def mix_body(
    where_ref, me_ref, start_ref, lengths_ref, mid_ref, next_ref, g_ref, gh_ref, score_ref, near_ref, far_ref, edge_ref,
    out_ref, keep_ref, send_ref, extra_ref,
    hid, rim, band, weights, sums, spill, table, onehot, spread, hidden, turned, hgrad, total, gathered, pulled, staged, few, light, scale,
    *, masks, taps,
):
    step = pl.program_id(0)
    rows = hid.shape[0]

    @pl.when(step < rows)
    def _():
        here = pl.ds(step, 1)
        lookup_body(
            where_ref, mid_ref, next_ref, g_ref, gh_ref, score_ref, near_ref, far_ref,
            hid.at[here], rim.at[here], band.at[here], table, onehot, spread, hidden, few, light, scale, masks=masks, taps=taps,
        )

    @pl.when(step == rows)
    def _():
        weigh_body(band, lengths_ref, start_ref, score_ref, rim, edge_ref, weights, sums, spill)

    @pl.when(step >= rows)
    def _():
        here = pl.ds(step - rows, 1)
        apply_body(
            me_ref, mid_ref, g_ref, gh_ref, score_ref, hid.at[here], spill.at[here], weights.at[here], sums,
            out_ref, keep_ref, send_ref, extra_ref, turned, hgrad, total, gathered, pulled, staged, first=rows,
        )


def mix(where, me, start, lengths, mid, out_grad, grad_rim, score, near, far, edges, masks, taps):
    rows, _, span = mid.shape
    half, width = out_grad.shape[1:]
    length = 2 * half
    tiles = length // TILE
    whole = lambda *shape: pl.BlockSpec(shape, lambda t: (0,) * len(shape), pipeline_mode=pl.Buffered(1))
    by_row = lambda *shape: pl.BlockSpec((1, *shape), lambda t: (lax.rem(t, rows),) + (0,) * len(shape))
    smem = pl.BlockSpec(memory_space=pltpu.SMEM)
    return pl.pallas_call(
        partial(mix_body, masks=masks, taps=taps),
        grid=(2 * rows,),
        in_specs=[
            smem,
            smem,
            smem,
            whole(rows, 1),
            by_row(8, span),
            pl.BlockSpec((1, 8, span), lambda t: (jnp.minimum(t + 1, rows - 1), 0, 0)),
            by_row(half, width),
            by_row(16, width),
            whole(1, width),
            whole(*near.shape),
            whole(*far.shape),
            whole(*edges.shape),
        ],
        out_specs=[
            pl.BlockSpec((1, half, width), lambda t: (jnp.maximum(t - rows, 0), 0, 0)),
            whole(2, taps * VOCAB // 2, width // 2),
            whole(2, taps * VOCAB // 2 + 16, width // 2),
            whole(2, 8, width // 2),
        ],
        out_shape=[
            jax.ShapeDtypeStruct((rows, half, width), F32),
            jax.ShapeDtypeStruct((2, taps * VOCAB // 2, width // 2), F32),
            jax.ShapeDtypeStruct((2, taps * VOCAB // 2 + 16, width // 2), jnp.int16),
            jax.ShapeDtypeStruct((2, 8, width // 2), F32),
        ],
        scratch_shapes=[
            pltpu.VMEM((rows, tiles, 2 * TILE, width), BF),
            pltpu.VMEM((rows, 16, width), F32),
            pltpu.VMEM((rows, 8, span), F32),
            pltpu.VMEM((rows, 8, span), F32),
            pltpu.VMEM((rows, TILE), F32),
            pltpu.VMEM((rows, 8, width), F32),
            pltpu.VMEM((taps * VOCAB + TILE, width), BF),
            pltpu.VMEM((length + 2 * HALO, taps * VOCAB), BF),
            pltpu.VMEM((width // TILE, length + 16, TILE), F32),
            pltpu.VMEM((length + 2 * HALO, width), F32),
            pltpu.VMEM((taps * VOCAB, length), BF),
            pltpu.VMEM((length, width), BF),
            pltpu.VMEM((half + 16, width), F32),
            pltpu.VMEM((taps * VOCAB, width), F32),
            pltpu.VMEM((8, width), F32),
            pltpu.VMEM((taps * VOCAB // 2, width // 2), F32),
            pltpu.VMEM((taps * VOCAB + TILE, width), LIGHT),
            pltpu.VMEM((length + 2 * HALO, taps * VOCAB), LIGHT),
            pltpu.VMEM((8, TILE), F32),
        ],
        compiler_params=pltpu.CompilerParams(vmem_limit_bytes=60 << 20),
    )(
        where, me, start.reshape(1), lengths.reshape(rows, 1), mid, mid, out_grad, grad_rim, score.reshape(1, width), near, far, edges
    )


def shifted_rim(cells, width):
    count = lax.axis_size("seq")
    head, tail = cells[:, :width], cells[:, cells.shape[1] - width :]
    left = lax.ppermute(tail, "seq", [(i, i + 1) for i in range(count - 1)])
    right = lax.ppermute(head, "seq", [(i + 1, i) for i in range(count - 1)])
    return left, right


def marked_ids(byte_ids, lengths, start, taps):
    rows, length = byte_ids.shape
    left, right = shifted_rim(byte_ids, HALO)
    near = jnp.concatenate([left, byte_ids, right], axis=1)
    place = start - HALO + jnp.arange(length + 2 * HALO, dtype=jnp.int32)
    valid = (place[None, :] >= 0) & (place[None, :] < lengths[:, None])
    near = jnp.where(valid, near, -1)
    near = jnp.pad(near, ((0, 0), (TILE - HALO + 2, TILE - HALO + 2)), constant_values=-1)
    span = length + 2 * TILE
    lists = [near[:, k : k + span] for k in range(taps)]
    lists += [jnp.full((rows, span), -1, jnp.int32)] * (8 - taps)
    return jnp.stack(lists, axis=1)


NN = (((1,), (0,)), ((), ()))
NT = (((1,), (1,)), ((), ()))
TN = (((0,), (0,)), ((), ()))


def dot(a, b, dims):
    return lax.dot_general(a, b, dims, preferred_element_type=F32)


def dot2(a, pair, dims):
    return dot(a, pair[0], dims) + dot(a, pair[1], dims)


def dot3(left, right, dims):
    return dot(left[0], right[0], dims) + dot(left[0], right[1], dims) + dot(left[1], right[0], dims)


def bits_of(count):
    return [1 << i for i in range(count.bit_length() - 1)]


def exchange_plan(seq_size, dp_size):
    across = bits_of(seq_size)
    half = len(across) // 2
    along = [("dp", 2 * bit) for bit in reversed(bits_of(dp_size // 2))]
    orders = [across, across[half:] + across[:half]]
    return [[("dp", 1)] + [("seq", bit) for bit in order] + along for order in orders]


def block_index(plan):
    index = jnp.int32(0)
    for axis, bit in plan[: BLOCKS.bit_length() - 1]:
        index = 2 * index + ((lax.axis_index(axis) & bit) != 0).astype(jnp.int32)
    return index


def swap(cells, axis, bit):
    return lax.ppermute(cells, axis, [(i, i ^ bit) for i in range(lax.axis_size(axis))])


def pack_body(where_ref, conv_ref, embed_ref, out_ref, *, slots):
    taps, own, width = conv_ref.shape
    rows = embed_ref.shape[0]
    blocks = width // TILE
    for j in range(blocks):
        out_ref[j * rows : (j + 1) * rows] = embed_ref[:, j * TILE : (j + 1) * TILE].astype(BF)
    for i in range(2 * slots):
        group = 2 * where_ref[1] + ((where_ref[0] & 1) ^ (i // slots))
        unit = jnp.minimum(group * slots + i % slots, taps * blocks - 1)
        column = pl.multiple_of(unit % blocks * TILE, TILE)
        first = blocks * rows + i * own
        out_ref[first : first + own] = conv_ref[unit // blocks, :, pl.ds(column, TILE)].astype(BF)


def pack_weights(where, conv, embed, slots):
    vmem = pl.BlockSpec(memory_space=pltpu.VMEM)
    rows = embed.shape[0] * embed.shape[1] // TILE + 2 * slots * conv.shape[1]
    return pl.pallas_call(
        partial(pack_body, slots=slots),
        in_specs=[pl.BlockSpec(memory_space=pltpu.SMEM), vmem, vmem],
        out_specs=vmem,
        out_shape=jax.ShapeDtypeStruct((rows, TILE), BF),
    )(where, conv, embed)


def tables_body(where_ref, *refs, slots, own, rows):
    *near, far_ref, embed_ref, upper_ref, lower_ref, units = refs
    blocks = embed_ref.shape[1] // TILE
    first = blocks * rows
    for m, near_ref in enumerate(near):
        for other in range(2):
            source = far_ref.at[m] if other else near_ref
            place = where_ref[0] ^ (2 * m + other)
            for j in range(blocks):
                embed_ref[pl.ds(pl.multiple_of(place * rows, 16), rows), j * TILE : (j + 1) * TILE] = source[
                    j * rows : (j + 1) * rows
                ]
            for t in range(slots):
                units[t, pl.ds(pl.multiple_of(place * own, 16), own)] = source[first + t * own : first + (t + 1) * own]
    for t in range(slots):
        table = jnp.dot(embed_ref[...], units[t], preferred_element_type=F32)
        for h, target in enumerate((upper_ref, lower_ref)):
            rows = table[h * TILE : (h + 1) * TILE]
            exponent = exponent_of(jnp.max(jnp.abs(rows), axis=1, keepdims=True))
            code, _ = to_code(rows, exponent)
            turned = jnp.transpose(jnp.broadcast_to(exponent * 16.0, (TILE, TILE)))[0:16]
            target[t] = as_short(jnp.concatenate([code, turned], axis=0))


def make_tables(where, near, far, slots, own, rows):
    width = 2 * len(near) * own
    vmem = pl.BlockSpec(memory_space=pltpu.VMEM)
    unit = jax.ShapeDtypeStruct((slots, TILE + 16, TILE), jnp.int16)
    return pl.pallas_call(
        partial(tables_body, slots=slots, own=own, rows=rows),
        in_specs=[pl.BlockSpec(memory_space=pltpu.SMEM)] + [vmem] * (len(near) + 1),
        out_specs=[vmem] * 3,
        out_shape=[jax.ShapeDtypeStruct((VOCAB, width), BF), unit, unit],
        scratch_shapes=[pltpu.VMEM((slots, width, TILE), BF)],
    )(where, *near, far)


def gather_tables(where, embed, conv, left_root, rims):
    taps, own, width = conv.shape
    rows = embed.shape[0]
    seq, chips = lax.axis_size("seq"), lax.axis_size("dp") // 2
    slots = -(-taps * (width // TILE) // (2 * seq))
    pack = pack_weights(where, conv, embed, slots)
    near = [pack] + [swap(pack, "dp", 2 * m) for m in range(1, chips)]
    first = rows * width // TILE
    other = first + slots * own
    far = swap(jnp.stack([jnp.concatenate([item[:first], item[other:]], axis=0) for item in near]), "dp", 1)
    far, rims = lax.optimization_barrier((far, rims))
    embed_all, *parts = make_tables(where, near, far, slots, own, rows)
    ready = make_ready(where, embed_all, left_root)
    across = bits_of(seq)
    masks = []
    for h in range(2):
        found = [0]
        half = len(across) // 2
        for bit in across[half:] + across[:half] if h else across:
            parts[h] = jnp.concatenate([parts[h], swap(parts[h], "seq", bit)], axis=0)
            found = found + [mask ^ bit for mask in found]
        masks.append(found)
    units, ready = lax.optimization_barrier((jnp.stack(parts), ready))
    return embed_all, units, swap(units, "dp", 1), masks, ready, rims


def final_code(rows):
    exponent = exponent_of(jnp.max(jnp.abs(rows), axis=0, keepdims=True))
    code, _ = to_code(rows, exponent)
    return as_short(jnp.concatenate([code, jnp.broadcast_to(exponent * 16.0, (8, rows.shape[1]))], axis=0))


def fold_body(keep_ref, extra_ref, *refs, gots, pieces, joint, last):
    got_refs, keep_out, extra_out, *sends = refs[:gots], refs[gots], refs[gots + 1], *refs[gots + 2 :]
    rest = keep_ref.shape[1] // pieces
    for h in range(2):
        total, extra = keep_ref[h], extra_ref[h]
        for ref in got_refs if got_refs[0].ndim == 3 else got_refs[h : h + 1]:
            cells, more = decode(ref[h] if ref.ndim == 3 else ref[...])
            total, extra = total + cells, extra + more
        keep_out[h] = final_code(total) if last else total[:rest]
        extra_out[h] = extra
        for m in range(1, pieces):
            code = encode(total[m * rest : (m + 1) * rest], extra)
            if joint:
                sends[m - 1][h] = code
            else:
                sends[h][...] = code


def fold(keep, extra, got, pieces, joint, last=False):
    _, count, width = keep.shape
    rest = count // pieces
    cells = jax.ShapeDtypeStruct((2, rest + 16, width) if joint else (rest + 16, width), jnp.int16)
    sends = 0 if pieces == 1 else pieces - 1 if joint else 2
    first = jax.ShapeDtypeStruct((2, rest, width), F32)
    if last:
        first = jax.ShapeDtypeStruct((2, rest + 8, width), jnp.int16)
    vmem = pl.BlockSpec(memory_space=pltpu.VMEM)
    return pl.pallas_call(
        partial(fold_body, gots=len(got), pieces=pieces, joint=joint, last=last),
        in_specs=[vmem] * (2 + len(got)),
        out_specs=[vmem] * (2 + sends),
        out_shape=[first, jax.ShapeDtypeStruct(extra.shape, F32)] + [cells] * sends,
    )(keep, extra, *got)


def finish_body(cells_ref, out_ref):
    for h in range(2):
        out_ref[h] = final_code(cells_ref[h])


def finish(cells):
    vmem = pl.BlockSpec(memory_space=pltpu.VMEM)
    return pl.pallas_call(
        finish_body,
        in_specs=[vmem],
        out_specs=vmem,
        out_shape=jax.ShapeDtypeStruct((2, cells.shape[1] + 8, cells.shape[2]), jnp.int16),
    )(cells)


def sum_over_devices(keep, send, extra, plans):
    depth = BLOCKS.bit_length() - 1
    across = len([axis for axis, _ in plans[0] if axis == "seq"])
    along = 1 << (depth - 1 - across)
    got = [swap(send, "dp", 1)]
    for step in range(1, 1 + across):
        keep, extra, *sends = fold(keep, extra, got, 2, False)
        got = [swap(sends[h], *plans[h][step]) for h in range(2)]
    keep, extra, *sends = fold(keep, extra, got, along, True)
    if along > 1:
        got = [swap(item, "dp", 2 * m) for m, item in enumerate(sends, 1)]
        keep, extra = fold(keep, extra, got, 1, True, last=len(plans[0]) == depth)
    for axis, bit in plans[0][depth:]:
        keep, extra = keep + swap(keep, axis, bit), extra + swap(extra, axis, bit)
    cells = keep if keep.dtype == jnp.int16 else finish(keep)
    if along > 1:
        cells = jnp.concatenate([cells] + [swap(cells, "dp", 2 * m) for m in range(1, along)], axis=1)
    parts = []
    for h in range(2):
        part = cells[h]
        for axis, bit in reversed(plans[h][1 : 1 + across]):
            part = jnp.concatenate([part, swap(part, axis, bit)], axis=0)
        parts.append(part)
    cells = jnp.stack(parts)
    return cells, swap(cells, "dp", 1), extra


def pick_rows(count, total, first):
    row = lax.broadcasted_iota(jnp.int32, (count, total), 0)
    return (lax.broadcasted_iota(jnp.int32, (count, total), 1) == row + first).astype(F32).astype(BF)


def order_body(
    me_ref, near_ref, far_ref, conv_ref, extra_ref, score_ref, second_ref,
    high_ref, low_ref, grad_ref, entropy_ref, score_grad_ref, score_out_ref, second_out_ref, table,
):
    sums = jnp.concatenate([extra_ref[0], extra_ref[1]], axis=1)
    entropy_ref[...] = sums[1:2, 0:1] / sums[1:2, 1:2]
    score_grad = sums[0:1]
    second = BETA_SECOND * second_ref[...] + (1.0 - BETA_SECOND) * score_grad * score_grad
    score_grad_ref[...] = score_grad
    second_out_ref[...] = second
    score_out_ref[...] = score_ref[...] - RATE_SCORE * score_grad / (jnp.sqrt(second) + EPSILON)
    block = table.shape[0] // BLOCKS
    part = table.shape[1] // 2
    for h in range(2):
        for p in range(BLOCKS):
            source = near_ref if p < BLOCKS // 2 else far_ref
            first = p % (BLOCKS // 2) * (block + 8)
            cells = as_float(source[h, first : first + block + 8])
            rows = cells[:block] * jnp.exp2(cells[block : block + 1] * 0.0625 - 15.0)
            table[pl.ds(pl.multiple_of((me_ref[h] ^ p) * block, 8), block), h * part : (h + 1) * part] = rows
    taps = conv_ref.shape[0]
    total = jnp.zeros(grad_ref.shape, F32)
    for k in range(taps):
        pair = split(table[k * VOCAB : (k + 1) * VOCAB])
        high_ref[k], low_ref[k] = pair
        total = total + dot2(conv_ref[k].astype(BF), pair, NT)
    grad_ref[...] = total


def order_table(me, near, far, conv, extra, score, second):
    taps, own, width = conv.shape
    vmem = pl.BlockSpec(memory_space=pltpu.VMEM)
    table = jax.ShapeDtypeStruct((taps, VOCAB, width), BF)
    row = jax.ShapeDtypeStruct((1, width), F32)
    return pl.pallas_call(
        order_body,
        in_specs=[pl.BlockSpec(memory_space=pltpu.SMEM)] + [vmem] * 6,
        out_specs=[vmem] * 7,
        out_shape=[
            table,
            table,
            jax.ShapeDtypeStruct((own, VOCAB), F32),
            jax.ShapeDtypeStruct((1, 1), F32),
            row,
            row,
            row,
        ],
        scratch_shapes=[pltpu.VMEM((taps * VOCAB, width), F32)],
        compiler_params=pltpu.CompilerParams(vmem_limit_bytes=60 << 20),
    )(me, near, far, conv, extra, score.reshape(1, width), second.reshape(1, width))


def dot2_left(pair, b, dims):
    return dot(pair[0], b, dims) + dot(pair[1], b, dims)


def both(left, right, dims):
    count = left[0].shape[0]
    first = dot(jnp.concatenate(left, axis=0), right[0], dims)
    return first[:count] + first[count:] + dot(left[0], right[1], dims)


def ready_body(where_ref, embed_ref, left_root_ref, square_high, square_low, columns_ref, rooted_high, rooted_low):
    own, width = left_root_ref.shape[1:]
    embed = embed_ref[...]

    @pl.when(pl.program_id(0) == 0)
    def _():
        square_high[...], square_low[...] = split(dot(embed, embed, NT))
        columns_ref[...] = dot(pick_rows(own, width, where_ref[0] * own), embed, NT).astype(BF)

    rooted_high[0], rooted_low[0] = split(dot2_left(split(left_root_ref[0]), embed, NT))


def make_ready(where, embed_all, left_root):
    taps, own, width = left_root.shape
    by_tap = lambda *shape: pl.BlockSpec((1, *shape), lambda k: (k,) + (0,) * len(shape))
    whole = lambda *shape: pl.BlockSpec(shape, lambda k: (0,) * len(shape))
    like = lambda *shape: jax.ShapeDtypeStruct(shape, BF)
    return pl.pallas_call(
        ready_body,
        grid=(taps,),
        in_specs=[
            pl.BlockSpec(memory_space=pltpu.SMEM),
            whole(VOCAB, width),
            by_tap(own, width),
        ],
        out_specs=[whole(VOCAB, VOCAB)] * 2 + [whole(own, VOCAB)] + [by_tap(own, VOCAB)] * 2,
        out_shape=[like(VOCAB, VOCAB)] * 2
        + [like(own, VOCAB)]
        + [like(taps, own, VOCAB)] * 2,
        compiler_params=pltpu.CompilerParams(vmem_limit_bytes=60 << 20),
        cost_estimate=pl.CostEstimate(flops=1 << 30, bytes_accessed=3 << 20, transcendentals=0),
    )(where, embed_all, left_root)


def conv_body(
    where_ref, high_ref, low_ref, embed_ref, square_high, square_low, columns_ref, rooted_high, rooted_low, right_root_ref,
    weight_ref, left_ref, right_ref, grad_out, weight_out, left_out, right_out,
):
    own, width = weight_ref.shape[1:]
    table = high_ref[0], low_ref[0]
    columns = columns_ref[...]
    pick = pick_rows(own, width, where_ref[0] * own)
    high = dot(jnp.concatenate([columns, rooted_high[0], rooted_low[0]], axis=0), table[0], NN)
    low = dot(jnp.concatenate([columns, rooted_high[0]], axis=0), table[1], NN)
    grad = high[:own] + low[:own]
    inner = high[own : 2 * own] + high[2 * own :] + low[own:]
    grad_out[0] = grad
    grad = split(grad)
    high = dot(jnp.concatenate([grad[0], grad[1], pick], axis=0), table[0], NT)
    low = dot(jnp.concatenate([grad[0], pick], axis=0), table[1], NT)
    crossed = split(high[:own] + high[own : 2 * own] + low[:own])
    mine = split(high[2 * own :] + low[own:])
    step = both(split(inner), split(right_root_ref[0]), NN)
    weight_out[0] = weight_ref[0] - RATE_CONV * step
    outer = dot(jnp.concatenate(crossed, axis=0), embed_ref[...], NN)
    left_out[0] = BETA_STAT * left_ref[0] + (1.0 - BETA_STAT) * (outer[:own] + outer[own:])
    outer = both(split(both(mine, (square_high[...], square_low[...]), NN)), table, NN)
    right_out[0] = BETA_STAT * right_ref[0] + (1.0 - BETA_STAT) * outer


def renew_conv(where, high, low, embed_all, ready, right_root, conv, left, right):
    taps, own, width = conv.shape
    by_tap = lambda *shape: pl.BlockSpec((1, *shape), lambda k: (k,) + (0,) * len(shape))
    whole = lambda *shape: pl.BlockSpec(shape, lambda k: (0,) * len(shape))
    rows = by_tap(own, width)
    return pl.pallas_call(
        conv_body,
        grid=(taps,),
        in_specs=[
            pl.BlockSpec(memory_space=pltpu.SMEM),
            by_tap(VOCAB, width),
            by_tap(VOCAB, width),
            whole(VOCAB, width),
            whole(VOCAB, VOCAB),
            whole(VOCAB, VOCAB),
            whole(own, VOCAB),
            by_tap(own, VOCAB),
            by_tap(own, VOCAB),
            by_tap(width, width),
            rows,
            rows,
            rows,
        ],
        out_specs=[rows] * 4,
        out_shape=[jax.ShapeDtypeStruct(conv.shape, F32)] * 4,
        compiler_params=pltpu.CompilerParams(vmem_limit_bytes=60 << 20),
        cost_estimate=pl.CostEstimate(flops=8 << 30, bytes_accessed=32 << 20, transcendentals=0),
    )(where, high, low, embed_all, *ready, right_root, conv, left, right)


def embed_body(
    owner_ref, near_ref, far_ref, weight_ref, left_ref, right_ref, left_root_ref, right_root_ref,
    grad_out, weight_out, left_out, right_out, table,
):
    count, own, _ = near_ref.shape
    rows = weight_ref.shape[0]
    owner = owner_ref[0]
    for m in range(count):
        table[pl.ds(pl.multiple_of((owner ^ (2 * m)) * own, 8), own)] = near_ref[m]
        table[pl.ds(pl.multiple_of((owner ^ (2 * m + 1)) * own, 8), own)] = far_ref[m]
    pair = split(table[...])
    grad = dot2(pick_rows(rows, VOCAB, owner * rows), pair, NT)
    grad_out[...] = grad
    left_out[...] = BETA_STAT * left_ref[...] + (1.0 - BETA_STAT) * dot3(split(grad), pair, NN)
    right_out[...] = BETA_STAT * right_ref[...] + (1.0 - BETA_STAT) * dot3(split(near_ref[0]), pair, NT)
    step = dot3(split(dot3(split(left_root_ref[...]), pair, NT)), split(right_root_ref[...]), NN)
    weight_out[...] = weight_ref[...] - RATE_EMBED * step


def renew_embed(owner, near, far, embed, left, right, left_root, right_root):
    vmem = pl.BlockSpec(memory_space=pltpu.VMEM)
    shapes = [jax.ShapeDtypeStruct(item.shape, F32) for item in (embed, embed, left, right)]
    return pl.pallas_call(
        embed_body,
        in_specs=[pl.BlockSpec(memory_space=pltpu.SMEM)] + [vmem] * 7,
        out_specs=[vmem] * 4,
        out_shape=shapes,
        scratch_shapes=[pltpu.VMEM((embed.shape[1], VOCAB), F32)],
        compiler_params=pltpu.CompilerParams(vmem_limit_bytes=60 << 20),
    )(owner, near, far, embed, left, right, left_root, right_root)


def shards(
    byte_ids,
    lengths,
    embed,
    conv,
    score,
    out_grad,
    embed_left,
    embed_right,
    conv_left,
    conv_right,
    embed_left_root,
    embed_right_root,
    conv_left_root,
    conv_right_root,
    score_second,
):
    length = byte_ids.shape[1]
    width = embed.shape[1]
    taps = conv.shape[0]
    owner = lax.axis_index("dp")
    start = lax.axis_index("seq") * length
    where = jnp.stack([owner, lax.axis_index("seq")]).astype(jnp.int32)
    mid = marked_ids(byte_ids, lengths, start, taps)
    left, right = shifted_rim(out_grad, 1)
    zero = jnp.zeros((byte_ids.shape[0], 7, width), F32)
    grad_rim = jnp.concatenate([zero, left, right, zero], axis=1)
    edges = jnp.stack([left[:, 0], out_grad[:, 0], out_grad[:, -1], right[:, 0]])
    embed_all, near, far, masks, ready, (mid, grad_rim) = gather_tables(
        where, embed, conv, conv_left_root, (mid, grad_rim)
    )
    plans = exchange_plan(lax.axis_size("seq"), lax.axis_size("dp"))
    me = jnp.stack([block_index(plan) for plan in plans])
    output, keep, send, extra = mix(
        where, me, start, lengths, mid, out_grad, grad_rim, score, near, far, edges, masks, taps
    )
    near, far, extra = sum_over_devices(keep, send, extra, plans)
    high, low, columns, entropy, score_grad, new_score, new_score_second = order_table(
        me, near, far, conv, extra, score, score_second
    )
    near = jnp.stack([columns] + [swap(columns, "dp", 2 * m) for m in range(1, lax.axis_size("dp") // 2)])
    conv_grad, new_conv, new_conv_left, new_conv_right = renew_conv(
        where, high, low, embed_all, ready, conv_right_root, conv, conv_left, conv_right
    )
    near, conv_grad = lax.optimization_barrier((near, conv_grad))
    far = swap(near, "dp", 1)
    embed_grad, new_embed, new_embed_left, new_embed_right = renew_embed(
        where, near, far, embed, embed_left, embed_right, embed_left_root, embed_right_root
    )
    return (
        output,
        entropy.reshape(()),
        embed_grad,
        conv_grad,
        score_grad.reshape(width),
        new_embed,
        new_conv,
        new_score.reshape(width),
        new_embed_left,
        new_embed_right,
        new_conv_left,
        new_conv_right,
        new_score_second.reshape(width),
    )


def solution(mesh):
    placed = (
        P("dp", "seq"),
        P("dp"),
        P("dp", None),
        P(None, "dp", None),
        P(),
        P("dp", "seq", None),
        P("dp", None),
        P("dp", None),
        P(None, "dp", None),
        P(None, "dp", None),
        P("dp", None),
        P(),
        P(None, "dp", None),
        P(),
        P(),
    )
    return jax.shard_map(
        shards,
        mesh=mesh,
        in_specs=placed,
        out_specs=(
            P("dp", "seq", None),
            P(),
            P("dp", None),
            P(None, "dp", None),
            P(),
            P("dp", None),
            P(None, "dp", None),
            P(),
            P("dp", None),
            P("dp", None),
            P(None, "dp", None),
            P(None, "dp", None),
            P(),
        ),
        check_vma=False,
    )
```

```python
from functools import partial

import jax
import jax.numpy as jnp
from jax import lax
from jax.experimental import pallas as pl
from jax.experimental.pallas import tpu as pltpu
from jax.sharding import PartitionSpec as P

VOCAB = 256
SIZES = 4
BETA_STAT = 0.9
BETA_SECOND = 0.99
RATE_EMBED = 10.0
RATE_CONV = 0.25
RATE_SCORE = 0.012
EPSILON = 1e-08
TILE = 128
HALO = 8
BLOCKS = 32
WIN = TILE // 2 + 16
BF = jnp.bfloat16
F32 = jnp.float32
LIGHT = jnp.float8_e4m3fn


def split(v):
    high = v.astype(BF)
    return high, (v - high.astype(F32)).astype(BF)


def exponent_of(v):
    return jnp.clip(jnp.ceil(jnp.log2(jnp.maximum(v, 1e-30)) * 16.0), -1440.0, 1920.0) * 0.0625


def to_code(v, exponent):
    scaled = v * jnp.exp2(15.0 - exponent)
    code = jnp.clip(jnp.floor(scaled + 0.5), -32767.0, 32767.0)
    return code, scaled - code


def as_short(v):
    return v.astype(jnp.int32).astype(jnp.int16)


def as_float(v):
    return v.astype(jnp.int32).astype(F32)


def encode(rows, extra):
    exponent = exponent_of(jnp.max(jnp.abs(rows), axis=0, keepdims=True))
    code, _ = to_code(rows, exponent)
    few = extra[0:2]
    powers = exponent_of(jnp.abs(few))
    high, rest = to_code(few, powers)
    low = jnp.floor(rest * 16384.0 + 0.5)
    blank = jnp.zeros((9, rows.shape[1]), F32)
    return as_short(jnp.concatenate([code, exponent * 16.0, high, low, powers * 16.0, blank], axis=0))


def decode(cells):
    cells = as_float(cells)
    count = cells.shape[0] - 16
    more = cells[count:]
    extra = (more[1:3] + more[3:5] * (1.0 / 16384.0)) * jnp.exp2(more[5:7] * 0.0625 - 15.0)
    extra = jnp.concatenate([extra, jnp.zeros((6, extra.shape[1]), F32)], axis=0)
    return cells[:count] * jnp.exp2(more[0:1] * 0.0625 - 15.0), extra


def roll_to(v, offset):
    width = v.shape[-1]
    return v if offset == 0 else pltpu.roll(v, (-offset) % width, v.ndim - 1)


def score_rows(score_ref):
    high, low = (part.astype(F32) for part in split(score_ref[...]))
    row = lax.broadcasted_iota(jnp.int32, (16, high.shape[1]), 0)
    return jnp.where((row == 0) | (row == 2), high, jnp.where(row == 1, low, 0.0)).astype(BF)


def grad_window(g_ref, gh_ref, r, i, tiles):
    half = tiles * TILE // 2
    first, last = i * TILE // 2 - 8, (i + 1) * TILE // 2 + 8
    parts = [g_ref[r, max(first, 0) : min(last, half)]]
    if i == 0:
        parts = [gh_ref[r, 0:8]] + parts
    if i == tiles - 1:
        parts = parts + [gh_ref[r, 8:16]]
    return split(jnp.concatenate(parts, axis=0))


def lookup_body(
    where_ref, mid_ref, next_ref, g_ref, gh_ref, score_ref, near_ref, far_ref, hid_ref, rim_ref, band_ref, table_ref, onehot_ref, spread, hidden, few_ref, light_ref, scale_ref,
    *, masks, taps,
):
    length = hid_ref.shape[1] * TILE
    blocks = table_ref.shape[1] // TILE
    slots = near_ref.shape[1] // len(masks[0])

    @pl.when(pl.program_id(0) == 0)
    def _():
        spare = taps * VOCAB
        top = jnp.full((1, TILE), -1440.0, F32)
        for h in range(2):
            for spot in range(near_ref.shape[1]):
                for source in (near_ref, far_ref):
                    top = jnp.maximum(top, as_float(source[h, spot, TILE : TILE + 16])[0:1])
        top = jnp.ceil(jnp.max(top, axis=1, keepdims=True) * 0.0625)
        scale_ref[...] = jnp.broadcast_to(jnp.exp2(top - 16.0), scale_ref.shape)
        grow = jnp.exp2(16.0 - top)
        for spot in range(near_ref.shape[1]):
            found = []
            for h in range(2):
                for other, source in enumerate((near_ref, far_ref)):
                    group = 2 * (where_ref[1] ^ masks[h][spot // slots]) + ((where_ref[0] & 1) ^ other)
                    unit = group * slots + spot % slots
                    cells = as_float(source[h, spot])
                    power = jnp.transpose(cells[TILE : TILE + 8])[:, 0:1]
                    rows = cells[:TILE] * jnp.exp2(power * 0.0625 - 15.0)
                    high = rows.astype(BF)
                    low = ((rows - high.astype(F32)) * grow).astype(LIGHT)
                    row = unit // blocks * VOCAB + h * TILE
                    row = pl.multiple_of(jnp.where(unit < taps * blocks, row, spare), TILE)
                    found.append((row, pl.multiple_of(unit % blocks * TILE, TILE), high, low))
            for row, column, high, low in found:
                table_ref[pl.ds(row, TILE), pl.ds(column, TILE)] = high
                few_ref[pl.ds(row, TILE), pl.ds(column, TILE)] = low

    tiles = length // TILE
    lanes = lax.broadcasted_iota(jnp.int32, (1, VOCAB), 1).astype(F32)

    def mark(ref):
        columns = jnp.transpose(ref[0].astype(F32))
        ids = [columns[TILE : TILE + length], columns[TILE - HALO : TILE], columns[TILE + length : TILE + length + HALO]]
        ids = jnp.concatenate(ids, axis=0)
        for k in range(taps):
            hit = (ids[:, k : k + 1] == lanes).astype(F32)
            onehot_ref[:, k * VOCAB : (k + 1) * VOCAB] = hit.astype(BF)
            light_ref[:, k * VOCAB : (k + 1) * VOCAB] = hit.astype(LIGHT)

    @pl.when(pl.program_id(0) == 0)
    def _():
        mark(mid_ref)

    onehot, light = onehot_ref[...], light_ref[...]
    scale = scale_ref[0:1, 0:1]
    for m in range(spread.shape[0]):
        at = slice(m * TILE, (m + 1) * TILE)
        spread[m, 0:8] = jnp.broadcast_to(gh_ref[0, 7:8, at], (8, TILE))
        spread[m, 8 + length :] = jnp.broadcast_to(gh_ref[0, 8:9, at], (8, TILE))
        rows = g_ref[0, :, at]
        spread[m, pl.ds(8, length // 2, stride=2)] = rows
        spread[m, pl.ds(9, length // 2, stride=2)] = rows
    for n in range(0, table_ref.shape[1], 256):
        low = jnp.dot(light, few_ref[0 : taps * VOCAB, n : n + 256], preferred_element_type=F32)
        cells = jnp.dot(onehot, table_ref[0 : taps * VOCAB, n : n + 256], preferred_element_type=F32) + low * scale
        hidden[:, n : n + 256] = cells
        h_high, h_low = split(cells[0:length])
        for i in range(tiles):
            hid_ref[0, i, 0:TILE, n : n + 256] = h_high[i * TILE : (i + 1) * TILE]
            hid_ref[0, i, TILE : 2 * TILE, n : n + 256] = h_low[i * TILE : (i + 1) * TILE]
        rim_ref[0, :, n : n + 256] = cells[length:]
    mark(next_ref)
    columns = []
    for t in range(0, length, 64):
        sums = [jnp.zeros((64, TILE), F32)] * 4
        for m in range(spread.shape[0]):
            part = hidden[t : t + 64, m * TILE : (m + 1) * TILE]
            for d in range(3):
                sums[d] = sums[d] + part * spread[m, 6 + 2 * d + t : 6 + 2 * d + t + 64]
            sums[3] = sums[3] + part * score_ref[:, m * TILE : (m + 1) * TILE]
        row = [jnp.sum(item, axis=1, keepdims=True) for item in sums]
        columns.append(jnp.concatenate(row + [jnp.zeros((64, 4), F32)], axis=1))
    band_ref[0, :, TILE : TILE + length] = jnp.transpose(jnp.concatenate(columns, axis=0))
    blank = jnp.zeros((8, TILE), F32)
    band_ref[0, :, 0:TILE] = blank
    band_ref[0, :, TILE + length :] = blank


def weigh_body(band_ref, lengths_ref, start_ref, score_ref, rim_ref, edge_ref, out_ref, sums_ref, spill_ref):
    rows, _, span = band_ref.shape
    length = span - 2 * TILE
    start = start_ref[0]
    lane = lax.broadcasted_iota(jnp.int32, (rows, span), 1)
    place = start + lane - TILE
    valid = ((place >= 0) & (place < lengths_ref[...])).astype(F32)
    phase3 = lax.rem(place + 3 * TILE, 3)
    phase4 = place & 3
    even = (place & 1) == 0
    inside = {
        1: {0: None},
        2: {0: None, 1: even, -1: ~even},
        3: {0: None, 1: phase3 <= 1, 2: phase3 == 0, -1: phase3 >= 1, -2: phase3 == 2},
        4: {0: None, **{d: phase4 <= 3 - d for d in (1, 2, 3)}, **{-d: phase4 >= d for d in (1, 2, 3)}},
    }

    def over_block(size, pick):
        total = pick(0)
        for d, mask in inside[size].items():
            if d != 0:
                total = total + jnp.where(mask, pick(d), 0.0)
        return total

    def shifts(v):
        return {d: roll_to(v, d) for d in range(-3, 4)}

    base = [band_ref[:, d, :] for d in range(4)]
    edges = [edge_ref[j] for j in range(4)]
    meets = {4: {2: 0}, 5: {2: 0}, 6: {1: 0, 2: 1}, 7: {1: 0, 2: 1}}
    meets.update({8: {1: 3, 0: 2}, 9: {1: 3, 0: 2}, 10: {0: 3}, 11: {0: 3}})
    spots = {spot: TILE - 8 + spot + (length if spot >= 8 else 0) for spot in meets}
    near = {spot: rim_ref[:, spot, :] for spot in meets}
    for spot, pairs in meets.items():
        here = lane == spots[spot]
        base[3] = jnp.where(here, jnp.sum(near[spot] * score_ref[...], axis=1, keepdims=True), base[3])
        for d, j in pairs.items():
            base[d] = jnp.where(here, jnp.sum(near[spot] * edges[j], axis=1, keepdims=True), base[d])
    dots = shifts(base[3] * valid)
    scores = [over_block(b, lambda d: dots[d]) * (1.0 / b) for b in range(1, SIZES + 1)]
    highest = jnp.maximum(jnp.maximum(scores[0], scores[1]), jnp.maximum(scores[2], scores[3]))
    powers = [jnp.exp(item - highest) for item in scores]
    total = powers[0] + powers[1] + powers[2] + powers[3]
    probs = [item / total for item in powers]
    log_total = jnp.log(total)
    entropy = jnp.zeros_like(total)
    for b in range(SIZES):
        entropy = entropy - probs[b] * (scores[b] - highest - log_total)
    own = (lane >= TILE) & (lane < TILE + length)
    own_valid = jnp.where(own, valid, 0.0)
    entropy = jnp.sum(jnp.where(own, entropy * valid, 0.0), axis=1, keepdims=True)
    count = jnp.sum(own_valid, axis=1, keepdims=True)
    sums_ref[...] = jnp.where(lax.broadcasted_iota(jnp.int32, (rows, TILE), 1) == 0, entropy, count)
    below, same, above = (shifts(base[d] * valid) for d in range(3))
    close = {0: same[0], 1: jnp.where(even, same[1], below[1]), 2: below[2], 3: below[3]}
    close.update({-1: jnp.where(even, above[-1], same[-1]), -2: above[-2], -3: above[-3]})
    inner = [over_block(b, lambda d: close[d]) * (valid * (0.5 / b)) for b in range(1, SIZES + 1)]
    mean = probs[0] * inner[0] + probs[1] * inner[1] + probs[2] * inner[2] + probs[3] * inner[3]
    score_in = [probs[b] * (inner[b] - mean) for b in range(SIZES)]
    pull = jnp.zeros_like(total)
    for b in range(1, SIZES + 1):
        moved = shifts(score_in[b - 1])
        pull = pull + over_block(b, lambda d: moved[d]) * (1.0 / b)
    weight = {d: jnp.zeros_like(total) for d in range(-3, 4)}
    for b in range(1, SIZES + 1):
        moved = shifts(probs[b - 1] * valid * (0.5 / b))
        for d, mask in inside[b].items():
            weight[d] = weight[d] + (moved[d] if mask is None else jnp.where(mask, moved[d], 0.0))
    below = valid * (weight[-2] + jnp.where(even, weight[-1], weight[-3]))
    above = valid * (weight[2] + jnp.where(even, weight[3], weight[1]))
    pick = lambda v, spot: jnp.sum(jnp.where(lane == spots[spot], v, 0.0), axis=1, keepdims=True) * near[spot]
    spill_ref[...] = jnp.zeros_like(spill_ref)
    spill_ref[:, 0, :] = pick(above, 6) + pick(above, 7)
    spill_ref[:, 7, :] = pick(below, 8) + pick(below, 9)
    out_ref[:, 0, :] = below
    out_ref[:, 1, :] = valid * (weight[0] + jnp.where(even, weight[1], weight[-1]))
    out_ref[:, 2, :] = above
    out_ref[:, 3, :] = valid * pull
    for d in range(4, 8):
        out_ref[:, d, :] = jnp.zeros_like(total)


def apply_body(
    me_ref, mid_ref, g_ref, gh_ref, score_ref, hid_ref, spill_ref, weight_ref, sums_ref,
    out_ref, keep_ref, send_ref, extra_ref, onehot, hgrad, total, table_ref, pull_ref, staged,
    *, first,
):
    length = hid_ref.shape[1] * TILE
    half = length // 2
    taps = table_ref.shape[0] // VOCAB

    @pl.when(pl.program_id(0) == first)
    def _():
        table_ref[...] = jnp.zeros_like(table_ref)
        pull_ref[...] = jnp.zeros_like(pull_ref)

    score = score_rows(score_ref)
    for r in range(mid_ref.shape[0]):
        cells = lax.broadcasted_iota(jnp.int32, (VOCAB, length), 0)
        for tap in range(taps):
            hit = mid_ref[r, tap : tap + 1, TILE : TILE + length] == cells
            onehot[tap * VOCAB : (tap + 1) * VOCAB, r * length : (r + 1) * length] = hit.astype(F32).astype(BF)
        total[...] = jnp.zeros_like(total)
        pulled = jnp.zeros((1, total.shape[1]), F32)
        for i in range(length // TILE):
            w = weight_ref[r, :, TILE * (i + 1) : TILE * (i + 2)]
            place = lax.broadcasted_iota(jnp.int32, (WIN, TILE), 0) - 8
            gap = place - (lax.broadcasted_iota(jnp.int32, (WIN, TILE), 1) >> 1)
            a = jnp.where(gap == 0, w[1:2], 0.0)
            a = jnp.where(gap == -1, w[0:1], a)
            a = jnp.where(gap == 1, w[2:3], a)
            a_high, a_low = split(a)
            q_high, q_low = split(w[3:4])
            sub = lax.broadcasted_iota(jnp.int32, (16, TILE), 0)
            q = jnp.where(sub < 2, q_high.astype(F32), jnp.where(sub == 2, q_low.astype(F32), 0.0)).astype(BF)
            g_high, g_low = grad_window(g_ref, gh_ref, r, i, length // TILE)
            stack = jnp.concatenate([g_high, g_low, g_high, score], axis=0)
            left = jnp.concatenate([a_high, a_high, a_low, q], axis=0)
            hg = lax.dot_general(left, stack, (((0,), (0,)), ((), ())), preferred_element_type=F32)
            hgrad[r * length + i * TILE : r * length + (i + 1) * TILE] = hg.astype(BF)
            left = jnp.concatenate([a_high, a_low, q], axis=0)
            res = jnp.dot(jnp.concatenate([left, left], axis=1), hid_ref[r, i], preferred_element_type=F32)
            total[i * TILE // 2 : i * TILE // 2 + WIN] += res[0:WIN] + res[WIN : 2 * WIN]
            pulled = pulled + res[2 * WIN : 2 * WIN + 1] + res[2 * WIN + 2 : 2 * WIN + 3]
        total[8:16] += jnp.where(lax.broadcasted_iota(jnp.int32, spill_ref.shape[1:], 0) == 0, spill_ref[r], 0.0)
        total[half : half + 8] += jnp.where(lax.broadcasted_iota(jnp.int32, spill_ref.shape[1:], 0) == 7, spill_ref[r], 0.0)
        out_ref[r] = total[8 : half + 8]
        pull_ref[0:1] += pulled
    table_ref[...] += jnp.dot(onehot[...], hgrad[...], preferred_element_type=F32)

    @pl.when(pl.program_id(0) == pl.num_programs(0) - 1)
    def _():
        row = lax.broadcasted_iota(jnp.int32, pull_ref.shape, 0)
        lane = lax.broadcasted_iota(jnp.int32, pull_ref.shape, 1)
        counts = jnp.sum(sums_ref[...], axis=0, keepdims=True)
        counts = jnp.concatenate([counts] + [jnp.zeros_like(counts)] * (pull_ref.shape[1] // TILE - 1), axis=1)
        extra = jnp.where((row == 1) & (lane < 2), counts, pull_ref[...])
        part = extra.shape[1] // 2
        block = table_ref.shape[0] // BLOCKS
        half_rows = BLOCKS // 2 * block
        for h in range(2):
            mine = extra[:, h * part : (h + 1) * part]
            extra_ref[h] = mine
            for p in range(BLOCKS):
                source = pl.multiple_of((me_ref[h] ^ p) * block, 8)
                rows = table_ref[pl.ds(source, block), h * part : (h + 1) * part]
                if p < BLOCKS // 2:
                    keep_ref[h, p * block : (p + 1) * block] = rows
                else:
                    staged[p * block - half_rows : (p + 1) * block - half_rows] = rows
            send_ref[h] = encode(staged[...], mine)


def mix_body(
    where_ref, me_ref, start_ref, lengths_ref, mid_ref, next_ref, g_ref, gh_ref, score_ref, near_ref, far_ref, edge_ref,
    out_ref, keep_ref, send_ref, extra_ref,
    hid, rim, band, weights, sums, spill, table, onehot, spread, hidden, turned, hgrad, total, gathered, pulled, staged, few, light, scale,
    *, masks, taps,
):
    step = pl.program_id(0)
    rows = hid.shape[0]

    @pl.when(step < rows)
    def _():
        here = pl.ds(step, 1)
        lookup_body(
            where_ref, mid_ref, next_ref, g_ref, gh_ref, score_ref, near_ref, far_ref,
            hid.at[here], rim.at[here], band.at[here], table, onehot, spread, hidden, few, light, scale, masks=masks, taps=taps,
        )

    @pl.when(step == rows)
    def _():
        weigh_body(band, lengths_ref, start_ref, score_ref, rim, edge_ref, weights, sums, spill)

    @pl.when(step >= rows)
    def _():
        here = pl.ds(step - rows, 1)
        apply_body(
            me_ref, mid_ref, g_ref, gh_ref, score_ref, hid.at[here], spill.at[here], weights.at[here], sums,
            out_ref, keep_ref, send_ref, extra_ref, turned, hgrad, total, gathered, pulled, staged, first=rows,
        )


def mix(where, me, start, lengths, mid, out_grad, grad_rim, score, near, far, edges, masks, taps):
    rows, _, span = mid.shape
    half, width = out_grad.shape[1:]
    length = 2 * half
    tiles = length // TILE
    whole = lambda *shape: pl.BlockSpec(shape, lambda t: (0,) * len(shape), pipeline_mode=pl.Buffered(1))
    by_row = lambda *shape: pl.BlockSpec((1, *shape), lambda t: (lax.rem(t, rows),) + (0,) * len(shape))
    smem = pl.BlockSpec(memory_space=pltpu.SMEM)
    return pl.pallas_call(
        partial(mix_body, masks=masks, taps=taps),
        grid=(2 * rows,),
        in_specs=[
            smem,
            smem,
            smem,
            whole(rows, 1),
            by_row(8, span),
            pl.BlockSpec((1, 8, span), lambda t: (jnp.minimum(t + 1, rows - 1), 0, 0)),
            by_row(half, width),
            by_row(16, width),
            whole(1, width),
            whole(*near.shape),
            whole(*far.shape),
            whole(*edges.shape),
        ],
        out_specs=[
            pl.BlockSpec((1, half, width), lambda t: (jnp.maximum(t - rows, 0), 0, 0)),
            whole(2, taps * VOCAB // 2, width // 2),
            whole(2, taps * VOCAB // 2 + 16, width // 2),
            whole(2, 8, width // 2),
        ],
        out_shape=[
            jax.ShapeDtypeStruct((rows, half, width), F32),
            jax.ShapeDtypeStruct((2, taps * VOCAB // 2, width // 2), F32),
            jax.ShapeDtypeStruct((2, taps * VOCAB // 2 + 16, width // 2), jnp.int16),
            jax.ShapeDtypeStruct((2, 8, width // 2), F32),
        ],
        scratch_shapes=[
            pltpu.VMEM((rows, tiles, 2 * TILE, width), BF),
            pltpu.VMEM((rows, 16, width), F32),
            pltpu.VMEM((rows, 8, span), F32),
            pltpu.VMEM((rows, 8, span), F32),
            pltpu.VMEM((rows, TILE), F32),
            pltpu.VMEM((rows, 8, width), F32),
            pltpu.VMEM((taps * VOCAB + TILE, width), BF),
            pltpu.VMEM((length + 2 * HALO, taps * VOCAB), BF),
            pltpu.VMEM((width // TILE, length + 16, TILE), F32),
            pltpu.VMEM((length + 2 * HALO, width), F32),
            pltpu.VMEM((taps * VOCAB, length), BF),
            pltpu.VMEM((length, width), BF),
            pltpu.VMEM((half + 16, width), F32),
            pltpu.VMEM((taps * VOCAB, width), F32),
            pltpu.VMEM((8, width), F32),
            pltpu.VMEM((taps * VOCAB // 2, width // 2), F32),
            pltpu.VMEM((taps * VOCAB + TILE, width), LIGHT),
            pltpu.VMEM((length + 2 * HALO, taps * VOCAB), LIGHT),
            pltpu.VMEM((8, TILE), F32),
        ],
        compiler_params=pltpu.CompilerParams(vmem_limit_bytes=60 << 20),
    )(
        where, me, start.reshape(1), lengths.reshape(rows, 1), mid, mid, out_grad, grad_rim, score.reshape(1, width), near, far, edges
    )


def shifted_rim(cells, width):
    count = lax.axis_size("seq")
    head, tail = cells[:, :width], cells[:, cells.shape[1] - width :]
    left = lax.ppermute(tail, "seq", [(i, i + 1) for i in range(count - 1)])
    right = lax.ppermute(head, "seq", [(i + 1, i) for i in range(count - 1)])
    return left, right


def marked_ids(byte_ids, lengths, start, taps):
    rows, length = byte_ids.shape
    left, right = shifted_rim(byte_ids, HALO)
    near = jnp.concatenate([left, byte_ids, right], axis=1)
    place = start - HALO + jnp.arange(length + 2 * HALO, dtype=jnp.int32)
    valid = (place[None, :] >= 0) & (place[None, :] < lengths[:, None])
    near = jnp.where(valid, near, -1)
    near = jnp.pad(near, ((0, 0), (TILE - HALO + 2, TILE - HALO + 2)), constant_values=-1)
    span = length + 2 * TILE
    lists = [near[:, k : k + span] for k in range(taps)]
    lists += [jnp.full((rows, span), -1, jnp.int32)] * (8 - taps)
    return jnp.stack(lists, axis=1)


NN = (((1,), (0,)), ((), ()))
NT = (((1,), (1,)), ((), ()))
TN = (((0,), (0,)), ((), ()))


def dot(a, b, dims):
    return lax.dot_general(a, b, dims, preferred_element_type=F32)


def dot2(a, pair, dims):
    return dot(a, pair[0], dims) + dot(a, pair[1], dims)


def dot3(left, right, dims):
    return dot(left[0], right[0], dims) + dot(left[0], right[1], dims) + dot(left[1], right[0], dims)


def bits_of(count):
    return [1 << i for i in range(count.bit_length() - 1)]


def exchange_plan(seq_size, dp_size):
    across = bits_of(seq_size)
    half = len(across) // 2
    along = [("dp", 2 * bit) for bit in reversed(bits_of(dp_size // 2))]
    orders = [across, across[half:] + across[:half]]
    return [[("dp", 1)] + [("seq", bit) for bit in order] + along for order in orders]


def block_index(plan):
    index = jnp.int32(0)
    for axis, bit in plan[: BLOCKS.bit_length() - 1]:
        index = 2 * index + ((lax.axis_index(axis) & bit) != 0).astype(jnp.int32)
    return index


def swap(cells, axis, bit):
    return lax.ppermute(cells, axis, [(i, i ^ bit) for i in range(lax.axis_size(axis))])


def pack_body(where_ref, conv_ref, embed_ref, out_ref, *, slots):
    taps, own, width = conv_ref.shape
    rows = embed_ref.shape[0]
    blocks = width // TILE
    for j in range(blocks):
        out_ref[j * rows : (j + 1) * rows] = embed_ref[:, j * TILE : (j + 1) * TILE].astype(BF)
    for i in range(2 * slots):
        group = 2 * where_ref[1] + ((where_ref[0] & 1) ^ (i // slots))
        unit = jnp.minimum(group * slots + i % slots, taps * blocks - 1)
        column = pl.multiple_of(unit % blocks * TILE, TILE)
        first = blocks * rows + i * own
        out_ref[first : first + own] = conv_ref[unit // blocks, :, pl.ds(column, TILE)].astype(BF)


def pack_weights(where, conv, embed, slots):
    vmem = pl.BlockSpec(memory_space=pltpu.VMEM)
    rows = embed.shape[0] * embed.shape[1] // TILE + 2 * slots * conv.shape[1]
    return pl.pallas_call(
        partial(pack_body, slots=slots),
        in_specs=[pl.BlockSpec(memory_space=pltpu.SMEM), vmem, vmem],
        out_specs=vmem,
        out_shape=jax.ShapeDtypeStruct((rows, TILE), BF),
    )(where, conv, embed)


def tables_body(where_ref, *refs, slots, own, rows):
    *near, far_ref, embed_ref, upper_ref, lower_ref, units = refs
    blocks = embed_ref.shape[1] // TILE
    first = blocks * rows
    for m, near_ref in enumerate(near):
        for other in range(2):
            source = far_ref.at[m] if other else near_ref
            place = where_ref[0] ^ (2 * m + other)
            for j in range(blocks):
                embed_ref[pl.ds(pl.multiple_of(place * rows, 16), rows), j * TILE : (j + 1) * TILE] = source[
                    j * rows : (j + 1) * rows
                ]
            for t in range(slots):
                units[t, pl.ds(pl.multiple_of(place * own, 16), own)] = source[first + t * own : first + (t + 1) * own]
    for t in range(slots):
        table = jnp.dot(embed_ref[...], units[t], preferred_element_type=F32)
        for h, target in enumerate((upper_ref, lower_ref)):
            rows = table[h * TILE : (h + 1) * TILE]
            exponent = exponent_of(jnp.max(jnp.abs(rows), axis=1, keepdims=True))
            code, _ = to_code(rows, exponent)
            turned = jnp.transpose(jnp.broadcast_to(exponent * 16.0, (TILE, TILE)))[0:16]
            target[t] = as_short(jnp.concatenate([code, turned], axis=0))


def make_tables(where, near, far, slots, own, rows):
    width = 2 * len(near) * own
    vmem = pl.BlockSpec(memory_space=pltpu.VMEM)
    unit = jax.ShapeDtypeStruct((slots, TILE + 16, TILE), jnp.int16)
    return pl.pallas_call(
        partial(tables_body, slots=slots, own=own, rows=rows),
        in_specs=[pl.BlockSpec(memory_space=pltpu.SMEM)] + [vmem] * (len(near) + 1),
        out_specs=[vmem] * 3,
        out_shape=[jax.ShapeDtypeStruct((VOCAB, width), BF), unit, unit],
        scratch_shapes=[pltpu.VMEM((slots, width, TILE), BF)],
    )(where, *near, far)


def gather_tables(where, embed, conv, left_root, rims):
    taps, own, width = conv.shape
    rows = embed.shape[0]
    seq, chips = lax.axis_size("seq"), lax.axis_size("dp") // 2
    slots = -(-taps * (width // TILE) // (2 * seq))
    pack = pack_weights(where, conv, embed, slots)
    near = [pack] + [swap(pack, "dp", 2 * m) for m in range(1, chips)]
    first = rows * width // TILE
    other = first + slots * own
    far = swap(jnp.stack([jnp.concatenate([item[:first], item[other:]], axis=0) for item in near]), "dp", 1)
    far, rims = lax.optimization_barrier((far, rims))
    embed_all, *parts = make_tables(where, near, far, slots, own, rows)
    ready = make_ready(where, embed_all, left_root)
    across = bits_of(seq)
    masks = []
    for h in range(2):
        found = [0]
        half = len(across) // 2
        for bit in across[half:] + across[:half] if h else across:
            parts[h] = jnp.concatenate([parts[h], swap(parts[h], "seq", bit)], axis=0)
            found = found + [mask ^ bit for mask in found]
        masks.append(found)
    units, ready = lax.optimization_barrier((jnp.stack(parts), ready))
    return embed_all, units, swap(units, "dp", 1), masks, ready, rims


def final_code(rows):
    exponent = exponent_of(jnp.max(jnp.abs(rows), axis=0, keepdims=True))
    code, _ = to_code(rows, exponent)
    return as_short(jnp.concatenate([code, jnp.broadcast_to(exponent * 16.0, (8, rows.shape[1]))], axis=0))


def fold_body(keep_ref, extra_ref, *refs, gots, pieces, joint, last):
    got_refs, keep_out, extra_out, *sends = refs[:gots], refs[gots], refs[gots + 1], *refs[gots + 2 :]
    rest = keep_ref.shape[1] // pieces
    for h in range(2):
        total, extra = keep_ref[h], extra_ref[h]
        for ref in got_refs if got_refs[0].ndim == 3 else got_refs[h : h + 1]:
            cells, more = decode(ref[h] if ref.ndim == 3 else ref[...])
            total, extra = total + cells, extra + more
        keep_out[h] = final_code(total) if last else total[:rest]
        extra_out[h] = extra
        for m in range(1, pieces):
            code = encode(total[m * rest : (m + 1) * rest], extra)
            if joint:
                sends[m - 1][h] = code
            else:
                sends[h][...] = code


def fold(keep, extra, got, pieces, joint, last=False):
    _, count, width = keep.shape
    rest = count // pieces
    cells = jax.ShapeDtypeStruct((2, rest + 16, width) if joint else (rest + 16, width), jnp.int16)
    sends = 0 if pieces == 1 else pieces - 1 if joint else 2
    first = jax.ShapeDtypeStruct((2, rest, width), F32)
    if last:
        first = jax.ShapeDtypeStruct((2, rest + 8, width), jnp.int16)
    vmem = pl.BlockSpec(memory_space=pltpu.VMEM)
    return pl.pallas_call(
        partial(fold_body, gots=len(got), pieces=pieces, joint=joint, last=last),
        in_specs=[vmem] * (2 + len(got)),
        out_specs=[vmem] * (2 + sends),
        out_shape=[first, jax.ShapeDtypeStruct(extra.shape, F32)] + [cells] * sends,
    )(keep, extra, *got)


def finish_body(cells_ref, out_ref):
    for h in range(2):
        out_ref[h] = final_code(cells_ref[h])


def finish(cells):
    vmem = pl.BlockSpec(memory_space=pltpu.VMEM)
    return pl.pallas_call(
        finish_body,
        in_specs=[vmem],
        out_specs=vmem,
        out_shape=jax.ShapeDtypeStruct((2, cells.shape[1] + 8, cells.shape[2]), jnp.int16),
    )(cells)


def sum_over_devices(keep, send, extra, plans):
    depth = BLOCKS.bit_length() - 1
    across = len([axis for axis, _ in plans[0] if axis == "seq"])
    along = 1 << (depth - 1 - across)
    got = [swap(send, "dp", 1)]
    for step in range(1, 1 + across):
        keep, extra, *sends = fold(keep, extra, got, 2, False)
        got = [swap(sends[h], *plans[h][step]) for h in range(2)]
    keep, extra, *sends = fold(keep, extra, got, along, True)
    if along > 1:
        got = [swap(item, "dp", 2 * m) for m, item in enumerate(sends, 1)]
        keep, extra = fold(keep, extra, got, 1, True, last=len(plans[0]) == depth)
    for axis, bit in plans[0][depth:]:
        keep, extra = keep + swap(keep, axis, bit), extra + swap(extra, axis, bit)
    cells = keep if keep.dtype == jnp.int16 else finish(keep)
    if along > 1:
        cells = jnp.concatenate([cells] + [swap(cells, "dp", 2 * m) for m in range(1, along)], axis=1)
    parts = []
    for h in range(2):
        part = cells[h]
        for axis, bit in reversed(plans[h][1 : 1 + across]):
            part = jnp.concatenate([part, swap(part, axis, bit)], axis=0)
        parts.append(part)
    cells = jnp.stack(parts)
    return cells, swap(cells, "dp", 1), extra


def pick_rows(count, total, first):
    row = lax.broadcasted_iota(jnp.int32, (count, total), 0)
    return (lax.broadcasted_iota(jnp.int32, (count, total), 1) == row + first).astype(F32).astype(BF)


def order_body(
    me_ref, near_ref, far_ref, conv_ref, extra_ref, score_ref, second_ref,
    high_ref, low_ref, grad_ref, entropy_ref, score_grad_ref, score_out_ref, second_out_ref, table,
):
    sums = jnp.concatenate([extra_ref[0], extra_ref[1]], axis=1)
    entropy_ref[...] = sums[1:2, 0:1] / sums[1:2, 1:2]
    score_grad = sums[0:1]
    second = BETA_SECOND * second_ref[...] + (1.0 - BETA_SECOND) * score_grad * score_grad
    score_grad_ref[...] = score_grad
    second_out_ref[...] = second
    score_out_ref[...] = score_ref[...] - RATE_SCORE * score_grad / (jnp.sqrt(second) + EPSILON)
    block = table.shape[0] // BLOCKS
    part = table.shape[1] // 2
    for h in range(2):
        for p in range(BLOCKS):
            source = near_ref if p < BLOCKS // 2 else far_ref
            first = p % (BLOCKS // 2) * (block + 8)
            cells = as_float(source[h, first : first + block + 8])
            rows = cells[:block] * jnp.exp2(cells[block : block + 1] * 0.0625 - 15.0)
            table[pl.ds(pl.multiple_of((me_ref[h] ^ p) * block, 8), block), h * part : (h + 1) * part] = rows
    taps = conv_ref.shape[0]
    total = jnp.zeros(grad_ref.shape, F32)
    for k in range(taps):
        pair = split(table[k * VOCAB : (k + 1) * VOCAB])
        high_ref[k], low_ref[k] = pair
        total = total + dot2(conv_ref[k].astype(BF), pair, NT)
    grad_ref[...] = total


def order_table(me, near, far, conv, extra, score, second):
    taps, own, width = conv.shape
    vmem = pl.BlockSpec(memory_space=pltpu.VMEM)
    table = jax.ShapeDtypeStruct((taps, VOCAB, width), BF)
    row = jax.ShapeDtypeStruct((1, width), F32)
    return pl.pallas_call(
        order_body,
        in_specs=[pl.BlockSpec(memory_space=pltpu.SMEM)] + [vmem] * 6,
        out_specs=[vmem] * 7,
        out_shape=[
            table,
            table,
            jax.ShapeDtypeStruct((own, VOCAB), F32),
            jax.ShapeDtypeStruct((1, 1), F32),
            row,
            row,
            row,
        ],
        scratch_shapes=[pltpu.VMEM((taps * VOCAB, width), F32)],
        compiler_params=pltpu.CompilerParams(vmem_limit_bytes=60 << 20),
    )(me, near, far, conv, extra, score.reshape(1, width), second.reshape(1, width))


def dot2_left(pair, b, dims):
    return dot(pair[0], b, dims) + dot(pair[1], b, dims)


def both(left, right, dims):
    count = left[0].shape[0]
    first = dot(jnp.concatenate(left, axis=0), right[0], dims)
    return first[:count] + first[count:] + dot(left[0], right[1], dims)


def ready_body(where_ref, embed_ref, left_root_ref, square_high, square_low, columns_ref, rooted_high, rooted_low):
    taps, own, width = left_root_ref.shape
    embed = embed_ref[...]
    square_high[...], square_low[...] = split(dot(embed, embed, NT))
    columns_ref[...] = dot(pick_rows(own, width, where_ref[0] * own), embed, NT).astype(BF)
    high, low = split(left_root_ref[...].reshape(taps * own, width))
    rooted = dot(jnp.concatenate([high, low], axis=0), embed, NT)
    high, low = split(rooted[: taps * own] + rooted[taps * own :])
    rooted_high[...] = high.reshape(rooted_high.shape)
    rooted_low[...] = low.reshape(rooted_low.shape)


def make_ready(where, embed_all, left_root):
    taps, own, width = left_root.shape
    vmem = pl.BlockSpec(memory_space=pltpu.VMEM)
    like = lambda *shape: jax.ShapeDtypeStruct(shape, BF)
    return pl.pallas_call(
        ready_body,
        in_specs=[pl.BlockSpec(memory_space=pltpu.SMEM), vmem, vmem],
        out_specs=[vmem] * 5,
        out_shape=[like(VOCAB, VOCAB)] * 2 + [like(own, VOCAB)] + [like(taps, own, VOCAB)] * 2,
        compiler_params=pltpu.CompilerParams(vmem_limit_bytes=60 << 20),
        cost_estimate=pl.CostEstimate(flops=1 << 30, bytes_accessed=3 << 20, transcendentals=0),
    )(where, embed_all, left_root)


def conv_body(
    where_ref, high_ref, low_ref, embed_ref, square_high, square_low, columns_ref, rooted_high, rooted_low, right_root_ref,
    weight_ref, left_ref, right_ref, grad_out, weight_out, left_out, right_out,
):
    own, width = weight_ref.shape[1:]
    table = high_ref[0], low_ref[0]
    columns = columns_ref[...]
    pick = pick_rows(own, width, where_ref[0] * own)
    high = dot(jnp.concatenate([columns, rooted_high[0], rooted_low[0]], axis=0), table[0], NN)
    low = dot(jnp.concatenate([columns, rooted_high[0]], axis=0), table[1], NN)
    grad = high[:own] + low[:own]
    inner = high[own : 2 * own] + high[2 * own :] + low[own:]
    grad_out[0] = grad
    grad = split(grad)
    high = dot(jnp.concatenate([grad[0], grad[1], pick], axis=0), table[0], NT)
    low = dot(jnp.concatenate([grad[0], pick], axis=0), table[1], NT)
    crossed = split(high[:own] + high[own : 2 * own] + low[:own])
    mine = split(high[2 * own :] + low[own:])
    step = both(split(inner), split(right_root_ref[0]), NN)
    weight_out[0] = weight_ref[0] - RATE_CONV * step
    outer = dot(jnp.concatenate(crossed, axis=0), embed_ref[...], NN)
    left_out[0] = BETA_STAT * left_ref[0] + (1.0 - BETA_STAT) * (outer[:own] + outer[own:])
    outer = both(split(both(mine, (square_high[...], square_low[...]), NN)), table, NN)
    right_out[0] = BETA_STAT * right_ref[0] + (1.0 - BETA_STAT) * outer


def renew_conv(where, high, low, embed_all, ready, right_root, conv, left, right):
    taps, own, width = conv.shape
    by_tap = lambda *shape: pl.BlockSpec((1, *shape), lambda k: (k,) + (0,) * len(shape))
    whole = lambda *shape: pl.BlockSpec(shape, lambda k: (0,) * len(shape))
    rows = by_tap(own, width)
    return pl.pallas_call(
        conv_body,
        grid=(taps,),
        in_specs=[
            pl.BlockSpec(memory_space=pltpu.SMEM),
            by_tap(VOCAB, width),
            by_tap(VOCAB, width),
            whole(VOCAB, width),
            whole(VOCAB, VOCAB),
            whole(VOCAB, VOCAB),
            whole(own, VOCAB),
            by_tap(own, VOCAB),
            by_tap(own, VOCAB),
            by_tap(width, width),
            rows,
            rows,
            rows,
        ],
        out_specs=[rows] * 4,
        out_shape=[jax.ShapeDtypeStruct(conv.shape, F32)] * 4,
        compiler_params=pltpu.CompilerParams(vmem_limit_bytes=60 << 20),
        cost_estimate=pl.CostEstimate(flops=8 << 30, bytes_accessed=32 << 20, transcendentals=0),
    )(where, high, low, embed_all, *ready, right_root, conv, left, right)


def embed_body(
    owner_ref, near_ref, far_ref, weight_ref, left_ref, right_ref, left_root_ref, right_root_ref,
    grad_out, weight_out, left_out, right_out, table,
):
    count, own, _ = near_ref.shape
    rows = weight_ref.shape[0]
    owner = owner_ref[0]
    for m in range(count):
        table[pl.ds(pl.multiple_of((owner ^ (2 * m)) * own, 8), own)] = near_ref[m]
        table[pl.ds(pl.multiple_of((owner ^ (2 * m + 1)) * own, 8), own)] = far_ref[m]
    pair = split(table[...])
    grad = dot2(pick_rows(rows, VOCAB, owner * rows), pair, NT)
    grad_out[...] = grad
    left_out[...] = BETA_STAT * left_ref[...] + (1.0 - BETA_STAT) * dot3(split(grad), pair, NN)
    right_out[...] = BETA_STAT * right_ref[...] + (1.0 - BETA_STAT) * dot3(split(near_ref[0]), pair, NT)
    step = dot3(split(dot3(split(left_root_ref[...]), pair, NT)), split(right_root_ref[...]), NN)
    weight_out[...] = weight_ref[...] - RATE_EMBED * step


def renew_embed(owner, near, far, embed, left, right, left_root, right_root):
    vmem = pl.BlockSpec(memory_space=pltpu.VMEM)
    shapes = [jax.ShapeDtypeStruct(item.shape, F32) for item in (embed, embed, left, right)]
    return pl.pallas_call(
        embed_body,
        in_specs=[pl.BlockSpec(memory_space=pltpu.SMEM)] + [vmem] * 7,
        out_specs=[vmem] * 4,
        out_shape=shapes,
        scratch_shapes=[pltpu.VMEM((embed.shape[1], VOCAB), F32)],
        compiler_params=pltpu.CompilerParams(vmem_limit_bytes=60 << 20),
    )(owner, near, far, embed, left, right, left_root, right_root)


def shards(
    byte_ids,
    lengths,
    embed,
    conv,
    score,
    out_grad,
    embed_left,
    embed_right,
    conv_left,
    conv_right,
    embed_left_root,
    embed_right_root,
    conv_left_root,
    conv_right_root,
    score_second,
):
    length = byte_ids.shape[1]
    width = embed.shape[1]
    taps = conv.shape[0]
    owner = lax.axis_index("dp")
    start = lax.axis_index("seq") * length
    where = jnp.stack([owner, lax.axis_index("seq")]).astype(jnp.int32)
    mid = marked_ids(byte_ids, lengths, start, taps)
    left, right = shifted_rim(out_grad, 1)
    zero = jnp.zeros((byte_ids.shape[0], 7, width), F32)
    grad_rim = jnp.concatenate([zero, left, right, zero], axis=1)
    edges = jnp.stack([left[:, 0], out_grad[:, 0], out_grad[:, -1], right[:, 0]])
    embed_all, near, far, masks, ready, (mid, grad_rim) = gather_tables(
        where, embed, conv, conv_left_root, (mid, grad_rim)
    )
    plans = exchange_plan(lax.axis_size("seq"), lax.axis_size("dp"))
    me = jnp.stack([block_index(plan) for plan in plans])
    output, keep, send, extra = mix(
        where, me, start, lengths, mid, out_grad, grad_rim, score, near, far, edges, masks, taps
    )
    near, far, extra = sum_over_devices(keep, send, extra, plans)
    high, low, columns, entropy, score_grad, new_score, new_score_second = order_table(
        me, near, far, conv, extra, score, score_second
    )
    near = jnp.stack([columns] + [swap(columns, "dp", 2 * m) for m in range(1, lax.axis_size("dp") // 2)])
    conv_grad, new_conv, new_conv_left, new_conv_right = renew_conv(
        where, high, low, embed_all, ready, conv_right_root, conv, conv_left, conv_right
    )
    near, conv_grad = lax.optimization_barrier((near, conv_grad))
    far = swap(near, "dp", 1)
    embed_grad, new_embed, new_embed_left, new_embed_right = renew_embed(
        where, near, far, embed, embed_left, embed_right, embed_left_root, embed_right_root
    )
    return (
        output,
        entropy.reshape(()),
        embed_grad,
        conv_grad,
        score_grad.reshape(width),
        new_embed,
        new_conv,
        new_score.reshape(width),
        new_embed_left,
        new_embed_right,
        new_conv_left,
        new_conv_right,
        new_score_second.reshape(width),
    )


def solution(mesh):
    placed = (
        P("dp", "seq"),
        P("dp"),
        P("dp", None),
        P(None, "dp", None),
        P(),
        P("dp", "seq", None),
        P("dp", None),
        P("dp", None),
        P(None, "dp", None),
        P(None, "dp", None),
        P("dp", None),
        P(),
        P(None, "dp", None),
        P(),
        P(),
    )
    return jax.shard_map(
        shards,
        mesh=mesh,
        in_specs=placed,
        out_specs=(
            P("dp", "seq", None),
            P(),
            P("dp", None),
            P(None, "dp", None),
            P(),
            P("dp", None),
            P(None, "dp", None),
            P(),
            P("dp", None),
            P("dp", None),
            P(None, "dp", None),
            P(None, "dp", None),
            P(),
        ),
        check_vma=False,
    )
```
